32 devices in a mesh: dp: 8 (over z, x), fsdp: 4 (over y, core).
Axes of the slice: x: 2, y: 2, z: 4, core: 2. Of those that a mesh axis runs over, the one named last changes fastest.
Arguments:
- tokens: bfloat16 [128, 256, 512], P(('dp', 'fsdp')), may hold values from -6 to 6
- cotangent: bfloat16 [128, 256, 512], P(('dp', 'fsdp')), may hold values from -6 to 6
- reveal_order: int32 [128, 256], P(('dp', 'fsdp')), may hold values from 0 to 255, each once within a row
- reveal_step: int32 [128], P(('dp', 'fsdp')), may hold values from 1 to 256
- lengths: int32 [128], P(('dp', 'fsdp')), may hold values from 224 to 256
- weight_qkv: float32 [512, 1536], P(('dp', 'fsdp')), may hold values from -0.25 to 0.25
- weight_out: float32 [512, 512], P(('dp', 'fsdp')), may hold values from -1 to 1
- weight_up: float32 [512, 2048], P(('dp', 'fsdp')), may hold values from -0.25 to 0.25
- weight_down: float32 [2048, 512], P(('dp', 'fsdp')), may hold values from -0.125 to 0.125
- vectors: float32 [5, 512], P(None, ('dp', 'fsdp')), may hold values from -4 to 4, as said below
- moment_qkv: float32 [512, 1536], P(('dp', 'fsdp')), may hold values from -64 to 64
- square_qkv: float32 [512, 1536], P(('dp', 'fsdp')), may hold values from 8.192 to 32.768
- moment_out: float32 [512, 512], P(('dp', 'fsdp')), may hold values from -20 to 20
- square_out: float32 [512, 512], P(('dp', 'fsdp')), may hold values from 0.73728 to 2.94912
- moment_up: float32 [512, 2048], P(('dp', 'fsdp')), may hold values from -32 to 32
- square_up: float32 [512, 2048], P(('dp', 'fsdp')), may hold values from 2.94912 to 11.79648
- moment_down: float32 [2048, 512], P(('dp', 'fsdp')), may hold values from -64 to 64
- square_down: float32 [2048, 512], P(('dp', 'fsdp')), may hold values from 11.79648 to 47.18592
- moment_vec: float32 [5, 512], P(None, ('dp', 'fsdp')), may hold values from -64 to 64
- square_vec: float32 [5, 512], P(None, ('dp', 'fsdp')), may hold values from 11.79648 to 47.18592
Outputs:
- block_output: bfloat16 [128, 256, 512], P(('dp', 'fsdp'))
- input_grad: float32 [128, 256, 512], P(('dp', 'fsdp'))
- new_moment_qkv: float32 [512, 1536], P(('dp', 'fsdp'))
- new_square_qkv: float32 [512, 1536], P(('dp', 'fsdp'))
- new_weight_qkv: float32 [512, 1536], P(('dp', 'fsdp'))
- new_moment_out: float32 [512, 512], P(('dp', 'fsdp'))
- new_square_out: float32 [512, 512], P(('dp', 'fsdp'))
- new_weight_out: float32 [512, 512], P(('dp', 'fsdp'))
- new_moment_up: float32 [512, 2048], P(('dp', 'fsdp'))
- new_square_up: float32 [512, 2048], P(('dp', 'fsdp'))
- new_weight_up: float32 [512, 2048], P(('dp', 'fsdp'))
- new_moment_down: float32 [2048, 512], P(('dp', 'fsdp'))
- new_square_down: float32 [2048, 512], P(('dp', 'fsdp'))
- new_weight_down: float32 [2048, 512], P(('dp', 'fsdp'))
- new_moment_vec: float32 [5, 512], P(None, ('dp', 'fsdp'))
- new_square_vec: float32 [5, 512], P(None, ('dp', 'fsdp'))
- new_vectors: float32 [5, 512], P(None, ('dp', 'fsdp'))
The draws below stay inside these ranges and needn't reach their ends.
Inputs may be any that keep to these rules, and one draw needn't show every extreme that they name: `vectors`: rows 0 and 1 lie in 0.7 to 1.3.
All inputs are finite; a program needn't handle non-finite values.
Results may differ from the reference program's by a relative error of at most 0.0085.
The reference program's roundings to bfloat16 on the way count: a program that leaves them out, or rounds other values in their place, can miss the bound.
Values may be sent and summed in bfloat16 or wider, within the bound.
No kernel may reach another device: no remote copies, remote signals or barrier semaphores. Data moves between devices by JAX's collectives and lax.ppermute only.
A program may use at most 128 MiB of HBM per device.

```python
import math
import jax
import jax.numpy as jnp
from jax import lax

D = 512
HEADS = 8
HEAD = 64
FF = 2048
SEQ = 256
STEP = 10
SPANS = 128
TOKENS = 32768


def draw_vectors(key, part):
    key = jax.random.fold_in(key, 11)
    gain_key, shift_key, mask_key = jax.random.split(key, 3)
    gains = jax.random.uniform(gain_key, (2, D), jnp.float32, 0.7, 1.3)
    shifts = 0.3 * jax.random.normal(shift_key, (2, D), jnp.float32)
    mask_row = jnp.clip(jax.random.normal(mask_key, (1, D), jnp.float32), -4.0, 4.0)
    return jnp.concatenate([gains, shifts, mask_row], axis=0)


def set_ends(drawn, stream_key, smallest, top_value):
    extent = drawn.shape
    index_at = [jax.random.randint(jax.random.fold_in(stream_key, axis), (), 0, extent[axis]) for axis in range(len(extent))]
    drawn = drawn.at[tuple(index_at)].set(smallest)
    longest = extent.index(max(extent))
    index_at[longest] = (index_at[longest] + 1) % extent[longest]
    return drawn.at[tuple(index_at)].set(top_value)


def block_levels(stream_key, dims, shards, least, largest):
    factor_of = 1.0
    for position, blocks in shards:
        heights = jax.random.uniform(jax.random.fold_in(jax.random.fold_in(stream_key, 6), position), (blocks,), jnp.float32, least / len(shards), largest / len(shards))
        factor_of = factor_of * jnp.repeat(jnp.exp(heights), dims[position] // blocks).reshape((-1,) + (1,) * (len(dims) - 1 - position))
    return factor_of


def bell_draw(key, shape, width, most, shards=(), kind=jnp.bfloat16):
    drawn = width * jax.random.normal(key, shape, jnp.float32)
    if shards:
        drawn = drawn * block_levels(key, shape, shards, -0.22, 0.18)
    return jnp.clip(drawn, -most, most).astype(kind)


def setup_inputs(seed: int = 0) -> dict:
    key_of = jax.random.split(jax.random.key(seed), 21)
    return {
        "tokens": bell_draw(key_of[0], (SPANS, SEQ, D), 1.0, 6.0, ((0, 32),)),
        "cotangent": bell_draw(key_of[1], (SPANS, SEQ, D), 1.0, 6.0, ((0, 32),)),
        "reveal_order": jax.vmap(lambda own: jax.random.permutation(own, SEQ))(jax.random.split(key_of[2], SPANS)).reshape((SPANS, SEQ)).astype(jnp.int32),
        "reveal_step": set_ends(jax.random.randint(key_of[3], (SPANS,), 1, SEQ + 1), jax.random.fold_in(key_of[3], 1), 1, SEQ).astype(jnp.int32),
        "lengths": set_ends(jax.random.randint(key_of[4], (SPANS,), SEQ - SEQ // 8, SEQ + 1), jax.random.fold_in(key_of[4], 1), SEQ - SEQ // 8, SEQ).astype(jnp.int32),
        "weight_qkv": bell_draw(key_of[5], (D, 3 * D), D ** -0.5, 0.25, ((0, 32),), jnp.float32),
        "weight_out": bell_draw(key_of[6], (D, D), (D // 16) ** -0.5, 1.0, ((0, 32),), jnp.float32),
        "weight_up": bell_draw(key_of[7], (D, FF), D ** -0.5, 0.25, ((0, 32),), jnp.float32),
        "weight_down": bell_draw(key_of[8], (FF, D), FF ** -0.5, 0.125, ((0, 32),), jnp.float32),
        "vectors": draw_vectors(jax.random.fold_in(key_of[20], 71), 0),
        "moment_qkv": bell_draw(key_of[10], (D, 3 * D), (0.055 * TOKENS ** 0.5), 64.0, ((0, 32),), jnp.float32),
        "square_qkv": jnp.clip(jnp.exp(math.log(32.768) - 1.3862944 * jax.random.uniform(key_of[11], (D, 3 * D), jnp.float32) ** block_levels(key_of[11], (D, 3 * D), ((0, 32),), -0.2, 0.2)), 8.192, 32.768),
        "moment_out": bell_draw(key_of[12], (D, D), (0.017 * TOKENS ** 0.5), 20.0, ((0, 32),), jnp.float32),
        "square_out": jnp.clip(jnp.exp(math.log(2.94912) - 1.3862944 * jax.random.uniform(key_of[13], (D, D), jnp.float32) ** block_levels(key_of[13], (D, D), ((0, 32),), -0.2, 0.2)), 0.73728, 2.94912),
        "moment_up": bell_draw(key_of[14], (D, FF), (0.033 * TOKENS ** 0.5), 32.0, ((0, 32),), jnp.float32),
        "square_up": jnp.clip(jnp.exp(math.log(11.79648) - 1.3862944 * jax.random.uniform(key_of[15], (D, FF), jnp.float32) ** block_levels(key_of[15], (D, FF), ((0, 32),), -0.2, 0.2)), 2.94912, 11.79648),
        "moment_down": bell_draw(key_of[16], (FF, D), (0.067 * TOKENS ** 0.5), 64.0, ((0, 32),), jnp.float32),
        "square_down": jnp.clip(jnp.exp(math.log(47.18592) - 1.3862944 * jax.random.uniform(key_of[17], (FF, D), jnp.float32) ** block_levels(key_of[17], (FF, D), ((0, 32),), -0.2, 0.2)), 11.79648, 47.18592),
        "moment_vec": bell_draw(key_of[18], (5, D), (0.067 * TOKENS ** 0.5), 64.0, ((1, 32),), jnp.float32),
        "square_vec": jnp.clip(jnp.exp(math.log(47.18592) - 1.3862944 * jax.random.uniform(key_of[19], (5, D), jnp.float32) ** block_levels(key_of[19], (5, D), ((1, 32),), -0.2, 0.2)), 11.79648, 47.18592),
    }


norm_epsilon = 1e-05
beta_first = 0.9
beta_second = 0.999
adam_epsilon = 1e-08
weight_decay = 0.1
matrix_rate = 0.02
output_rate = 0.1
vector_rate = 0.2
masked_score = -1000000000.0

@jax.custom_vjp
def low(v):
    return lax.optimization_barrier(v.astype(jnp.bfloat16)).astype(jnp.float32)

@jax.custom_vjp
def low_back(v):
    return v

def low_keep(v):
    return (low(v), None)

def low_pass(kept, grad):
    return (grad,)

def back_keep(v):
    return (v, None)

def back_low(kept, grad):
    return (low(grad),)
low.defvjp(low_keep, low_pass)
low_back.defvjp(back_keep, back_low)

def layer_norm(values, gain, shift):
    centred = values - lax.optimization_barrier(jnp.mean(values, axis=-1, keepdims=True))
    spread = lax.optimization_barrier(jnp.mean(centred * centred, axis=-1, keepdims=True))
    return centred * lax.rsqrt(spread + norm_epsilon) * gain + shift

def block_forward(weight_qkv, weight_out, weight_up, weight_down, vectors, inputs, masked, key_valid):
    highest = lax.Precision.HIGHEST
    qkv_low = low(weight_qkv)
    out_low = low(weight_out)
    up_low = low(weight_up)
    down_low = low(weight_down)
    vec_low = low(vectors)
    span_count = inputs.shape[0]
    started = jnp.where(masked[..., None], vec_low[4], inputs)
    normed = low(layer_norm(started, vec_low[0], vec_low[2]))
    projected = low(low_back(jnp.einsum('csd,de->cse', normed, qkv_low, precision=highest)))
    qkv_split = projected.reshape(span_count, SEQ, 3, HEADS, HEAD)
    queries = qkv_split[:, :, 0]
    keys_all = qkv_split[:, :, 1]
    values_all = qkv_split[:, :, 2]
    scores = low_back(jnp.einsum('cqhd,ckhd->chqk', queries, keys_all, precision=highest) * HEAD ** (-0.5))
    scores = jnp.where(key_valid[:, None, None, :], scores, masked_score)
    row_peak = lax.optimization_barrier(jnp.max(scores, axis=-1, keepdims=True))
    exp_scores = jnp.exp(scores - row_peak)
    probability = exp_scores / lax.optimization_barrier(jnp.sum(exp_scores, axis=-1, keepdims=True))
    attended = low(low_back(jnp.einsum('chqk,ckhd->cqhd', low(probability), values_all, precision=highest)))
    mixed_out = low_back(jnp.einsum('csd,de->cse', attended.reshape(span_count, SEQ, D), out_low, precision=highest))
    middle = started + mixed_out
    second = low(layer_norm(middle, vec_low[1], vec_low[3]))
    hidden_pre = low_back(jnp.einsum('csd,df->csf', second, up_low, precision=highest))
    activated = low(jax.nn.gelu(hidden_pre))
    branch = low_back(jnp.einsum('csf,fd->csd', activated, down_low, precision=highest))
    return middle + branch

def adam_update(master, gradient, moment, square, step_rate, decay_rate):
    moment_new = beta_first * moment + (1.0 - beta_first) * gradient
    square_new = beta_second * square + (1.0 - beta_second) * gradient * gradient
    corrected = moment_new / (1.0 - beta_first ** STEP) / (jnp.sqrt(square_new / (1.0 - beta_second ** STEP)) + adam_epsilon)
    return (moment_new, square_new, master - step_rate * (corrected + decay_rate * master))

def reference(tokens, cotangent, reveal_order, reveal_step, lengths, weight_qkv, weight_out, weight_up, weight_down, vectors, moment_qkv, square_qkv, moment_out, square_out, moment_up, square_up, moment_down, square_down, moment_vec, square_vec):
    masters = (weight_qkv, weight_out, weight_up, weight_down, vectors)
    group_size = 16
    group_count = SPANS // group_size
    positions = jnp.arange(SEQ, dtype=jnp.int32)

    def scan_step(totals, pieces):
        tok_piece, cot_piece, order_piece, step_piece, length_piece = pieces
        masked = order_piece >= step_piece[:, None]
        key_valid = positions[None, :] < length_piece[:, None]

        def forward(*operands):
            return block_forward(*operands, masked, key_valid)
        result, pullback = jax.vjp(forward, *masters, tok_piece.astype(jnp.float32))
        gradients = pullback(cot_piece.astype(jnp.float32))
        totals = tuple((summed + fresh_grads for summed, fresh_grads in zip(totals, gradients[:5])))
        return (totals, (result.astype(jnp.bfloat16), gradients[5]))
    initial = tuple((jnp.zeros(master.shape, jnp.float32) for master in masters))
    pieces = (tokens.reshape(group_count, group_size, SEQ, D), cotangent.reshape(group_count, group_size, SEQ, D), reveal_order.reshape(group_count, group_size, SEQ), reveal_step.reshape(group_count, group_size), lengths.reshape(group_count, group_size))
    totals, (outputs, input_grads) = lax.scan(scan_step, initial, pieces)
    block_output = outputs.reshape(SPANS, SEQ, D)
    input_grad = input_grads.reshape(SPANS, SEQ, D)
    m_qkv, s_qkv, w_qkv = adam_update(weight_qkv, totals[0], moment_qkv, square_qkv, matrix_rate, weight_decay)
    m_out, s_out, w_out = adam_update(weight_out, totals[1], moment_out, square_out, output_rate, weight_decay)
    m_up, s_up, w_up = adam_update(weight_up, totals[2], moment_up, square_up, matrix_rate, weight_decay)
    m_down, s_down, w_down = adam_update(weight_down, totals[3], moment_down, square_down, matrix_rate, weight_decay)
    m_vec, s_vec, w_vec = adam_update(vectors, totals[4], moment_vec, square_vec, vector_rate, 0.0)
    return (block_output, input_grad, m_qkv, s_qkv, w_qkv, m_out, s_out, w_out, m_up, s_up, w_up, m_down, s_down, w_down, m_vec, s_vec, w_vec)
```

```python
import functools

import jax
import jax.numpy as jnp
from jax import lax
from jax.experimental import pallas as pl
from jax.experimental.pallas import tpu as pltpu
from jax.sharding import PartitionSpec as P

D = 512
HEADS = 8
HEAD = 64
STEP = 10


norm_epsilon = 1e-05
beta_first = 0.9
beta_second = 0.999
adam_epsilon = 1e-08
weight_decay = 0.1
matrix_rate = 0.02
output_rate = 0.1
vector_rate = 0.2
masked_score = -1000000000.0


def layer_norm(values, gain, shift):
    centred = values - jnp.mean(values, axis=-1, keepdims=True)
    spread = jnp.mean(centred * centred, axis=-1, keepdims=True)
    return centred * lax.rsqrt(spread + norm_epsilon) * gain + shift


def attention_scores(qkv_split, key_valid):
    scores = jnp.einsum(
        "cqhd,ckhd->chqk",
        qkv_split[:, :, 0],
        qkv_split[:, :, 1],
        preferred_element_type=jnp.float32,
    ) * HEAD ** (-0.5)
    return jnp.where(key_valid[:, None, None, :], scores, masked_score)


def forward_pass(gathered, inputs, masked, key_valid):
    qkv_full, out_full, up_full, down_full, vec_full = gathered
    vec_wide = vec_full.astype(jnp.float32)
    span_count, seq_len = (inputs.shape[0], inputs.shape[1])
    started = jnp.where(masked[..., None], vec_wide[4], inputs.astype(jnp.float32))
    normed = layer_norm(started, vec_wide[0], vec_wide[2]).astype(jnp.bfloat16)
    projected = jnp.einsum(
        "csd,de->cse", normed, qkv_full, preferred_element_type=jnp.float32
    ).astype(jnp.bfloat16)
    qkv_split = projected.reshape(span_count, seq_len, 3, HEADS, HEAD)
    scores = attention_scores(qkv_split, key_valid)
    row_peak = jnp.max(scores, axis=-1, keepdims=True)
    exp_scores = jnp.exp(scores - row_peak)
    row_total = jnp.sum(exp_scores, axis=-1, keepdims=True)
    probability = exp_scores / row_total
    log_total = row_peak + jnp.log(row_total)
    attended = jnp.einsum(
        "chqk,ckhd->cqhd",
        probability.astype(jnp.bfloat16),
        qkv_split[:, :, 2],
        preferred_element_type=jnp.float32,
    )
    attended = attended.astype(jnp.bfloat16).reshape(span_count, seq_len, D)
    middle = started + jnp.einsum(
        "csd,de->cse", attended, out_full, preferred_element_type=jnp.float32
    )
    second = layer_norm(middle, vec_wide[1], vec_wide[3]).astype(jnp.bfloat16)
    hidden_pre = jnp.einsum("csd,df->csf", second, up_full, preferred_element_type=jnp.float32)
    activated = jax.nn.gelu(hidden_pre).astype(jnp.bfloat16)
    result = middle + jnp.einsum(
        "csf,fd->csd", activated, down_full, preferred_element_type=jnp.float32
    )
    saved_state = (
        started,
        normed,
        qkv_split,
        log_total,
        attended,
        middle,
        second,
        hidden_pre,
        activated,
    )
    return (result, saved_state)


def backward_pass(gathered, saved_state, cot_rows, masked, key_valid):
    qkv_full, out_full, up_full, down_full, vec_full = gathered
    vec_wide = vec_full.astype(jnp.float32)
    started, normed, qkv_split, log_total, attended, middle, second, hidden_pre, activated = (
        saved_state
    )
    span_count, seq_len = (cot_rows.shape[0], cot_rows.shape[1])
    upstream = cot_rows.astype(jnp.float32)
    down_grad = upstream.astype(jnp.bfloat16)
    grad_down = jnp.einsum("csf,csd->fd", activated, down_grad, preferred_element_type=jnp.float32)
    grad_act = jnp.einsum("csd,fd->csf", down_grad, down_full, preferred_element_type=jnp.float32)
    ignored, gelu_back = jax.vjp(jax.nn.gelu, hidden_pre)
    grad_pre = gelu_back(grad_act)[0].astype(jnp.bfloat16)
    grad_up = jnp.einsum("csd,csf->df", second, grad_pre, preferred_element_type=jnp.float32)
    grad_second = jnp.einsum("csf,df->csd", grad_pre, up_full, preferred_element_type=jnp.float32)
    ignored, second_back = jax.vjp(layer_norm, middle, vec_wide[1], vec_wide[3])
    grad_middle_norm, grad_gain_two, grad_shift_two = second_back(grad_second)
    grad_middle = upstream + grad_middle_norm
    mix_grad = grad_middle.astype(jnp.bfloat16)
    grad_out = jnp.einsum("csd,cse->de", attended, mix_grad, preferred_element_type=jnp.float32)
    grad_att = jnp.einsum("cse,de->csd", mix_grad, out_full, preferred_element_type=jnp.float32)
    grad_att = grad_att.astype(jnp.bfloat16).reshape(span_count, seq_len, HEADS, HEAD)
    scores = attention_scores(qkv_split, key_valid)
    probability = jnp.exp(scores - log_total)
    grad_values = jnp.einsum(
        "chqk,cqhd->ckhd",
        probability.astype(jnp.bfloat16),
        grad_att,
        preferred_element_type=jnp.float32,
    )
    grad_probs = jnp.einsum(
        "cqhd,ckhd->chqk", grad_att, qkv_split[:, :, 2], preferred_element_type=jnp.float32
    )
    grad_scores = probability * (
        grad_probs - jnp.sum(probability * grad_probs, axis=-1, keepdims=True)
    )
    grad_scores = grad_scores.astype(jnp.bfloat16)
    grad_queries = jnp.einsum(
        "chqk,ckhd->cqhd", grad_scores, qkv_split[:, :, 1], preferred_element_type=jnp.float32
    ) * HEAD ** (-0.5)
    grad_keys = jnp.einsum(
        "chqk,cqhd->ckhd", grad_scores, qkv_split[:, :, 0], preferred_element_type=jnp.float32
    ) * HEAD ** (-0.5)
    grad_split = jnp.stack([grad_queries, grad_keys, grad_values], axis=2).astype(jnp.bfloat16)
    grad_split = grad_split.reshape(span_count, seq_len, 3 * D)
    grad_qkv = jnp.einsum("csd,cse->de", normed, grad_split, preferred_element_type=jnp.float32)
    grad_normed = jnp.einsum(
        "cse,de->csd", grad_split, qkv_full, preferred_element_type=jnp.float32
    )
    ignored, first_back = jax.vjp(layer_norm, started, vec_wide[0], vec_wide[2])
    grad_started_norm, grad_gain_one, grad_shift_one = first_back(grad_normed)
    grad_started = grad_middle + grad_started_norm
    grad_mask = jnp.sum(jnp.where(masked[..., None], grad_started, 0.0), axis=(0, 1))
    input_grad = jnp.where(masked[..., None], 0.0, grad_started)
    grad_vec = jnp.stack([grad_gain_one, grad_gain_two, grad_shift_one, grad_shift_two, grad_mask])
    return (input_grad, (grad_qkv, grad_out, grad_up, grad_down, grad_vec))


def adam_update(master, gradient, moment, square, step_rate, decay_rate):
    moment_new = beta_first * moment + (1.0 - beta_first) * gradient
    square_new = beta_second * square + (1.0 - beta_second) * gradient * gradient
    corrected = (
        moment_new
        / (1.0 - beta_first**STEP)
        / (jnp.sqrt(square_new / (1.0 - beta_second**STEP)) + adam_epsilon)
    )
    return (moment_new, square_new, master - step_rate * (corrected + decay_rate * master))


AXES = ("dp", "fsdp")
LANES = 128


def device_count(mesh):
    return mesh.shape["dp"] * mesh.shape["fsdp"]


def far_masks(count):
    masks = []
    bit = 8
    while bit < count:
        masks.append(bit)
        bit *= 2
    return masks


def exchange(values, count, even_mask, odd_mask):
    pairs = [(i, i ^ (odd_mask if i % 2 else even_mask)) for i in range(count)]
    return lax.ppermute(values, AXES, pairs)


def far_offsets(count):
    offsets = [0]
    for mask in far_masks(count):
        offsets = offsets + [old + mask for old in offsets]
    return offsets


def block_device(me, core, place, far):
    quarter = len(far)
    first = jnp.where(core == 0, 4, 2)
    second = 6 - first
    group = place // quarter
    near = (0, first, second, first + second)[group]
    return me ^ near ^ far[place % quarter]


def gather_stack(shard, count):
    far = far_offsets(count)
    stack = [shard] + [exchange(shard, count, offset, offset) for offset in far[1:]]
    stack = jnp.concatenate(stack, axis=0)
    stack = jnp.concatenate([stack, exchange(stack, count, 4, 2)], axis=0)
    late = exchange(stack, count, 2, 4)
    return (stack, late, exchange(stack, count, 1, 1), exchange(late, count, 1, 1))


def assemble_kernel(me_ref, own_ref, late_ref, other_ref, other_late_ref, full_ref, *, far, rows):
    me = me_ref[0]
    core = me & 1
    half = len(far) * 2
    for place in range(half):
        for stream, refs in ((0, (own_ref, late_ref)), (1, (other_ref, other_late_ref))):
            for upper in range(2):
                device = block_device(me ^ stream, core ^ stream, place + upper * half, far)
                start = pl.multiple_of(device * rows, rows)
                full_ref[pl.ds(start, rows), :] = refs[upper][pl.ds(place * rows, rows), :]


def whole_vmem():
    return pl.BlockSpec(memory_space=pltpu.VMEM)


def assemble(me, stacks, count):
    half, columns = stacks[0].shape
    far = far_offsets(count)
    rows = half // (2 * len(far))
    return pl.pallas_call(
        functools.partial(assemble_kernel, far=far, rows=rows),
        out_shape=jax.ShapeDtypeStruct((rows * count, columns), stacks[0].dtype),
        in_specs=[pl.BlockSpec(memory_space=pltpu.SMEM)] + [whole_vmem()] * 4,
        out_specs=whole_vmem(),
        name="assemble",
    )(me, *stacks)


def arrange_kernel(me_ref, full_ref, keep_ref, send_ref, *, far, rows):
    me = me_ref[0]
    core = me & 1
    for place in range(len(far) * 4):
        here = pl.ds(place * rows, rows)
        device = block_device(me, core, place, far)
        keep_ref[here, :] = full_ref[pl.ds(pl.multiple_of(device * rows, rows), rows), :]
        device = block_device(me ^ 1, core ^ 1, place, far)
        taken = full_ref[pl.ds(pl.multiple_of(device * rows, rows), rows), :]
        send_ref[here, :] = taken.astype(jnp.bfloat16)


def arrange(me, full, count):
    total, columns = full.shape
    return pl.pallas_call(
        functools.partial(arrange_kernel, far=far_offsets(count), rows=total // count),
        out_shape=(
            jax.ShapeDtypeStruct((total // 2, columns), jnp.float32),
            jax.ShapeDtypeStruct((total // 2, columns), jnp.bfloat16),
        ),
        in_specs=[pl.BlockSpec(memory_space=pltpu.SMEM), whole_vmem()],
        out_specs=(whole_vmem(), whole_vmem()),
        name="arrange",
    )(me, full)


def low(values):
    return values.astype(jnp.bfloat16)


def wide(values):
    return values.astype(jnp.float32)


def scatter_stack(keep, send, count):
    total = keep + wide(exchange(send, count, 1, 1))
    half = total.shape[0] // 2
    total = total[:half] + wide(exchange(low(total[half:]), count, 2, 4))
    half = half // 2
    total = total[:half] + wide(exchange(low(total[half:]), count, 4, 2))
    far = far_offsets(count)
    rows = half // len(far)
    own = total[:rows]
    for place in range(1, len(far)):
        part = low(total[place * rows : (place + 1) * rows])
        own = own + wide(exchange(part, count, far[place], far[place]))
    return own


def gather_rows(me, shard, count):
    if shard.shape[0] % 16 == 0:
        return assemble(me, gather_stack(shard, count), count)
    return lax.all_gather(shard, AXES, axis=0, tiled=True)


def scatter_rows(me, full, count):
    if (full.shape[0] // count) % 16 == 0:
        keep, send = arrange(me, full, count)
        return scatter_stack(keep, send, count)
    return lax.psum_scatter(full, AXES, scatter_dimension=0, tiled=True)


def local(
    tokens,
    cotangent,
    reveal_order,
    reveal_step,
    lengths,
    weight_qkv,
    weight_out,
    weight_up,
    weight_down,
    vectors,
    moment_qkv,
    square_qkv,
    moment_out,
    square_out,
    moment_up,
    square_up,
    moment_down,
    square_down,
    moment_vec,
    square_vec,
):
    me = (lax.axis_index("dp") * lax.axis_size("fsdp") + lax.axis_index("fsdp")).astype(jnp.int32)[None]
    count = lax.axis_size("dp") * lax.axis_size("fsdp")
    vector_rows = jnp.pad(low(vectors).T, ((0, 0), (0, LANES - vectors.shape[0])))
    first = gather_rows(me, jnp.concatenate([low(weight_qkv), vector_rows], axis=1), count)
    second = gather_rows(me, jnp.concatenate([low(weight_out), low(weight_up)], axis=1), count)
    down_full = gather_rows(me, low(weight_down), count)
    gathered = (
        first[:, : 3 * D],
        second[:, :D],
        second[:, D:],
        down_full,
        first[:, 3 * D : 3 * D + vectors.shape[0]].T,
    )
    positions = jnp.arange(tokens.shape[1], dtype=jnp.int32)
    masked = reveal_order >= reveal_step[:, None]
    key_valid = positions[None, :] < lengths[:, None]
    result, saved_state = forward_pass(gathered, tokens, masked, key_valid)
    block_output = low(result)
    input_grad, fresh_grads = backward_pass(gathered, saved_state, cotangent, masked, key_valid)
    grad_qkv, grad_out, grad_up, grad_down, grad_vec = fresh_grads
    share_down = scatter_rows(me, grad_down, count)
    share_second = scatter_rows(me, jnp.concatenate([grad_out, grad_up], axis=1), count)
    vec_columns = jnp.pad(grad_vec.T, ((0, 0), (0, LANES - vectors.shape[0])))
    share_first = scatter_rows(me, jnp.concatenate([grad_qkv, vec_columns], axis=1), count)
    running = (
        share_first[:, : 3 * D],
        share_second[:, :D],
        share_second[:, D:],
        share_down,
        share_first[:, 3 * D : 3 * D + vectors.shape[0]].T,
    )
    m_qkv, s_qkv, w_qkv = adam_update(
        weight_qkv, running[0], moment_qkv, square_qkv, matrix_rate, weight_decay
    )
    m_out, s_out, w_out = adam_update(
        weight_out, running[1], moment_out, square_out, output_rate, weight_decay
    )
    m_up, s_up, w_up = adam_update(
        weight_up, running[2], moment_up, square_up, matrix_rate, weight_decay
    )
    m_down, s_down, w_down = adam_update(
        weight_down, running[3], moment_down, square_down, matrix_rate, weight_decay
    )
    m_vec, s_vec, w_vec = adam_update(vectors, running[4], moment_vec, square_vec, vector_rate, 0.0)
    return (
        block_output,
        input_grad,
        m_qkv,
        s_qkv,
        w_qkv,
        m_out,
        s_out,
        w_out,
        m_up,
        s_up,
        w_up,
        m_down,
        s_down,
        w_down,
        m_vec,
        s_vec,
        w_vec,
    )


def solution(mesh):
    return jax.shard_map(
        local,
        mesh=mesh,
        in_specs=(
            P(("dp", "fsdp"), None, None),
            P(("dp", "fsdp"), None, None),
            P(("dp", "fsdp"), None),
            P(("dp", "fsdp")),
            P(("dp", "fsdp")),
            P(("dp", "fsdp"), None),
            P(("dp", "fsdp"), None),
            P(("dp", "fsdp"), None),
            P(("dp", "fsdp"), None),
            P(None, ("dp", "fsdp")),
            P(("dp", "fsdp"), None),
            P(("dp", "fsdp"), None),
            P(("dp", "fsdp"), None),
            P(("dp", "fsdp"), None),
            P(("dp", "fsdp"), None),
            P(("dp", "fsdp"), None),
            P(("dp", "fsdp"), None),
            P(("dp", "fsdp"), None),
            P(None, ("dp", "fsdp")),
            P(None, ("dp", "fsdp")),
        ),
        out_specs=(
            P(("dp", "fsdp"), None, None),
            P(("dp", "fsdp"), None, None),
            P(("dp", "fsdp"), None),
            P(("dp", "fsdp"), None),
            P(("dp", "fsdp"), None),
            P(("dp", "fsdp"), None),
            P(("dp", "fsdp"), None),
            P(("dp", "fsdp"), None),
            P(("dp", "fsdp"), None),
            P(("dp", "fsdp"), None),
            P(("dp", "fsdp"), None),
            P(("dp", "fsdp"), None),
            P(("dp", "fsdp"), None),
            P(("dp", "fsdp"), None),
            P(None, ("dp", "fsdp")),
            P(None, ("dp", "fsdp")),
            P(None, ("dp", "fsdp")),
        ),
        check_vma=False,
    )
```

```python
import functools

import jax
import jax.numpy as jnp
from jax import lax
from jax.experimental import pallas as pl
from jax.experimental.pallas import tpu as pltpu
from jax.sharding import PartitionSpec as P

D = 512
HEADS = 8
HEAD = 64
FF = 2048
HALF_FF = FF // 2
LANES = 128
ROWS = 16
STEP = 10
AXES = ("dp", "fsdp")
PARTS = 2
VMEM_BYTES = 48 * 1024 * 1024

norm_epsilon = 1e-05
beta_first = 0.9
beta_second = 0.999
adam_epsilon = 1e-08
weight_decay = 0.1
matrix_rate = 0.02
output_rate = 0.1
vector_rate = 0.2
masked_score = -1000000000.0
gelu_scale = 0.7978845608028654
gelu_cubic = 0.044715
FIRST_PAD = 224


def low(values):
    return values.astype(jnp.bfloat16)


def wide(values):
    return values.astype(jnp.float32)


def dot(left, right):
    return lax.dot_general(left, right, (((1,), (0,)), ((), ())), preferred_element_type=jnp.float32)


def dot_rows(left, right):
    return lax.dot_general(left, right, (((1,), (1,)), ((), ())), preferred_element_type=jnp.float32)


def dot_columns(left, right):
    return lax.dot_general(left, right, (((0,), (0,)), ((), ())), preferred_element_type=jnp.float32)


def whole():
    return pl.BlockSpec(memory_space=pltpu.VMEM)


def scalars():
    return pl.BlockSpec(memory_space=pltpu.SMEM)


def row_block(rows, columns):
    return pl.BlockSpec((rows, columns), lambda i: (i, 0))


def fixed_block(rows, columns):
    return pl.BlockSpec((rows, columns), lambda i: (0, 0))


FAR = (0, 8, 16, 24)


def block_device(me, core, place):
    first = jnp.where(core == 0, 4, 2)
    near = (0, first, 6 - first, 6)[place // len(FAR)]
    return me ^ near ^ FAR[place % len(FAR)]


def assemble(me, stacks, targets):
    for stream in range(2):
        for upper in range(2):
            stack = stacks[2 * stream + upper]
            for place in range(8):
                device = block_device(me ^ stream, (me & 1) ^ stream, place + upper * 8)
                here = pl.ds(place * ROWS, ROWS)
                for ref, column, columns, groups in targets:
                    for group in range(groups):
                        start = pl.multiple_of(device * (ROWS * groups) + group * ROWS, ROWS)
                        ref[pl.ds(start, ROWS), :] = stack[here, pl.ds(column + group * columns, columns)]


def arrange(me, sources, keep_ref, send_ref):
    for place in range(16):
        here = pl.ds(place * ROWS, ROWS)
        for stream, out in ((0, keep_ref), (1, send_ref)):
            device = block_device(me ^ stream, (me & 1) ^ stream, place)
            for ref, column, columns, groups in sources:
                for group in range(groups):
                    start = pl.multiple_of(device * (ROWS * groups) + group * ROWS, ROWS)
                    taken = ref[pl.ds(start, ROWS), :]
                    out[here, pl.ds(column + group * columns, columns)] = taken.astype(out.dtype)


def arranged(columns):
    return (
        jax.ShapeDtypeStruct((16 * ROWS, columns), jnp.float32),
        jax.ShapeDtypeStruct((16 * ROWS, columns), jnp.bfloat16),
    )


def centre(values):
    centred = values - jnp.mean(values, axis=-1, keepdims=True)
    scale = lax.rsqrt(jnp.mean(centred * centred, axis=-1, keepdims=True) + norm_epsilon)
    return centred * scale, scale


def norm_back(grad, gain, hat, scale):
    inner = grad * gain
    return scale * (
        inner - jnp.mean(inner, axis=-1, keepdims=True) - hat * jnp.mean(inner * hat, axis=-1, keepdims=True)
    )


def masked_rows(order_row, step):
    seq = order_row.shape[1]
    flags = jnp.where(order_row >= step, 1.0, 0.0)
    column = jnp.transpose(jnp.broadcast_to(flags, (LANES, seq)))
    return jnp.concatenate([column] * (D // LANES), axis=1) > 0.5


def pair_split(pair, scale=None):
    lane = lax.broadcasted_iota(jnp.int32, pair.shape, 1)
    values = wide(pair)
    if scale is not None:
        values = values * scale
    return jnp.concatenate([low(jnp.where(lane < HEAD, values, 0.0)), low(jnp.where(lane < HEAD, 0.0, values))], axis=0)


def key_scores(keys, both_queries, length):
    scores = dot_rows(keys, both_queries)
    seq = scores.shape[0]
    tail = scores[FIRST_PAD:]
    row = lax.broadcasted_iota(jnp.int32, tail.shape, 0) + FIRST_PAD
    return jnp.concatenate([scores[:FIRST_PAD], jnp.where(row < length, tail, masked_score)], axis=0)


def load_input(tokens_ref, order_ref, step, vec_ref):
    masked = masked_rows(order_ref[0], step)
    return masked, jnp.where(masked, vec_ref[4:5, :], wide(tokens_ref[...]))


def attention_kernel(
    me_ref, step_ref, length_ref, order_ref, tokens_ref, own_ref, late_ref, other_ref, other_late_ref,
    p_ref, l_ref, o_ref, weight_ref, vec_ref, columns_ref,
):
    span = pl.program_id(0)

    @pl.when(span == 0)
    def _():
        targets = ((weight_ref, 0, 3 * D, 1), (columns_ref, 3 * D, LANES, 1))
        assemble(me_ref[0], (own_ref, late_ref, other_ref, other_late_ref), targets)
        vec_ref[...] = jnp.transpose(wide(columns_ref[...]))[:8]

    started = load_input(tokens_ref, order_ref, step_ref[span], vec_ref)[1]
    normed = low(centre(started)[0] * vec_ref[0:1, :] + vec_ref[2:3, :])
    p_ref[...] = low(dot(normed, weight_ref[...]))
    seq = started.shape[0]
    for pair in range(D // LANES):
        lanes = pl.ds(pair * LANES, LANES)
        queries = pair_split(p_ref[:, lanes], HEAD**-0.5)
        scores = key_scores(p_ref[:, pl.ds(D + pair * LANES, LANES)], queries, length_ref[span])
        peak = jnp.max(scores, axis=0, keepdims=True)
        exped = jnp.exp(scores - peak)
        total = jnp.sum(exped, axis=0, keepdims=True)
        probability = low(exped / total)
        l_ref[0, pair : pair + 1, :] = peak + jnp.log(total)
        values = jnp.transpose(p_ref[:, pl.ds(2 * D + pair * LANES, LANES)])
        attended = jnp.concatenate(
            [dot(values[:HEAD], probability[:, :seq]), dot(values[HEAD:], probability[:, seq:])], axis=0
        )
        o_ref[:, lanes] = jnp.transpose(low(attended))


def span_specs(seq):
    return [pl.BlockSpec((1, 1, seq), lambda i: (i, 0, 0)), row_block(seq, D)]


def pair_block(seq):
    return pl.BlockSpec((1, D // LANES, 2 * seq), lambda i: (i, 0, 0))


def attention(me, steps, lengths, order, tokens, stacks):
    spans, seq = order.shape[0], order.shape[2]
    return pl.pallas_call(
        attention_kernel,
        grid=(spans,),
        out_shape=(
            jax.ShapeDtypeStruct((spans * seq, 3 * D), jnp.bfloat16),
            jax.ShapeDtypeStruct((spans, D // LANES, 2 * seq), jnp.float32),
            jax.ShapeDtypeStruct((spans * seq, D), jnp.bfloat16),
            jax.ShapeDtypeStruct((D, 3 * D), jnp.bfloat16),
            jax.ShapeDtypeStruct((8, D), jnp.float32),
        ),
        in_specs=[scalars()] * 3 + span_specs(seq) + [whole()] * 4,
        out_specs=(
            row_block(seq, 3 * D),
            pair_block(seq),
            row_block(seq, D),
            fixed_block(D, 3 * D),
            fixed_block(8, D),
        ),
        scratch_shapes=[pltpu.VMEM((D, LANES), jnp.bfloat16)],
        compiler_params=pltpu.CompilerParams(vmem_limit_bytes=VMEM_BYTES),
        name="attention",
    )(me, steps, lengths, order, tokens, *stacks)


def add_into(ref, index, value, start):
    @pl.when(start)
    def _():
        ref[index] = value

    @pl.when(jnp.logical_not(start))
    def _():
        ref[index] += value


def hidden_half(normed, upstream, up_ref, down_ref, grad_up_ref, grad_down_ref, start):
    width = HALF_FF // PARTS
    branch = 0.0
    grad_normed = 0.0
    for part in range(PARTS):
        units = pl.ds(part * width, width)
        hidden = dot(normed, up_ref[:, units])
        grad_act = dot_rows(upstream, down_ref[units, :])
        squared = hidden * hidden
        tilt = jnp.tanh(hidden * (gelu_scale + (gelu_scale * gelu_cubic) * squared))
        gate = 0.5 + 0.5 * tilt
        active = hidden * gate
        slope = gate + active * (1.0 - tilt) * (gelu_scale + (3.0 * gelu_scale * gelu_cubic) * squared)
        active = low(active)
        grad_hidden = low(grad_act * slope)
        branch = branch + dot(active, down_ref[units, :])
        grad_normed = grad_normed + dot_rows(grad_hidden, up_ref[:, units])
        add_into(grad_up_ref, (slice(None), units), dot_columns(normed, grad_hidden), start)
        add_into(grad_down_ref, (units, slice(None)), dot_columns(active, upstream), start)
    return branch, grad_normed


def first_half_kernel(
    me_ref, step_ref, order_ref, tokens_ref, cot_ref, vec_ref, o_ref, own_ref, late_ref, other_ref, other_late_ref,
    middle_ref, normed_ref, branch_ref, back_ref, out_ref, keep_ref, send_ref,
    up_ref, down_ref, grad_up_ref, grad_down_ref,
):
    span = pl.program_id(0)

    @pl.when(span == 0)
    def _():
        targets = ((up_ref, 0, HALF_FF, 1), (down_ref, HALF_FF, D, 2), (out_ref, 2 * HALF_FF, D, 1))
        assemble(me_ref[0], (own_ref, late_ref, other_ref, other_late_ref), targets)

    started = load_input(tokens_ref, order_ref, step_ref[span], vec_ref)[1]
    middle = started + dot(o_ref[...], out_ref[...])
    middle_ref[...] = middle
    normed = low(centre(middle)[0] * vec_ref[1:2, :] + vec_ref[3:4, :])
    normed_ref[...] = normed
    branch, back = hidden_half(normed, cot_ref[...], up_ref, down_ref, grad_up_ref, grad_down_ref, span == 0)
    branch_ref[...] = middle + branch
    back_ref[...] = back

    @pl.when(span == pl.num_programs(0) - 1)
    def _():
        sources = ((grad_up_ref, 0, HALF_FF, 1), (grad_down_ref, HALF_FF, D, 2))
        arrange(me_ref[0], sources, keep_ref, send_ref)


def half_scratch():
    return [
        pltpu.VMEM((D, HALF_FF), jnp.bfloat16),
        pltpu.VMEM((HALF_FF, D), jnp.bfloat16),
        pltpu.VMEM((D, HALF_FF), jnp.float32),
        pltpu.VMEM((HALF_FF, D), jnp.float32),
    ]


def first_half(me, steps, order, tokens, cotangent, vec, attended, stacks):
    spans, seq = order.shape[0], order.shape[2]
    tall = jax.ShapeDtypeStruct((spans * seq, D), jnp.float32)
    keep, send = arranged(2 * HALF_FF)
    return pl.pallas_call(
        first_half_kernel,
        grid=(spans,),
        out_shape=(
            tall,
            jax.ShapeDtypeStruct((spans * seq, D), jnp.bfloat16),
            tall,
            tall,
            jax.ShapeDtypeStruct((D, D), jnp.bfloat16),
            keep,
            send,
        ),
        in_specs=[scalars()] * 2
        + span_specs(seq)
        + [row_block(seq, D), fixed_block(8, D), row_block(seq, D)]
        + [whole()] * 4,
        out_specs=(
            row_block(seq, D),
            row_block(seq, D),
            row_block(seq, D),
            row_block(seq, D),
            fixed_block(D, D),
            fixed_block(*keep.shape),
            fixed_block(*send.shape),
        ),
        scratch_shapes=half_scratch(),
        compiler_params=pltpu.CompilerParams(vmem_limit_bytes=VMEM_BYTES),
        name="first_half",
    )(me, steps, order, tokens, cotangent, vec, attended, *stacks)


def second_half_kernel(
    me_ref, cot_ref, vec_ref, o_ref, middle_ref, normed_ref, branch_ref, back_ref, out_ref,
    own_ref, late_ref, other_ref, other_late_ref,
    result_ref, dmiddle_ref, dattended_ref, dvec_ref, keep_ref, send_ref,
    up_ref, down_ref, grad_up_ref, grad_down_ref, grad_out_ref,
):
    span = pl.program_id(0)
    start = span == 0

    @pl.when(start)
    def _():
        targets = ((up_ref, 0, HALF_FF, 1), (down_ref, HALF_FF, D, 2))
        assemble(me_ref[0], (own_ref, late_ref, other_ref, other_late_ref), targets)
        dvec_ref[...] = jnp.zeros_like(dvec_ref)

    upstream = cot_ref[...]
    branch, back = hidden_half(normed_ref[...], upstream, up_ref, down_ref, grad_up_ref, grad_down_ref, start)
    result_ref[...] = low(branch_ref[...] + branch)
    back = back_ref[...] + back
    hat, scale = centre(middle_ref[...])
    dmiddle = wide(upstream) + norm_back(back, vec_ref[1:2, :], hat, scale)
    dmiddle_ref[...] = dmiddle
    dvec_ref[1:2, :] += jnp.sum(back * hat, axis=0, keepdims=True)
    dvec_ref[3:4, :] += jnp.sum(back, axis=0, keepdims=True)
    mixed = low(dmiddle)
    dattended_ref[...] = low(dot_rows(mixed, out_ref[...]))
    add_into(grad_out_ref, Ellipsis, dot_columns(o_ref[...], mixed), start)

    @pl.when(span == pl.num_programs(0) - 1)
    def _():
        sources = ((grad_up_ref, 0, HALF_FF, 1), (grad_down_ref, HALF_FF, D, 2), (grad_out_ref, 2 * HALF_FF, D, 1))
        arrange(me_ref[0], sources, keep_ref, send_ref)


def second_half(me, cotangent, vec, attended, middle, normed, branch, back, out_full, stacks, seq):
    total = middle.shape[0]
    keep, send = arranged(2 * HALF_FF + D)
    rows = row_block(seq, D)
    return pl.pallas_call(
        second_half_kernel,
        grid=(total // seq,),
        out_shape=(
            jax.ShapeDtypeStruct((total, D), jnp.bfloat16),
            jax.ShapeDtypeStruct((total, D), jnp.float32),
            jax.ShapeDtypeStruct((total, D), jnp.bfloat16),
            jax.ShapeDtypeStruct((8, D), jnp.float32),
            keep,
            send,
        ),
        in_specs=[scalars(), rows, fixed_block(8, D), rows, rows, rows, rows, rows, fixed_block(D, D)] + [whole()] * 4,
        out_specs=(rows, rows, rows, fixed_block(8, D), fixed_block(*keep.shape), fixed_block(*send.shape)),
        scratch_shapes=half_scratch() + [pltpu.VMEM((D, D), jnp.float32)],
        compiler_params=pltpu.CompilerParams(vmem_limit_bytes=VMEM_BYTES),
        name="second_half",
    )(me, cotangent, vec, attended, middle, normed, branch, back, out_full, *stacks)


def attention_back_kernel(
    me_ref, step_ref, length_ref, order_ref, tokens_ref, vec_ref, p_ref, l_ref, dattended_ref, dmiddle_ref, weight_ref,
    dvec_in_ref, grad_ref, keep_ref, send_ref, dp_ref, grad_qkv_ref, dvec_ref, columns_ref,
):
    span = pl.program_id(0)
    start = span == 0

    @pl.when(start)
    def _():
        dvec_ref[...] = jnp.zeros_like(dvec_ref)
        dvec_ref[:8, :] = dvec_in_ref[...]

    seq = p_ref.shape[0]
    for pair in range(D // LANES):
        lanes = pl.ds(pair * LANES, LANES)
        key_lanes = pl.ds(D + pair * LANES, LANES)
        value_lanes = pl.ds(2 * D + pair * LANES, LANES)
        queries = pair_split(p_ref[:, lanes], HEAD**-0.5)
        dattended = pair_split(dattended_ref[:, lanes])
        keys = p_ref[:, key_lanes]
        scores = key_scores(keys, queries, length_ref[span])
        probability = jnp.exp(scores - l_ref[0, pair : pair + 1, :])
        dprobability = dot_rows(p_ref[:, value_lanes], dattended)
        inner = jnp.sum(probability * dprobability, axis=0, keepdims=True)
        dscores = low(probability * (dprobability - inner))
        dp_ref[:, value_lanes] = low(dot(low(probability), dattended))
        dp_ref[:, key_lanes] = low(dot(dscores, queries))
        keys = jnp.transpose(low(wide(keys) * HEAD**-0.5))
        dqueries = jnp.concatenate([dot(keys[:HEAD], dscores[:, :seq]), dot(keys[HEAD:], dscores[:, seq:])], axis=0)
        dp_ref[:, lanes] = jnp.transpose(low(dqueries))

    masked, started = load_input(tokens_ref, order_ref, step_ref[span], vec_ref)
    hat, scale = centre(started)
    normed = low(hat * vec_ref[0:1, :] + vec_ref[2:3, :])
    add_into(grad_qkv_ref, Ellipsis, dot_columns(normed, dp_ref[...]), start)
    back = dot_rows(dp_ref[...], weight_ref[...])
    dstarted = dmiddle_ref[...] + norm_back(back, vec_ref[0:1, :], hat, scale)
    dvec_ref[0:1, :] += jnp.sum(back * hat, axis=0, keepdims=True)
    dvec_ref[2:3, :] += jnp.sum(back, axis=0, keepdims=True)
    dvec_ref[4:5, :] += jnp.sum(jnp.where(masked, dstarted, 0.0), axis=0, keepdims=True)
    grad_ref[...] = jnp.where(masked, 0.0, dstarted)

    @pl.when(span == pl.num_programs(0) - 1)
    def _():
        columns_ref[...] = jnp.transpose(dvec_ref[...])
        arrange(me_ref[0], ((grad_qkv_ref, 0, 3 * D, 1), (columns_ref, 3 * D, LANES, 1)), keep_ref, send_ref)


def attention_back(me, steps, lengths, order, tokens, vec, projected, logs, dattended, dmiddle, weight, dvec):
    spans, seq = order.shape[0], order.shape[2]
    keep, send = arranged(3 * D + LANES)
    return pl.pallas_call(
        attention_back_kernel,
        grid=(spans,),
        out_shape=(jax.ShapeDtypeStruct((spans * seq, D), jnp.float32), keep, send),
        in_specs=[scalars()] * 3
        + span_specs(seq)
        + [
            fixed_block(8, D),
            row_block(seq, 3 * D),
            pair_block(seq),
            row_block(seq, D),
            row_block(seq, D),
            fixed_block(D, 3 * D),
            fixed_block(8, D),
        ],
        out_specs=(row_block(seq, D), fixed_block(*keep.shape), fixed_block(*send.shape)),
        scratch_shapes=[
            pltpu.VMEM((seq, 3 * D), jnp.bfloat16),
            pltpu.VMEM((D, 3 * D), jnp.float32),
            pltpu.VMEM((LANES, D), jnp.float32),
            pltpu.VMEM((D, LANES), jnp.float32),
        ],
        compiler_params=pltpu.CompilerParams(vmem_limit_bytes=VMEM_BYTES),
        name="attention_back",
    )(me, steps, lengths, order, tokens, vec, projected, logs, dattended, dmiddle, weight, dvec)


def exchange(values, count, even_mask, odd_mask):
    pairs = [(i, i ^ (odd_mask if i % 2 else even_mask)) for i in range(count)]
    return lax.ppermute(values, AXES, pairs)


def gather_stacks(shard, count):
    stack = [shard] + [exchange(shard, count, offset, offset) for offset in FAR[1:]]
    stack = jnp.concatenate(stack, axis=0)
    stack = jnp.concatenate([stack, exchange(stack, count, 4, 2)], axis=0)
    late = exchange(stack, count, 2, 4)
    return (stack, late, exchange(stack, count, 1, 1), exchange(late, count, 1, 1))


def scatter_stack(keep, send, count):
    total = keep + wide(exchange(send, count, 1, 1))
    half = 8 * ROWS
    total = total[:half] + wide(exchange(low(total[half:]), count, 2, 4))
    half = half // 2
    total = total[:half] + wide(exchange(low(total[half:]), count, 4, 2))
    own = total[:ROWS]
    for place in range(1, len(FAR)):
        part = low(total[place * ROWS : (place + 1) * ROWS])
        own = own + wide(exchange(part, count, FAR[place], FAR[place]))
    return own


def split_units(up, down):
    rows, units = up.shape
    up_halves = up.reshape(rows, units // 64, 2, 32)
    down_halves = down.reshape(rows // ROWS, 2, 2, ROWS, D)
    pieces = []
    for half in range(2):
        up_part = up_halves[:, :, half].reshape(rows, units // 2)
        down_part = jnp.swapaxes(down_halves[:, half], 1, 2).reshape(rows, 2 * D)
        pieces.append(jnp.concatenate([up_part, down_part], axis=1))
    return pieces


def join_units(pieces):
    rows = pieces[0].shape[0]
    up = jnp.stack([piece[:, :HALF_FF].reshape(rows, HALF_FF // 32, 32) for piece in pieces], axis=2)
    down = [jnp.swapaxes(piece[:, HALF_FF:].reshape(rows // ROWS, ROWS, 2, D), 1, 2) for piece in pieces]
    down = jnp.stack(down, axis=1).reshape(rows * 4, D)
    return up.reshape(rows, 2 * HALF_FF), down


def stack_order(core):
    near = (0, 4, 2, 6) if core == 0 else (0, 2, 4, 6)
    return [core ^ group ^ offset for group in near for offset in FAR]


def gather_piece(piece, count):
    if piece.shape[0] == ROWS:
        return gather_stacks(piece, count)
    blocks = piece.reshape(32, ROWS, piece.shape[1])
    stacks = []
    for core in range(2):
        ordered = jnp.stack([blocks[device] for device in stack_order(core)])
        ordered = ordered.reshape(16 * ROWS, piece.shape[1])
        stacks += [ordered[: 8 * ROWS], ordered[8 * ROWS :]]
    return tuple(stacks)


def full_piece(keep, send):
    columns = keep.shape[1]
    blocks = jnp.concatenate([keep, wide(send)], axis=0).reshape(32, ROWS, columns)
    order = stack_order(0) + stack_order(1)
    return jnp.stack([blocks[order.index(device)] for device in range(32)]).reshape(32 * ROWS, columns)


def adam_update(master, gradient, moment, square, step_rate, decay_rate):
    moment_new = beta_first * moment + (1.0 - beta_first) * gradient
    square_new = beta_second * square + (1.0 - beta_second) * gradient * gradient
    corrected = (
        moment_new
        / (1.0 - beta_first**STEP)
        / (jnp.sqrt(square_new / (1.0 - beta_second**STEP)) + adam_epsilon)
    )
    return (moment_new, square_new, master - step_rate * (corrected + decay_rate * master))


def local(
    tokens,
    cotangent,
    reveal_order,
    reveal_step,
    lengths,
    weight_qkv,
    weight_out,
    weight_up,
    weight_down,
    vectors,
    moment_qkv,
    square_qkv,
    moment_out,
    square_out,
    moment_up,
    square_up,
    moment_down,
    square_down,
    moment_vec,
    square_vec,
):
    count = lax.axis_size("dp") * lax.axis_size("fsdp")
    direct = weight_qkv.shape[0] == ROWS and count == 32
    me = lax.axis_index("dp") * lax.axis_size("fsdp") + lax.axis_index("fsdp")
    me = (me if direct else 0 * me).astype(jnp.int32)[None]
    spans, seq = reveal_order.shape
    order = reveal_order.reshape(spans, 1, seq)
    flat = tokens.reshape(spans * seq, D)
    upstream = cotangent.reshape(spans * seq, D)

    halves = [low(weight_qkv), low(weight_out), low(weight_up), low(weight_down), low(vectors).T]
    if not direct:
        halves = [lax.all_gather(half, AXES, axis=0, tiled=True) for half in halves]
    qkv, out, up, down, columns = halves
    columns = jnp.pad(columns, ((0, 0), (0, LANES - columns.shape[1])))
    hidden = split_units(up, down)
    first = gather_piece(jnp.concatenate([qkv, columns], axis=1), count)
    second = gather_piece(jnp.concatenate([hidden[0], out], axis=1), count)
    third = gather_piece(hidden[1], count)

    projected, logs, attended, weight, vec = attention(me, reveal_step, lengths, order, flat, first)
    middle, normed, branch, back, out_full, keep_one, send_one = first_half(
        me, reveal_step, order, flat, upstream, vec, attended, second
    )
    result, dmiddle, dattended, dvec, keep_two, send_two = second_half(
        me, upstream, vec, attended, middle, normed, branch, back, out_full, third, seq
    )
    input_grad, keep_three, send_three = attention_back(
        me, reveal_step, lengths, order, flat, vec, projected, logs, dattended, dmiddle, weight, dvec
    )

    stacks = [(keep_one, send_one), (keep_two, send_two), (keep_three, send_three)]
    if direct:
        sums = [scatter_stack(keep, send, count) for keep, send in stacks]
    else:
        sums = [full_piece(keep, send) for keep, send in stacks]
    grad_up, grad_down = join_units([sums[0], sums[1][:, : 2 * HALF_FF]])
    grads = (
        sums[2][:, : 3 * D],
        sums[1][:, 2 * HALF_FF :],
        grad_up,
        grad_down,
        sums[2][:, 3 * D : 3 * D + vectors.shape[0]],
    )
    if not direct:
        grads = [lax.psum_scatter(grad, AXES, scatter_dimension=0, tiled=True) for grad in grads]
    m_qkv, s_qkv, w_qkv = adam_update(weight_qkv, grads[0], moment_qkv, square_qkv, matrix_rate, weight_decay)
    m_out, s_out, w_out = adam_update(weight_out, grads[1], moment_out, square_out, output_rate, weight_decay)
    m_up, s_up, w_up = adam_update(weight_up, grads[2], moment_up, square_up, matrix_rate, weight_decay)
    m_down, s_down, w_down = adam_update(weight_down, grads[3], moment_down, square_down, matrix_rate, weight_decay)
    m_vec, s_vec, w_vec = adam_update(vectors, grads[4].T, moment_vec, square_vec, vector_rate, 0.0)
    return (
        result.reshape(tokens.shape),
        input_grad.reshape(tokens.shape),
        m_qkv,
        s_qkv,
        w_qkv,
        m_out,
        s_out,
        w_out,
        m_up,
        s_up,
        w_up,
        m_down,
        s_down,
        w_down,
        m_vec,
        s_vec,
        w_vec,
    )


def solution(mesh):
    return jax.shard_map(
        local,
        mesh=mesh,
        in_specs=(
            P(("dp", "fsdp"), None, None),
            P(("dp", "fsdp"), None, None),
            P(("dp", "fsdp"), None),
            P(("dp", "fsdp")),
            P(("dp", "fsdp")),
            P(("dp", "fsdp"), None),
            P(("dp", "fsdp"), None),
            P(("dp", "fsdp"), None),
            P(("dp", "fsdp"), None),
            P(None, ("dp", "fsdp")),
            P(("dp", "fsdp"), None),
            P(("dp", "fsdp"), None),
            P(("dp", "fsdp"), None),
            P(("dp", "fsdp"), None),
            P(("dp", "fsdp"), None),
            P(("dp", "fsdp"), None),
            P(("dp", "fsdp"), None),
            P(("dp", "fsdp"), None),
            P(None, ("dp", "fsdp")),
            P(None, ("dp", "fsdp")),
        ),
        out_specs=(
            P(("dp", "fsdp"), None, None),
            P(("dp", "fsdp"), None, None),
            P(("dp", "fsdp"), None),
            P(("dp", "fsdp"), None),
            P(("dp", "fsdp"), None),
            P(("dp", "fsdp"), None),
            P(("dp", "fsdp"), None),
            P(("dp", "fsdp"), None),
            P(("dp", "fsdp"), None),
            P(("dp", "fsdp"), None),
            P(("dp", "fsdp"), None),
            P(("dp", "fsdp"), None),
            P(("dp", "fsdp"), None),
            P(("dp", "fsdp"), None),
            P(None, ("dp", "fsdp")),
            P(None, ("dp", "fsdp")),
            P(None, ("dp", "fsdp")),
        ),
        check_vma=False,
    )
```

```python
import functools

import jax
import jax.numpy as jnp
from jax import lax
from jax.experimental import pallas as pl
from jax.experimental.pallas import tpu as pltpu
from jax.sharding import PartitionSpec as P

D = 512
HEADS = 8
HEAD = 64
FF = 2048
QUARTER = FF // 4
LANES = 128
PAIRS = D // LANES
ROWS = 16
STEP = 10
AXES = ("dp", "fsdp")
VMEM_BYTES = 28 * 1024 * 1024

norm_epsilon = 1e-05
beta_first = 0.9
beta_second = 0.999
adam_epsilon = 1e-08
weight_decay = 0.1
matrix_rate = 0.02
output_rate = 0.1
vector_rate = 0.2
masked_score = -1000000000.0
gelu_scale = 0.7978845608028654
gelu_cubic = 0.044715
FIRST_PAD = 224


def low(values):
    return values.astype(jnp.bfloat16)


def wide(values):
    return values.astype(jnp.float32)


def dot(left, right):
    return lax.dot_general(left, right, (((1,), (0,)), ((), ())), preferred_element_type=jnp.float32)


def dot_rows(left, right):
    return lax.dot_general(left, right, (((1,), (1,)), ((), ())), preferred_element_type=jnp.float32)


def dot_columns(left, right):
    return lax.dot_general(left, right, (((0,), (0,)), ((), ())), preferred_element_type=jnp.float32)


def cost(micros):
    return pl.CostEstimate(flops=int(micros * 1.15e9), bytes_accessed=0, transcendentals=0)


class Refs:
    pass


def call(body, name, grid, micros, ins, outs, scratch=(), continued=None):
    aliases = {}
    if continued is not None:
        for n, entry in enumerate(outs):
            aliases[len(ins)] = n
            ins = ins + [("old_" + entry[0], getattr(continued, entry[0]), pl.BlockSpec(memory_space=pl.ANY))]
    names = [entry[0] for entry in ins] + [entry[0] for entry in outs] + [entry[0] for entry in scratch]

    def kernel(*refs):
        named = Refs()
        for entry, ref in zip(names, refs):
            setattr(named, entry, ref)
        body(named)

    results = pl.pallas_call(
        kernel,
        grid=grid,
        out_shape=[jax.ShapeDtypeStruct(shape, kind) for _, shape, kind, _ in outs],
        in_specs=[spec for _, _, spec in ins],
        out_specs=[spec for _, _, _, spec in outs],
        scratch_shapes=[pltpu.VMEM(shape, kind) for _, shape, kind in scratch],
        compiler_params=pltpu.CompilerParams(vmem_limit_bytes=VMEM_BYTES),
        cost_estimate=cost(micros),
        input_output_aliases=aliases,
        name=name,
    )(*[array for _, array, _ in ins])
    out = Refs()
    for entry, value in zip(outs, results):
        setattr(out, entry[0], value)
    return out


def whole():
    return pl.BlockSpec(memory_space=pltpu.VMEM)


def scalars():
    return pl.BlockSpec(memory_space=pltpu.SMEM)


def row_block(rows, columns, at=0):
    return pl.BlockSpec((rows, columns), lambda i: (i, at))


def fixed_block(rows, columns, at=0):
    return pl.BlockSpec((rows, columns), lambda i: (0, at))


FAR = (0, 8, 16, 24)


def block_device(me, core, place):
    first = jnp.where(core == 0, 4, 2)
    near = (0, first, 6 - first, 6)[place // len(FAR)]
    return me ^ near ^ FAR[place % len(FAR)]


def assemble(me, stacks, targets):
    for stream in range(2):
        for upper in range(2):
            stack = stacks[2 * stream + upper]
            for place in range(8):
                device = block_device(me ^ stream, (me & 1) ^ stream, place + upper * 8)
                rows = pl.ds(pl.multiple_of(device * ROWS, ROWS), ROWS)
                for ref, column in targets:
                    ref[rows, :] = stack[pl.ds(place * ROWS, ROWS), pl.ds(column, ref.shape[1])]


def arrange(me, sources, keep_ref, send_ref):
    for place in range(16):
        here = pl.ds(place * ROWS, ROWS)
        for stream, out in ((0, keep_ref), (1, send_ref)):
            device = block_device(me ^ stream, (me & 1) ^ stream, place)
            rows = pl.ds(pl.multiple_of(device * ROWS, ROWS), ROWS)
            column = 0
            for ref in sources:
                out[here, pl.ds(column, ref.shape[1])] = ref[rows, :].astype(out.dtype)
                column += ref.shape[1]


def arranged(columns):
    shape = (16 * ROWS, columns)
    return [("keep", shape, jnp.float32, fixed_block(*shape)), ("send", shape, jnp.bfloat16, fixed_block(*shape))]


def centre(values):
    centred = values - jnp.mean(values, axis=-1, keepdims=True)
    scale = lax.rsqrt(jnp.mean(centred * centred, axis=-1, keepdims=True) + norm_epsilon)
    return centred * scale, scale


def norm_back(grad, gain, hat, scale):
    inner = grad * gain
    return scale * (
        inner - jnp.mean(inner, axis=-1, keepdims=True) - hat * jnp.mean(inner * hat, axis=-1, keepdims=True)
    )


def masked_rows(order_row, step):
    seq = order_row.shape[1]
    flags = jnp.where(order_row >= step, 1.0, 0.0)
    column = jnp.transpose(jnp.broadcast_to(flags, (LANES, seq)))
    return jnp.concatenate([column] * (D // LANES), axis=1) > 0.5


def pair_split(pair, scale=None):
    lane = lax.broadcasted_iota(jnp.int32, pair.shape, 1)
    values = wide(pair)
    if scale is not None:
        values = values * scale
    return jnp.concatenate([low(jnp.where(lane < HEAD, values, 0.0)), low(jnp.where(lane < HEAD, 0.0, values))], axis=0)


def key_scores(keys, both_queries, length):
    scores = dot_rows(keys, both_queries)
    seq = scores.shape[0]
    tail = scores[FIRST_PAD:]
    row = lax.broadcasted_iota(jnp.int32, tail.shape, 0) + FIRST_PAD
    return jnp.concatenate([scores[:FIRST_PAD], jnp.where(row < length, tail, masked_score)], axis=0)


def load_input(tokens_ref, order_ref, step, vec_ref):
    masked = masked_rows(order_ref[0], step)
    return masked, jnp.where(masked, vec_ref[4:5, :], wide(tokens_ref[...]))


def add_into(ref, index, value, start):
    @pl.when(start)
    def _():
        ref[index] = value

    @pl.when(jnp.logical_not(start))
    def _():
        ref[index] += value


def span_inputs(order, tokens, seq):
    return [
        ("order", order, pl.BlockSpec((1, 1, seq), lambda i: (i, 0, 0))),
        ("tokens", tokens, row_block(seq, D)),
    ]


def attention(scalar, order, tokens, first, spans, front=None):
    count, _, seq = order.shape
    fresh = front is None

    def body(r):
        span = pl.program_id(0)
        at = span + spans[0]
        if fresh:

            @pl.when(span == 0)
            def _():
                stacks = (r.stack0, r.stack1, r.stack2, r.stack3)
                assemble(r.me[0], stacks, ((r.weight, 0), (r.columns, 3 * D)))
                r.vec[...] = jnp.transpose(wide(r.columns[...]))[:8]

        started = load_input(r.tokens, r.order, r.step[at], r.vec)[1]
        normed = low(centre(started)[0] * r.vec[0:1, :] + r.vec[2:3, :])
        r.normed[...] = normed
        r.p[...] = low(dot(normed, r.weight[...]))
        for pair in range(PAIRS):
            lanes = pl.ds(pair * LANES, LANES)
            queries = pair_split(r.p[:, lanes], HEAD**-0.5)
            scores = key_scores(r.p[:, pl.ds(D + pair * LANES, LANES)], queries, r.length[at])
            peak = jnp.max(scores, axis=0, keepdims=True)
            exped = jnp.exp(scores - peak)
            total = jnp.sum(exped, axis=0, keepdims=True)
            probability = low(exped / total)
            r.logs[0, pair : pair + 1, :] = peak + jnp.log(total)
            values = jnp.transpose(r.p[:, pl.ds(2 * D + pair * LANES, LANES)])
            attended = jnp.concatenate(
                [dot(values[:HEAD], probability[:, :seq]), dot(values[HEAD:], probability[:, seq:])], axis=0
            )
            r.attended[:, lanes] = jnp.transpose(low(attended))

    ins = [(name, array, scalars()) for name, array in scalar.items()]
    ins += [
        ("order", order, pl.BlockSpec((1, 1, seq), lambda i: (i + spans[0], 0, 0))),
        ("tokens", tokens, pl.BlockSpec((seq, D), lambda i: (i + spans[0], 0))),
    ]
    def placed(columns):
        return pl.BlockSpec((seq, columns), lambda i: (i + spans[0], 0))

    rows = count * seq
    outs = [
        ("normed", (rows, D), jnp.bfloat16, placed(D)),
        ("p", (rows, 3 * D), jnp.bfloat16, placed(3 * D)),
        ("attended", (rows, D), jnp.bfloat16, placed(D)),
        ("logs", (count, PAIRS, 2 * seq), jnp.float32, pl.BlockSpec((1, PAIRS, 2 * seq), lambda i: (i + spans[0], 0, 0))),
    ]
    scratch = []
    if fresh:
        ins += [("stack%d" % n, stack, whole()) for n, stack in enumerate(first)]
        outs += [
            ("weight", (D, 3 * D), jnp.bfloat16, fixed_block(D, 3 * D)),
            ("vec", (8, D), jnp.float32, fixed_block(8, D)),
        ]
        scratch = [("columns", (D, LANES), jnp.bfloat16)]
    else:
        ins += [("weight", first[0], fixed_block(D, 3 * D)), ("vec", first[1], fixed_block(8, D))]
    return call(body, "attention", (len(spans),), 3 * len(spans), ins, outs, scratch, front)


def hidden_quarter(normed, upstream, up, down):
    hidden = dot(normed, up)
    grad_act = dot_rows(upstream, down)
    squared = hidden * hidden
    tilt = jnp.tanh(hidden * (gelu_scale + (gelu_scale * gelu_cubic) * squared))
    gate = 0.5 + 0.5 * tilt
    active = hidden * gate
    slope = gate + active * (1.0 - tilt) * (gelu_scale + (3.0 * gelu_scale * gelu_cubic) * squared)
    active = low(active)
    grad_hidden = low(grad_act * slope)
    return dot(active, down), dot_rows(grad_hidden, up), dot_columns(normed, grad_hidden), dot_columns(active, upstream)


def quarter_inputs(stacks, quarter):
    ins = []
    for name, group in (("up", quarter % 2), ("down", 2 + quarter % 2)):
        ins += [("%s%d" % (name, n), stack, fixed_block(8 * ROWS, QUARTER, group)) for n, stack in enumerate(stacks)]
    return ins


def quarter_call(quarter, seq, total, scalar, cotangent, stacks, ins, outs, before, after, micros, last=None):
    def body(r):
        span = pl.program_id(0)
        start = span == 0

        @pl.when(start)
        def _():
            assemble(r.me[0], (r.up0, r.up1, r.up2, r.up3), ((r.up, 0),))
            assemble(r.me[0], (r.down0, r.down1, r.down2, r.down3), ((r.down, 0),))

        normed = before(r, span)
        branch, back, grad_up, grad_down = hidden_quarter(normed, r.cot[...], r.up[...], r.down[...])
        add_into(r.grad_up, Ellipsis, grad_up, start)
        add_into(r.grad_down, Ellipsis, grad_down, start)
        after(r, branch, back, start)
        if last is not None:

            @pl.when(span == pl.num_programs(0) - 1)
            def _():
                last(r)

    scratch = [("up", (D, QUARTER), jnp.bfloat16), ("down", (QUARTER, D), jnp.bfloat16)]
    grads = [("grad_up", (D, QUARTER), jnp.float32), ("grad_down", (QUARTER, D), jnp.float32)]
    if last is None:
        outs = outs + [(name, shape, kind, fixed_block(*shape)) for name, shape, kind in grads]
    else:
        scratch = scratch + grads
    if any(entry[0] == "out_grad" for entry in outs):
        outs = [entry for entry in outs if entry[0] != "out_grad"]
        scratch = scratch + [("out_grad", (D, D), jnp.float32)]
    ins = [("me", scalar["me"], scalars()), ("cot", cotangent, row_block(seq, D))] + ins + quarter_inputs(stacks, quarter)
    return call(body, "hidden%d" % quarter, (total // seq,), micros, ins, outs, scratch)


def tall(name, total, seq, kind=jnp.float32):
    return (name, (total, D), kind, row_block(seq, D))


def hidden_forward_back(scalar, order, tokens, cotangent, vec, attended, stacks):
    seq = order.shape[2]
    total = tokens.shape[0]
    rows = row_block(seq, D)

    def enter(r, span):
        @pl.when(span == 0)
        def _():
            assemble(r.me[0], (r.out0, r.out1, r.out2, r.out3), ((r.out_full, 0),))

        middle = load_input(r.tokens, r.order, r.step[span], r.vec)[1] + dot(r.attended[...], r.out_full[...])
        r.middle[...] = middle
        normed = low(centre(middle)[0] * r.vec[1:2, :] + r.vec[3:4, :])
        r.normed[...] = normed
        return normed

    def leave_first(r, branch, back, start):
        r.branch[...] = r.middle[...] + branch
        r.back[...] = back

    ins = [("step", scalar["step"], scalars())] + span_inputs(order, tokens, seq)
    ins += [("vec", vec, fixed_block(8, D)), ("attended", attended, rows)]
    ins += [("out%d" % n, stack, fixed_block(8 * ROWS, D, 4)) for n, stack in enumerate(stacks)]
    outs = [tall("middle", total, seq), tall("normed", total, seq, jnp.bfloat16)]
    outs += [tall("branch", total, seq), tall("back", total, seq)]
    outs += [("out_full", (D, D), jnp.bfloat16, fixed_block(D, D))]
    one = quarter_call(0, seq, total, scalar, cotangent, stacks, ins, outs, enter, leave_first, 7)

    stacks, waits = yield one
    cotangent = tie(cotangent, *waits)

    def carried(last):
        return [("normed", one.normed, rows), ("branch_in", last.branch, rows), ("back_in", last.back, rows)]

    def leave(r, branch, back, start):
        r.branch[...] = r.branch_in[...] + branch
        r.back[...] = r.back_in[...] + back

    def arrange_half(r):
        arrange(r.me[0], (r.old_up, r.grad_up, r.old_down, r.grad_down), r.keep, r.send)

    def old(grads):
        return [("old_up", grads.grad_up, fixed_block(D, QUARTER)), ("old_down", grads.grad_down, fixed_block(QUARTER, D))]

    sums = [tall("branch", total, seq), tall("back", total, seq)]
    take = lambda r, span: r.normed[...]
    two = quarter_call(
        1, seq, total, scalar, cotangent, stacks, carried(one) + old(one), sums + arranged(4 * QUARTER), take, leave, 7, arrange_half
    )
    stacks, waits = yield two
    cotangent = tie(cotangent, *waits)
    three = quarter_call(2, seq, total, scalar, cotangent, stacks, carried(two), sums, take, leave, 7)

    def leave_last(r, branch, back, start):
        @pl.when(start)
        def _():
            r.dvec[...] = jnp.zeros_like(r.dvec)

        r.result[...] = low(r.branch_in[...] + branch)
        back = r.back_in[...] + back
        hat, scale = centre(r.middle[...])
        dmiddle = wide(r.cot[...]) + norm_back(back, r.vec[1:2, :], hat, scale)
        r.dmiddle[...] = dmiddle
        r.dvec[1:2, :] += jnp.sum(back * hat, axis=0, keepdims=True)
        r.dvec[3:4, :] += jnp.sum(back, axis=0, keepdims=True)
        mixed = low(dmiddle)
        r.dattended[...] = low(dot_rows(mixed, r.out_full[...]))
        add_into(r.out_grad, Ellipsis, dot_columns(r.attended[...], mixed), start)

    def arrange_last(r):
        arrange(r.me[0], (r.old_up, r.grad_up, r.old_down, r.grad_down, r.out_grad), r.keep, r.send)

    ins = carried(three) + old(three)
    ins += [("middle", one.middle, rows), ("vec", vec, fixed_block(8, D)), ("attended", attended, rows)]
    ins += [("out_full", one.out_full, fixed_block(D, D))]
    outs = [tall("result", total, seq, jnp.bfloat16), tall("dmiddle", total, seq), tall("dattended", total, seq, jnp.bfloat16)]
    outs += [("dvec", (8, D), jnp.float32, fixed_block(8, D)), ("out_grad", None, None, None)]
    outs += arranged(4 * QUARTER + D)
    stacks, waits = yield three
    cotangent = tie(cotangent, *waits)
    yield quarter_call(3, seq, total, scalar, cotangent, stacks, ins, outs, take, leave_last, 9, arrange_last)


def attention_back_part(scalar, pairs, normed, p, logs, dattended, seq):
    width = len(pairs) * LANES
    at = pairs[0] // len(pairs)
    groups = PAIRS // len(pairs)

    def body(r):
        span = pl.program_id(0)
        pair_gradients(r, pairs, r.length[span], seq, 0)
        add_into(r.grad, Ellipsis, dot_columns(r.normed[...], r.dp[...]), span == 0)

    total = normed.shape[0]
    ins = [("length", scalar["length"], scalars()), ("normed", normed, row_block(seq, D))]
    ins += pair_inputs(p, logs, dattended, seq, width, at, groups)
    outs = [("dp", (total, 3 * width), jnp.bfloat16, row_block(seq, 3 * width))]
    outs += [("grad", (D, 3 * width), jnp.float32, fixed_block(D, 3 * width))]
    return call(body, "attention_back", (total // seq,), 4.5 * len(pairs), ins, outs)


def pair_inputs(p, logs, dattended, seq, width, at, groups):
    return [
        ("q", p, row_block(seq, width, at)),
        ("k", p, row_block(seq, width, at + groups)),
        ("v", p, row_block(seq, width, at + 2 * groups)),
        ("logs", logs, pl.BlockSpec((1, PAIRS, 2 * seq), lambda i: (i, 0, 0))),
        ("dattended", dattended, row_block(seq, width, at)),
    ]


def pair_gradients(r, pairs, length, seq, column):
    width = len(pairs) * LANES
    for n, pair in enumerate(pairs):
        lanes = pl.ds(n * LANES, LANES)
        queries = pair_split(r.q[:, lanes], HEAD**-0.5)
        dattended = pair_split(r.dattended[:, lanes])
        keys = r.k[:, lanes]
        scores = key_scores(keys, queries, length)
        probability = jnp.exp(scores - r.logs[0, pair : pair + 1, :])
        dprobability = dot_rows(r.v[:, lanes], dattended)
        inner = jnp.sum(probability * dprobability, axis=0, keepdims=True)
        dscores = low(probability * (dprobability - inner))
        r.dp[:, pl.ds(column + 2 * width + n * LANES, LANES)] = low(dot(low(probability), dattended))
        r.dp[:, pl.ds(column + width + n * LANES, LANES)] = low(dot(dscores, queries))
        keys = jnp.transpose(low(wide(keys) * HEAD**-0.5))
        dqueries = jnp.concatenate([dot(keys[:HEAD], dscores[:, :seq]), dot(keys[HEAD:], dscores[:, seq:])], axis=0)
        r.dp[:, pl.ds(column + n * LANES, LANES)] = jnp.transpose(low(dqueries))


def attention_back_last(scalar, pairs, normed, p, logs, dattended, seq, order, tokens, vec, dmiddle, weight, dvec, parts):
    width = len(pairs) * LANES
    at = pairs[0] // len(pairs)
    groups = PAIRS // len(pairs)
    total = normed.shape[0]

    def body(r):
        span = pl.program_id(0)
        start = span == 0

        @pl.when(start)
        def _():
            r.dvec[...] = jnp.zeros_like(r.dvec)
            r.dvec[:8, :] = r.dvec_in[...]

        pair_gradients(r, pairs, r.length[span], seq, 0)
        add_into(r.grad, Ellipsis, dot_columns(r.normed[...], r.dp[...]), start)
        back = 0.0
        for n, part in enumerate(parts + [None]):
            dp = r.dp if part is None else getattr(r, "dp%d" % n)
            size = dp.shape[1] // 3
            for kind in range(3):
                columns = pl.ds(kind * D + n * size, size)
                back = back + dot_rows(dp[:, pl.ds(kind * size, size)], r.weight[:, columns])
        masked, started = load_input(r.tokens, r.order, r.step[span], r.vec)
        hat, scale = centre(started)
        dstarted = r.dmiddle[...] + norm_back(back, r.vec[0:1, :], hat, scale)
        r.dvec[0:1, :] += jnp.sum(back * hat, axis=0, keepdims=True)
        r.dvec[2:3, :] += jnp.sum(back, axis=0, keepdims=True)
        r.dvec[4:5, :] += jnp.sum(jnp.where(masked, dstarted, 0.0), axis=0, keepdims=True)
        r.input_grad[...] = jnp.where(masked, 0.0, dstarted)

        @pl.when(span == pl.num_programs(0) - 1)
        def _():
            r.columns[...] = jnp.transpose(r.dvec[...])
            grads = [getattr(r, "grad%d" % n) for n in range(len(parts))]
            arrange(r.me[0], grads + [r.grad, r.columns], r.keep, r.send)

    ins = [(name, array, scalars()) for name, array in scalar.items()] + span_inputs(order, tokens, seq)
    ins += [("normed", normed, row_block(seq, D)), ("vec", vec, fixed_block(8, D)), ("dmiddle", dmiddle, row_block(seq, D))]
    ins += [("weight", weight, fixed_block(D, 3 * D)), ("dvec_in", dvec, fixed_block(8, D))]
    ins += pair_inputs(p, logs, dattended, seq, width, at, groups)
    for n, part in enumerate(parts):
        ins += [("dp%d" % n, part.dp, row_block(seq, part.dp.shape[1]))]
        ins += [("grad%d" % n, part.grad, fixed_block(*part.grad.shape))]
    outs = [tall("input_grad", total, seq)] + arranged(3 * D + LANES)
    scratch = [
        ("dp", (seq, 3 * width), jnp.bfloat16),
        ("grad", (D, 3 * width), jnp.float32),
        ("dvec", (LANES, D), jnp.float32),
        ("columns", (D, LANES), jnp.float32),
    ]
    return call(body, "attention_back_last", (total // seq,), 4.5 * len(pairs) + 4, ins, outs, scratch)


def exchange(values, count, even_mask, odd_mask):
    pairs = [(i, i ^ (odd_mask if i % 2 else even_mask)) for i in range(count)]
    return lax.ppermute(values, AXES, pairs)


def tie(value, *others):
    return lax.optimization_barrier((value, others))[0]


class Gather:
    def __init__(self, piece, count):
        self.piece, self.count, self.direct = piece, count, piece.shape[0] == ROWS

    def far(self):
        if self.direct:
            parts = [self.piece] + [exchange(self.piece, self.count, offset, offset) for offset in FAR[1:]]
            self.piece = jnp.concatenate(parts, axis=0)
        return self.piece

    def near(self, *waits):
        if self.direct:
            taken = exchange(self.piece, self.count, 4, 2)
            self.piece = jnp.concatenate([self.piece, tie(taken, *waits)], axis=0)
        return self.piece

    def middle(self):
        if self.direct:
            self.late = exchange(self.piece, self.count, 2, 4)
            self.other = exchange(self.piece, self.count, 1, 1)
            return self.other
        return self.piece

    def finish(self, *waits):
        if not self.direct:
            return ordered_stacks(self.piece)
        late = tie(self.late, *waits)
        return (self.piece, late, self.other, exchange(late, self.count, 1, 1))


class Scatter:
    def __init__(self, arranged, count, direct):
        self.total, self.send, self.count, self.direct = arranged.keep, arranged.send, count, direct

    def fold(self, even, odd):
        if self.direct:
            total = self.total + wide(exchange(self.send, self.count, even, odd))
            half = total.shape[0] // 2
            self.total, self.send = total[:half], low(total[half:])
        return self.total, self.send

    def core(self):
        return self.fold(1, 1)

    def near(self):
        return self.fold(2, 4)

    def next(self):
        if self.direct:
            self.total = self.total + wide(exchange(self.send, self.count, 4, 2))
        return self.total

    def finish(self):
        if not self.direct:
            self.own = full_piece(self.total, self.send)
            return self.own
        own = self.total[:ROWS]
        for place in range(1, len(FAR)):
            part = low(self.total[place * ROWS : (place + 1) * ROWS])
            own = own + wide(exchange(part, self.count, FAR[place], FAR[place]))
        self.own = own
        return own


def split_units(up, down):
    rows, units = up.shape
    up = up.reshape(rows, units // 64, 4, ROWS)
    down = down.reshape(rows // ROWS, 4, ROWS, D)
    ups = [up[:, :, quarter].reshape(rows, units // 4) for quarter in range(4)]
    downs = [down[:, quarter].reshape(rows, D) for quarter in range(4)]
    return [jnp.concatenate(ups[n : n + 2] + downs[n : n + 2], axis=1) for n in (0, 2)]


def join_units(pieces):
    rows = pieces[0].shape[0]
    groups = [[piece[:, n * QUARTER : (n + 1) * QUARTER] for n in range(4)] for piece in pieces]
    ups = groups[0][:2] + groups[1][:2]
    downs = groups[0][2:] + groups[1][2:]
    up = jnp.stack([group.reshape(rows, QUARTER // ROWS, ROWS) for group in ups], axis=2)
    down = jnp.stack([group.reshape(rows // ROWS, ROWS, D) for group in downs], axis=1)
    return up.reshape(rows, 4 * QUARTER), down.reshape(rows * 4, D)


def stack_order(core):
    near = (0, 4, 2, 6) if core == 0 else (0, 2, 4, 6)
    return [core ^ group ^ offset for group in near for offset in FAR]


def ordered_stacks(piece):
    blocks = piece.reshape(32, ROWS, piece.shape[1])
    stacks = []
    for core in range(2):
        ordered = jnp.stack([blocks[device] for device in stack_order(core)])
        ordered = ordered.reshape(16 * ROWS, piece.shape[1])
        stacks += [ordered[: 8 * ROWS], ordered[8 * ROWS :]]
    return tuple(stacks)


def full_piece(keep, send):
    columns = keep.shape[1]
    blocks = jnp.concatenate([keep, wide(send)], axis=0).reshape(32, ROWS, columns)
    order = stack_order(0) + stack_order(1)
    return jnp.stack([blocks[order.index(device)] for device in range(32)]).reshape(32 * ROWS, columns)


def adam_update(master, gradient, moment, square, step_rate, decay_rate):
    moment_new = beta_first * moment + (1.0 - beta_first) * gradient
    square_new = beta_second * square + (1.0 - beta_second) * gradient * gradient
    corrected = (
        moment_new
        / (1.0 - beta_first**STEP)
        / (jnp.sqrt(square_new / (1.0 - beta_second**STEP)) + adam_epsilon)
    )
    return (moment_new, square_new, master - step_rate * (corrected + decay_rate * master))


def local(
    tokens,
    cotangent,
    reveal_order,
    reveal_step,
    lengths,
    weight_qkv,
    weight_out,
    weight_up,
    weight_down,
    vectors,
    moment_qkv,
    square_qkv,
    moment_out,
    square_out,
    moment_up,
    square_up,
    moment_down,
    square_down,
    moment_vec,
    square_vec,
):
    count = lax.axis_size("dp") * lax.axis_size("fsdp")
    direct = weight_qkv.shape[0] == ROWS and count == 32
    me = lax.axis_index("dp") * lax.axis_size("fsdp") + lax.axis_index("fsdp")
    me = (me if direct else 0 * me).astype(jnp.int32)[None]
    spans, seq = reveal_order.shape
    order = reveal_order.reshape(spans, 1, seq)
    flat = tokens.reshape(spans * seq, D)
    upstream = cotangent.reshape(spans * seq, D)

    halves = [low(weight_qkv), low(weight_out), low(weight_up), low(weight_down), low(vectors).T]
    if not direct:
        halves = [lax.all_gather(half, AXES, axis=0, tiled=True) for half in halves]
    qkv, out, up, down, columns = halves
    columns = jnp.pad(columns, ((0, 0), (0, LANES - columns.shape[1])))
    hidden = split_units(up, down)
    scalar = {"me": me, "step": reveal_step, "length": lengths}

    one = Gather(jnp.concatenate([qkv, columns], axis=1), count)
    one.far()
    one.near()
    two = Gather(tie(jnp.concatenate([hidden[0], out], axis=1), one.middle()), count)
    two.far()
    first = one.finish()
    front = attention(scalar, order, flat, first, range(0, spans // 2))
    two.near(front.logs)
    three = Gather(tie(hidden[1], front.logs), count)
    three.far()
    rear = attention(
        scalar, order, tie(flat, two.piece), (front.weight, front.vec), range(spans // 2, spans), front
    )
    vec, weight = front.vec, front.weight
    two.middle()
    second = two.finish(rear.logs)
    quarters = hidden_forward_back(scalar, order, flat, tie(upstream, three.piece), vec, rear.attended, second)
    three.near(next(quarters).back)
    half_one = quarters.send((second, [three.piece]))
    three.middle()
    third = three.finish(half_one.send)
    quarters.send((third, []))
    sum_one = Scatter(half_one, count, direct)
    half_two = quarters.send((third, sum_one.core()))
    sum_two = Scatter(half_two, count, direct)

    def part(pairs, *waits):
        dattended = tie(half_two.dattended, *waits)
        return attention_back_part(scalar, pairs, rear.normed, rear.p, rear.logs, dattended, seq)

    parts = [part((0,), *sum_one.near())]
    parts += [part((1,), *sum_two.core(), sum_one.next())]
    parts += [part((2,), *sum_two.near(), sum_one.finish())]
    final = attention_back_last(
        scalar, (3,), rear.normed, rear.p, rear.logs, tie(half_two.dattended, sum_two.next()), seq,
        order, flat, vec, half_two.dmiddle, weight, half_two.dvec, parts,
    )
    sum_three = Scatter(final, count, direct)
    for step in (sum_three.core, sum_three.near, sum_three.next):
        step()
    sums = [sum_one.own, sum_two.finish(), sum_three.finish()]
    grad_up, grad_down = join_units(sums[:2])
    order = [3 * pair + kind for kind in range(3) for pair in range(PAIRS)]
    columns = [sums[2][:, n * LANES : (n + 1) * LANES] for n in order]
    grads = (
        jnp.concatenate(columns, axis=1),
        sums[1][:, 4 * QUARTER :],
        grad_up,
        grad_down,
        sums[2][:, 3 * D : 3 * D + vectors.shape[0]],
    )
    if not direct:
        grads = [lax.psum_scatter(grad, AXES, scatter_dimension=0, tiled=True) for grad in grads]
    m_qkv, s_qkv, w_qkv = adam_update(weight_qkv, grads[0], moment_qkv, square_qkv, matrix_rate, weight_decay)
    m_out, s_out, w_out = adam_update(weight_out, grads[1], moment_out, square_out, output_rate, weight_decay)
    m_up, s_up, w_up = adam_update(weight_up, grads[2], moment_up, square_up, matrix_rate, weight_decay)
    m_down, s_down, w_down = adam_update(weight_down, grads[3], moment_down, square_down, matrix_rate, weight_decay)
    m_vec, s_vec, w_vec = adam_update(vectors, grads[4].T, moment_vec, square_vec, vector_rate, 0.0)
    return (
        half_two.result.reshape(tokens.shape),
        final.input_grad.reshape(tokens.shape),
        m_qkv,
        s_qkv,
        w_qkv,
        m_out,
        s_out,
        w_out,
        m_up,
        s_up,
        w_up,
        m_down,
        s_down,
        w_down,
        m_vec,
        s_vec,
        w_vec,
    )


def solution(mesh):
    return jax.shard_map(
        local,
        mesh=mesh,
        in_specs=(
            P(("dp", "fsdp"), None, None),
            P(("dp", "fsdp"), None, None),
            P(("dp", "fsdp"), None),
            P(("dp", "fsdp")),
            P(("dp", "fsdp")),
            P(("dp", "fsdp"), None),
            P(("dp", "fsdp"), None),
            P(("dp", "fsdp"), None),
            P(("dp", "fsdp"), None),
            P(None, ("dp", "fsdp")),
            P(("dp", "fsdp"), None),
            P(("dp", "fsdp"), None),
            P(("dp", "fsdp"), None),
            P(("dp", "fsdp"), None),
            P(("dp", "fsdp"), None),
            P(("dp", "fsdp"), None),
            P(("dp", "fsdp"), None),
            P(("dp", "fsdp"), None),
            P(None, ("dp", "fsdp")),
            P(None, ("dp", "fsdp")),
        ),
        out_specs=(
            P(("dp", "fsdp"), None, None),
            P(("dp", "fsdp"), None, None),
            P(("dp", "fsdp"), None),
            P(("dp", "fsdp"), None),
            P(("dp", "fsdp"), None),
            P(("dp", "fsdp"), None),
            P(("dp", "fsdp"), None),
            P(("dp", "fsdp"), None),
            P(("dp", "fsdp"), None),
            P(("dp", "fsdp"), None),
            P(("dp", "fsdp"), None),
            P(("dp", "fsdp"), None),
            P(("dp", "fsdp"), None),
            P(("dp", "fsdp"), None),
            P(None, ("dp", "fsdp")),
            P(None, ("dp", "fsdp")),
            P(None, ("dp", "fsdp")),
        ),
        check_vma=False,
    )
```

```python
import functools

import jax
import jax.numpy as jnp
from jax import lax
from jax.experimental import pallas as pl
from jax.experimental.pallas import tpu as pltpu
from jax.sharding import PartitionSpec as P

D = 512
HEADS = 8
HEAD = 64
FF = 2048
QUARTER = FF // 4
LANES = 128
PAIRS = D // LANES
ROWS = 16
STEP = 10
AXES = ("dp", "fsdp")
SCALE = 0.4
VMEM_BYTES = 16 * 1024 * 1024

norm_epsilon = 1e-05
beta_first = 0.9
beta_second = 0.999
adam_epsilon = 1e-08
weight_decay = 0.1
matrix_rate = 0.02
output_rate = 0.1
vector_rate = 0.2
masked_score = -1000000000.0
gelu_scale = 0.7978845608028654
gelu_cubic = 0.044715
FIRST_PAD = 224


def low(values):
    return values.astype(jnp.bfloat16)


def wide(values):
    return values.astype(jnp.float32)


def dot(left, right):
    return lax.dot_general(left, right, (((1,), (0,)), ((), ())), preferred_element_type=jnp.float32)


def dot_rows(left, right):
    return lax.dot_general(left, right, (((1,), (1,)), ((), ())), preferred_element_type=jnp.float32)


def dot_columns(left, right):
    return lax.dot_general(left, right, (((0,), (0,)), ((), ())), preferred_element_type=jnp.float32)


def cost(micros):
    return pl.CostEstimate(flops=int(micros * SCALE * 1.15e9), bytes_accessed=0, transcendentals=0)


class Refs:
    pass


def call(body, name, micros, ins, outs, scratch=(), reused=()):
    in_names, out_names = [entry[0] for entry in ins], [entry[0] for entry in outs]
    aliases = {in_names.index(taken): out_names.index(given) for taken, given in reused}
    names = [entry[0] for entry in ins] + [entry[0] for entry in outs] + [entry[0] for entry in scratch]

    def kernel(*refs):
        named = Refs()
        for entry, ref in zip(names, refs):
            setattr(named, entry, ref)
        body(named)

    results = pl.pallas_call(
        kernel,
        out_shape=[jax.ShapeDtypeStruct(shape, kind) for _, shape, kind in outs],
        in_specs=[entry[2] if len(entry) > 2 else whole() for entry in ins],
        out_specs=[whole() for _ in outs],
        scratch_shapes=[pltpu.VMEM(shape, kind) for _, shape, kind in scratch],
        compiler_params=pltpu.CompilerParams(vmem_limit_bytes=VMEM_BYTES),
        cost_estimate=cost(micros),
        input_output_aliases=aliases,
        name=name,
    )(*[entry[1] for entry in ins])
    out = Refs()
    for entry, value in zip(outs, results):
        setattr(out, entry[0], value)
    return out


def whole():
    return pl.BlockSpec(memory_space=pltpu.VMEM)


def scalars():
    return pl.BlockSpec(memory_space=pltpu.SMEM)


FAR = (0, 8, 16, 24)


def block_device(me, core, place):
    first = jnp.where(core == 0, 4, 2)
    near = (0, first, 6 - first, 6)[place // len(FAR)]
    return me ^ near ^ FAR[place % len(FAR)]


def assemble(me, stacks, targets):
    for stream in range(2):
        for upper in range(2):
            stack = stacks[2 * stream + upper]
            for place in range(8):
                device = block_device(me ^ stream, (me & 1) ^ stream, place + upper * 8)
                rows = pl.ds(pl.multiple_of(device * ROWS, ROWS), ROWS)
                for ref, column in targets:
                    ref[rows, :] = stack[pl.ds(place * ROWS, ROWS), pl.ds(column, ref.shape[1])]


def arrange(me, sources, keep_ref, send_ref):
    for place in range(16):
        here = pl.ds(place * ROWS, ROWS)
        for stream, out in ((0, keep_ref), (1, send_ref)):
            device = block_device(me ^ stream, (me & 1) ^ stream, place)
            rows = pl.ds(pl.multiple_of(device * ROWS, ROWS), ROWS)
            at = 0
            for ref in sources:
                out[here, pl.ds(at, ref.shape[1])] = ref[rows, :].astype(out.dtype)
                at += ref.shape[1]


def arranged(columns):
    shape = (16 * ROWS, columns)
    return [("keep", shape, jnp.float32), ("send", shape, jnp.bfloat16)]


def centre(values):
    centred = values - jnp.mean(values, axis=-1, keepdims=True)
    scale = lax.rsqrt(jnp.mean(centred * centred, axis=-1, keepdims=True) + norm_epsilon)
    return centred * scale, scale


def norm_back(grad, gain, hat, scale):
    inner = grad * gain
    return scale * (
        inner - jnp.mean(inner, axis=-1, keepdims=True) - hat * jnp.mean(inner * hat, axis=-1, keepdims=True)
    )


def masked_rows(order_row, step):
    seq = order_row.shape[1]
    flags = jnp.where(order_row >= step, 1.0, 0.0)
    column = jnp.transpose(jnp.broadcast_to(flags, (LANES, seq)))
    return jnp.concatenate([column] * (D // LANES), axis=1) > 0.5


def pair_split(pair, scale=None):
    lane = lax.broadcasted_iota(jnp.int32, pair.shape, 1)
    values = wide(pair)
    if scale is not None:
        values = values * scale
    return jnp.concatenate([low(jnp.where(lane < HEAD, values, 0.0)), low(jnp.where(lane < HEAD, 0.0, values))], axis=0)


def key_scores(keys, both_queries, length):
    scores = dot_rows(keys, both_queries)
    seq = scores.shape[0]
    tail = scores[FIRST_PAD:]
    row = lax.broadcasted_iota(jnp.int32, tail.shape, 0) + FIRST_PAD
    return jnp.concatenate([scores[:FIRST_PAD], jnp.where(row < length, tail, masked_score)], axis=0)


def load_input(r, span, rows):
    masked = masked_rows(r.order[span], r.step[span])
    return masked, jnp.where(masked, r.vec[4:5, :], wide(r.tokens[rows, :]))


def span_rows(seq, spans):
    return [(span, pl.ds(span * seq, seq)) for span in spans]


def attention(scalar, order, tokens, first, spans, front=None):
    count, _, seq = order.shape
    fresh = front is None

    def body(r):
        if fresh:
            stacks = (r.stack0, r.stack1, r.stack2, r.stack3)
            assemble(r.me[0], stacks, ((r.weight, 0), (r.columns, 3 * D)))
            r.vec[...] = jnp.transpose(wide(r.columns[...]))[:8]
        else:
            for name in ("normed", "p", "attended"):
                old = getattr(r, "front_" + name)
                getattr(r, name)[pl.ds(0, old.shape[0]), :] = old[...]
            r.logs[: spans[0]] = r.front_logs[...]
        for span, rows in span_rows(seq, spans):
            started = load_input(r, span, rows)[1]
            normed = low(centre(started)[0] * r.vec[0:1, :] + r.vec[2:3, :])
            r.normed[rows, :] = normed
            r.p[rows, :] = low(dot(normed, r.weight[...]))
            for pair in range(PAIRS):
                lanes = pl.ds(pair * LANES, LANES)
                queries = pair_split(r.p[rows, lanes], HEAD**-0.5)
                scores = key_scores(r.p[rows, pl.ds(D + pair * LANES, LANES)], queries, r.length[span])
                peak = jnp.max(scores, axis=0, keepdims=True)
                exped = jnp.exp(scores - peak)
                total = jnp.sum(exped, axis=0, keepdims=True)
                probability = low(exped / total)
                r.logs[span, pair : pair + 1, :] = peak + jnp.log(total)
                values = jnp.transpose(r.p[rows, pl.ds(2 * D + pair * LANES, LANES)])
                attended = jnp.concatenate(
                    [dot(values[:HEAD], probability[:, :seq]), dot(values[HEAD:], probability[:, seq:])], axis=0
                )
                r.attended[rows, lanes] = jnp.transpose(low(attended))

    ins = [(name, array, scalars()) for name, array in scalar.items()] + [("order", order), ("tokens", tokens)]
    count = spans[-1] + 1
    rows = count * seq
    outs = [
        ("normed", (rows, D), jnp.bfloat16),
        ("p", (rows, 3 * D), jnp.bfloat16),
        ("attended", (rows, D), jnp.bfloat16),
        ("logs", (count, PAIRS, 2 * seq), jnp.float32),
    ]
    scratch = []
    if fresh:
        ins += [("stack%d" % n, stack) for n, stack in enumerate(first)]
        outs += [("weight", (D, 3 * D), jnp.bfloat16), ("vec", (8, D), jnp.float32)]
        scratch = [("columns", (D, LANES), jnp.bfloat16)]
    else:
        ins += [("weight", front.weight), ("vec", front.vec)]
        ins += [("front_" + name, getattr(front, name)) for name in ("normed", "p", "attended", "logs")]
    return call(body, "attention", 3 * len(spans), ins, outs, scratch)


def hidden_quarter(normed, upstream, up, down):
    hidden = dot(normed, up)
    grad_act = dot_rows(upstream, down)
    squared = hidden * hidden
    tilt = jnp.tanh(hidden * (gelu_scale + (gelu_scale * gelu_cubic) * squared))
    gate = 0.5 + 0.5 * tilt
    active = hidden * gate
    slope = gate + active * (1.0 - tilt) * (gelu_scale + (3.0 * gelu_scale * gelu_cubic) * squared)
    grad_hidden = low(grad_act * slope)
    return low(active), grad_hidden, dot_rows(grad_hidden, up)


def quarter_call(quarter, scalar, cotangent, stacks, ins, outs, seq, before, after, micros, reused=(), mate=None):
    total = cotangent.shape[0]
    column = 2 * QUARTER * (quarter % 2)

    def body(r):
        stacks = (r.stack0, r.stack1, r.stack2, r.stack3)
        targets = [(r.up, column), (r.down_full, column + QUARTER)]
        if quarter == 0:
            targets.append((r.out_full, 4 * QUARTER))
        assemble(r.me[0], stacks, targets)
        for span, rows in span_rows(seq, range(total // seq)):
            normed = before(r, span, rows)
            active, grad_hidden, back = hidden_quarter(normed, r.cot[rows, :], r.up[...], r.down_full[...])
            r.active[rows, :] = active
            r.grad_hidden[rows, :] = grad_hidden
            after(r, rows, back)
        r.grad_up[...] = dot_columns(r.middle_normed[...], r.grad_hidden[...])
        r.grad_down[...] = dot_columns(r.active[...], r.cot[...])
        if mate is not None:
            arrange(r.me[0], (r.mate_up, r.mate_down, r.grad_up, r.grad_down), r.keep, r.send)

    ins = [("me", scalar["me"], scalars()), ("cot", cotangent)] + ins
    ins += [("stack%d" % n, stack) for n, stack in enumerate(stacks)]
    outs = outs + [("active", (total, QUARTER), jnp.bfloat16), ("down_full", (QUARTER, D), jnp.bfloat16)]
    grads = [("grad_up", (D, QUARTER), jnp.float32), ("grad_down", (QUARTER, D), jnp.float32)]
    scratch = [("up", (D, QUARTER), jnp.bfloat16), ("grad_hidden", (total, QUARTER), jnp.bfloat16)]
    if mate is None:
        outs = outs + grads
    else:
        ins += [("mate_up", mate.grad_up), ("mate_down", mate.grad_down)]
        outs = outs + arranged(4 * QUARTER)
        scratch = scratch + grads
    return call(body, "hidden%d" % quarter, micros, ins, outs, scratch, reused)


def first_quarter(scalar, order, tokens, cotangent, vec, attended, stacks):
    seq = order.shape[2]
    total = tokens.shape[0]

    def enter(r, span, rows):
        middle = load_input(r, span, rows)[1] + dot(r.attended[rows, :], r.out_full[...])
        r.middle[rows, :] = middle
        normed = low(centre(middle)[0] * r.vec[1:2, :] + r.vec[3:4, :])
        r.middle_normed[rows, :] = normed
        return normed

    def leave(r, rows, back):
        r.back[rows, :] = back

    ins = [("step", scalar["step"], scalars()), ("order", order), ("tokens", tokens), ("vec", vec), ("attended", attended)]
    outs = [("middle", (total, D), jnp.float32), ("middle_normed", (total, D), jnp.bfloat16)]
    outs += [("back", (total, D), jnp.float32), ("out_full", (D, D), jnp.bfloat16)]
    return quarter_call(0, scalar, cotangent, stacks, ins, outs, seq, enter, leave, 8.5)


def next_quarter(quarter, scalar, cotangent, stacks, normed, back, seq, mate=None):
    total = normed.shape[0]

    def take(r, span, rows):
        return r.middle_normed[rows, :]

    def leave(r, rows, back):
        r.back[rows, :] = r.old_back[rows, :] + back

    ins = [("middle_normed", normed), ("old_back", back)]
    outs = [("back", (total, D), jnp.float32)]
    reused = [("old_back", "back")]
    return quarter_call(quarter, scalar, cotangent, stacks, ins, outs, seq, take, leave, 6.5, reused, mate)


def middle_back(scalar, cotangent, vec, attended, middle, back, out_full, seq, quarters):
    total = middle.shape[0]

    def body(r):
        sums = [0.0, 0.0]
        for span, rows in span_rows(seq, range(total // seq)):
            back = r.back[rows, :]
            hat, scale = centre(r.middle[rows, :])
            dmiddle = wide(r.cot[rows, :]) + norm_back(back, r.vec[1:2, :], hat, scale)
            r.dmiddle[rows, :] = dmiddle
            sums[0] = sums[0] + jnp.sum(back * hat, axis=0, keepdims=True)
            sums[1] = sums[1] + jnp.sum(back, axis=0, keepdims=True)
            mixed = low(dmiddle)
            r.mixed[rows, :] = mixed
            r.dattended[rows, :] = low(dot_rows(mixed, r.out_full[...]))
        r.dvec[...] = jnp.zeros_like(r.dvec)
        r.dvec[1:2, :] = sums[0]
        r.dvec[3:4, :] = sums[1]
        r.grad_out[...] = dot_columns(r.attended[...], r.mixed[...])
        arrange(r.me[0], (r.up0, r.down0, r.up1, r.down1, r.grad_out), r.keep, r.send)

    ins = [("me", scalar["me"], scalars()), ("cot", cotangent), ("vec", vec), ("attended", attended)]
    ins += [("middle", middle), ("back", back), ("out_full", out_full)]
    for n, quarter in enumerate(quarters):
        ins += [("up%d" % n, quarter.grad_up), ("down%d" % n, quarter.grad_down)]
    outs = [("dmiddle", (total, D), jnp.float32), ("dattended", (total, D), jnp.bfloat16), ("dvec", (8, D), jnp.float32)]
    outs += arranged(4 * QUARTER + D)
    scratch = [("grad_out", (D, D), jnp.float32), ("mixed", (total, D), jnp.bfloat16)]
    return call(body, "middle_back", 4, ins, outs, scratch)


def branch_output(middle, quarters, seq, spans, front=None):
    def body(r):
        if front is not None:
            r.result[pl.ds(0, front.shape[0]), :] = r.front[...]
        for _, rows in span_rows(seq, spans):
            result = r.middle[rows, :]
            for n in range(4):
                result = result + dot(getattr(r, "active%d" % n)[rows, :], getattr(r, "down%d" % n)[...])
            r.result[rows, :] = low(result)

    ins = [("middle", middle)]
    for n, quarter in enumerate(quarters):
        ins += [("active%d" % n, quarter.active), ("down%d" % n, quarter.down_full)]
    if front is not None:
        ins += [("front", front)]
    return call(body, "branch_output", 25, ins, [("result", ((spans[-1] + 1) * seq, D), jnp.bfloat16)]).result


def attention_back(scalar, pair, normed, p, logs, dattended, seq):
    total = normed.shape[0]
    last = pair == PAIRS - 1

    def body(r):
        for span, rows in span_rows(seq, range(total // seq)):
            queries = pair_split(r.p[rows, pl.ds(pair * LANES, LANES)], HEAD**-0.5)
            dattended = pair_split(r.dattended[rows, pl.ds(pair * LANES, LANES)])
            keys = r.p[rows, pl.ds(D + pair * LANES, LANES)]
            scores = key_scores(keys, queries, r.length[span])
            probability = jnp.exp(scores - r.logs[span, pair : pair + 1, :])
            dprobability = dot_rows(r.p[rows, pl.ds(2 * D + pair * LANES, LANES)], dattended)
            inner = jnp.sum(probability * dprobability, axis=0, keepdims=True)
            dscores = low(probability * (dprobability - inner))
            dvalues = low(dot(low(probability), dattended))
            dkeys = low(dot(dscores, queries))
            keys = jnp.transpose(low(wide(keys) * HEAD**-0.5))
            dqueries = jnp.concatenate([dot(keys[:HEAD], dscores[:, :seq]), dot(keys[HEAD:], dscores[:, seq:])], axis=0)
            r.dp[rows, :] = jnp.concatenate([jnp.transpose(low(dqueries)), dkeys, dvalues], axis=1)
        if not last:
            r.grad[...] = dot_columns(r.normed[...], r.dp[...])

    ins = [("me", scalar["me"], scalars()), ("length", scalar["length"], scalars())]
    ins += [("normed", normed), ("p", p), ("logs", logs), ("dattended", dattended)]
    outs = [("dp", (total, 3 * LANES), jnp.bfloat16)]
    if not last:
        outs += [("grad", (D, 3 * LANES), jnp.float32)]
    return call(body, "attention_back", 4.6, ins, outs)


def input_back(scalar, order, tokens, vec, normed, dmiddle, weight, dvec, parts):
    seq = order.shape[2]
    total = tokens.shape[0]

    def body(r):
        parts = [getattr(r, "dp%d" % n) for n in range(PAIRS)]
        sums = [0.0, 0.0, 0.0]
        for span, rows in span_rows(seq, range(total // seq)):
            dp = [part[rows, pl.ds(kind * LANES, LANES)] for kind in range(3) for part in parts]
            back = dot_rows(jnp.concatenate(dp, axis=1), r.weight[...])
            masked, started = load_input(r, span, rows)
            hat, scale = centre(started)
            dstarted = r.dmiddle[rows, :] + norm_back(back, r.vec[0:1, :], hat, scale)
            r.input_grad[rows, :] = jnp.where(masked, 0.0, dstarted)
            sums[0] = sums[0] + jnp.sum(back * hat, axis=0, keepdims=True)
            sums[1] = sums[1] + jnp.sum(back, axis=0, keepdims=True)
            sums[2] = sums[2] + jnp.sum(jnp.where(masked, dstarted, 0.0), axis=0, keepdims=True)
        r.dvec[...] = jnp.zeros_like(r.dvec)
        r.dvec[:8, :] = r.dvec_in[...]
        for row, value in zip((0, 2, 4), sums):
            r.dvec[row : row + 1, :] = value
        r.columns[...] = jnp.transpose(r.dvec[...])
        r.grad[...] = dot_columns(r.normed[...], parts[-1][...])
        arrange(r.me[0], (r.grad0, r.grad1, r.grad2, r.grad, r.columns), r.keep, r.send)

    ins = [("me", scalar["me"], scalars()), ("step", scalar["step"], scalars()), ("order", order), ("tokens", tokens)]
    ins += [("vec", vec), ("dmiddle", dmiddle), ("normed", normed), ("weight", weight), ("dvec_in", dvec)]
    ins += [("dp%d" % n, part.dp) for n, part in enumerate(parts)]
    ins += [("grad%d" % n, part.grad) for n, part in enumerate(parts[:-1])]
    outs = [("input_grad", (total, D), jnp.float32)] + arranged(3 * D + LANES)
    scratch = [
        ("dvec", (LANES, D), jnp.float32),
        ("columns", (D, LANES), jnp.float32),
        ("grad", (D, 3 * LANES), jnp.float32),
    ]
    return call(body, "input_back", 6.5, ins, outs, scratch)


def fold_kernel(keep_ref, taken_ref, total_ref, send_ref):
    half = total_ref.shape[0]
    total_ref[...] = keep_ref[:half, :] + wide(taken_ref[:half, :])
    send_ref[...] = low(keep_ref[half:, :] + wide(taken_ref[half:, :]))


def fold(keep, taken):
    rows, columns = keep.shape
    return pl.pallas_call(
        fold_kernel,
        out_shape=(
            jax.ShapeDtypeStruct((rows // 2, columns), jnp.float32),
            jax.ShapeDtypeStruct((rows // 2, columns), jnp.bfloat16),
        ),
        in_specs=[whole()] * 2,
        out_specs=(whole(), whole()),
        compiler_params=pltpu.CompilerParams(vmem_limit_bytes=VMEM_BYTES),
        cost_estimate=cost(1),
        name="fold",
    )(keep, taken)


def adam_update(master, gradient, moment, square, step_rate, decay_rate):
    moment_new = beta_first * moment + (1.0 - beta_first) * gradient
    square_new = beta_second * square + (1.0 - beta_second) * gradient * gradient
    corrected = (
        moment_new
        / (1.0 - beta_first**STEP)
        / (jnp.sqrt(square_new / (1.0 - beta_second**STEP)) + adam_epsilon)
    )
    return (moment_new, square_new, master - step_rate * (corrected + decay_rate * master))


def unit_order():
    unit = lax.broadcasted_iota(jnp.int32, (D, D), 0)
    place = lax.broadcasted_iota(jnp.int32, (D, D), 1)
    wanted = (place % LANES // ROWS) * 64 + (place // LANES) * ROWS + place % ROWS
    return jnp.where(unit == wanted, 1.0, 0.0).astype(jnp.bfloat16)


def hidden_update_kernel(*refs):
    halves = (refs[0:4], refs[4:8])
    up, down, out = refs[8:11], refs[11:14], refs[14:17]
    new_up, new_down, new_out = refs[17:20], refs[20:23], refs[23:26]

    def summed(half, columns):
        return half[0][:ROWS, columns] + sum(wide(part[:, columns]) for part in half[1:])

    def update(new, old, index, grad, rate):
        results = adam_update(old[0][index], grad, old[1][index], old[2][index], rate, weight_decay)
        for ref, value in zip(new, results):
            ref[index] = value

    sort = unit_order()
    for group in range(FF // D):
        grads = []
        for quarter in range(4):
            columns = pl.ds((quarter % 2) * 2 * QUARTER + group * LANES, LANES)
            grads.append(summed(halves[quarter // 2], columns))
        rest = jnp.concatenate(grads, axis=1)
        grad = 0.0
        for _ in range(3):
            piece = low(rest)
            grad = grad + dot_rows(piece, sort)
            rest = rest - wide(piece)
        update(new_up, up, (slice(None), pl.ds(group * D, D)), grad, matrix_rate)
    for quarter in range(4):
        grad = summed(halves[quarter // 2], pl.ds((quarter % 2) * 2 * QUARTER + QUARTER, D))
        update(new_down, down, (pl.ds(quarter * ROWS, ROWS), slice(None)), grad, matrix_rate)
    update(new_out, out, Ellipsis, summed(halves[1], pl.ds(4 * QUARTER, D)), output_rate)


def hidden_update(total_one, parts_one, total_two, parts_two, up, down, out):
    outs = [jax.ShapeDtypeStruct(state[0].shape, jnp.float32) for state in (up, down, out) for _ in range(3)]
    results = pl.pallas_call(
        hidden_update_kernel,
        out_shape=outs,
        in_specs=[whole()] * 17,
        out_specs=[whole()] * 9,
        compiler_params=pltpu.CompilerParams(vmem_limit_bytes=VMEM_BYTES),
        cost_estimate=cost(3),
        name="hidden_update",
    )(total_one, *parts_one, total_two, *parts_two, *up, *down, *out)
    return results[:3], results[3:6], results[6:]


def last_update_kernel(*refs):
    total, one, two, three = refs[:4]
    qkv, vec = refs[4:7], refs[7:10]
    new_qkv, new_vec = refs[10:13], refs[13:16]
    for pair in range(PAIRS):
        for kind in range(3):
            there = pl.ds((3 * pair + kind) * LANES, LANES)
            here = pl.ds((kind * PAIRS + pair) * LANES, LANES)
            grad = total[:ROWS, there] + sum(wide(part[:, there]) for part in (one, two, three))
            moment, square, master = adam_update(
                qkv[0][:, here], grad, qkv[1][:, here], qkv[2][:, here], matrix_rate, weight_decay
            )
            new_qkv[0][:, here], new_qkv[1][:, here], new_qkv[2][:, here] = moment, square, master
    there = pl.ds(3 * D, LANES)
    grad = total[:ROWS, there] + sum(wide(part[:, there]) for part in (one, two, three))
    grad = jnp.transpose(jnp.concatenate([grad, jnp.zeros((LANES - ROWS, LANES), jnp.float32)], axis=0))
    grad = grad[: vec[0].shape[0], :ROWS]
    results = adam_update(vec[0][...], grad, vec[1][...], vec[2][...], vector_rate, 0.0)
    for ref, value in zip(new_vec, results):
        ref[...] = value


def last_update(total, taken, qkv, vec):
    outs = [jax.ShapeDtypeStruct(qkv[0].shape, jnp.float32)] * 3 + [jax.ShapeDtypeStruct(vec[0].shape, jnp.float32)] * 3
    results = pl.pallas_call(
        last_update_kernel,
        out_shape=outs,
        in_specs=[whole()] * 10,
        out_specs=[whole()] * 6,
        compiler_params=pltpu.CompilerParams(vmem_limit_bytes=VMEM_BYTES),
        cost_estimate=cost(1),
        name="last_update",
    )(total, *taken, *qkv, *vec)
    return results[:3], results[3:]


def exchange(values, count, even_mask, odd_mask):
    pairs = [(i, i ^ (odd_mask if i % 2 else even_mask)) for i in range(count)]
    return lax.ppermute(values, AXES, pairs)


def tie(value, *others):
    return lax.optimization_barrier((value, others))[0]


class Gather:
    def __init__(self, piece, count):
        self.piece, self.count, self.direct = piece, count, piece.shape[0] == ROWS

    def far(self):
        if self.direct:
            parts = [self.piece] + [exchange(self.piece, self.count, offset, offset) for offset in FAR[1:]]
            self.piece = jnp.concatenate(parts, axis=0)
        return self.piece

    def near(self, *waits):
        if self.direct:
            taken = exchange(self.piece, self.count, 4, 2)
            self.piece = jnp.concatenate([self.piece, tie(taken, *waits)], axis=0)
        return self.piece

    def middle(self):
        if self.direct:
            self.late = exchange(self.piece, self.count, 2, 4)
            self.other = exchange(self.piece, self.count, 1, 1)
            return self.other
        return self.piece

    def finish(self, *waits):
        if not self.direct:
            return ordered_stacks(self.piece)
        late = tie(self.late, *waits)
        return (self.piece, late, self.other, exchange(late, self.count, 1, 1))


class Scatter:
    def __init__(self, arranged, count, direct):
        self.total, self.send, self.count, self.direct = arranged.keep, arranged.send, count, direct

    def step(self, even, odd, *waits):
        if self.direct:
            self.total, self.send = fold(self.total, tie(exchange(self.send, self.count, even, odd), *waits))
        return self.total, self.send

    def core(self, *waits):
        return self.step(1, 1, *waits)

    def near(self, *waits):
        return self.step(2, 4, *waits)

    def next(self, *waits):
        if self.direct:
            self.total = self.total + wide(tie(exchange(self.send, self.count, 4, 2), *waits))
        return self.total

    def parts(self, *waits):
        if not self.direct:
            return []
        taken = []
        for place in range(1, len(FAR)):
            part = low(self.total[place * ROWS : (place + 1) * ROWS])
            taken.append(tie(exchange(part, self.count, FAR[place], FAR[place]), *waits))
        return taken

    def full(self):
        return full_piece(self.total, self.send)


def split_units(up, down):
    rows, units = up.shape
    up = up.reshape(rows, units // 64, 4, ROWS)
    down = down.reshape(rows // ROWS, 4, ROWS, D)
    ups = [up[:, :, quarter].reshape(rows, units // 4) for quarter in range(4)]
    downs = [down[:, quarter].reshape(rows, D) for quarter in range(4)]
    return [jnp.concatenate([ups[n], downs[n], ups[n + 1], downs[n + 1]], axis=1) for n in (0, 2)]


def pack_kernel(out_ref, up_ref, down_ref, second_ref, third_ref):
    sort = unit_order()
    for group in range(FF // D):
        mixed = low(dot(low(up_ref[:, pl.ds(group * D, D)]), sort))
        for quarter in range(4):
            piece = (second_ref, third_ref)[quarter // 2]
            column = (quarter % 2) * 2 * QUARTER + group * LANES
            piece[:, pl.ds(column, LANES)] = mixed[:, quarter * LANES : (quarter + 1) * LANES]
    for quarter in range(4):
        piece = (second_ref, third_ref)[quarter // 2]
        rows = down_ref[pl.ds(quarter * ROWS, ROWS), :]
        piece[:, pl.ds((quarter % 2) * 2 * QUARTER + QUARTER, D)] = low(rows)
    second_ref[:, pl.ds(4 * QUARTER, D)] = low(out_ref[...])


def pack(out, up, down):
    return pl.pallas_call(
        pack_kernel,
        out_shape=(
            jax.ShapeDtypeStruct((ROWS, 4 * QUARTER + D), jnp.bfloat16),
            jax.ShapeDtypeStruct((ROWS, 4 * QUARTER), jnp.bfloat16),
        ),
        in_specs=[whole()] * 3,
        out_specs=(whole(), whole()),
        compiler_params=pltpu.CompilerParams(vmem_limit_bytes=VMEM_BYTES),
        cost_estimate=cost(1),
        name="pack",
    )(out, up, down)


def join_units(pieces):
    rows = pieces[0].shape[0]
    groups = [[piece[:, n * QUARTER : (n + 1) * QUARTER] for n in range(4)] for piece in pieces]
    ups = [groups[0][0], groups[0][2], groups[1][0], groups[1][2]]
    downs = [groups[0][1], groups[0][3], groups[1][1], groups[1][3]]
    up = jnp.stack([group.reshape(rows, QUARTER // ROWS, ROWS) for group in ups], axis=2)
    down = jnp.stack([group.reshape(rows // ROWS, ROWS, D) for group in downs], axis=1)
    return up.reshape(rows, 4 * QUARTER), down.reshape(rows * 4, D)


def stack_order(core):
    near = (0, 4, 2, 6) if core == 0 else (0, 2, 4, 6)
    return [core ^ group ^ offset for group in near for offset in FAR]


def ordered_stacks(piece):
    blocks = piece.reshape(32, ROWS, piece.shape[1])
    stacks = []
    for core in range(2):
        ordered = jnp.stack([blocks[device] for device in stack_order(core)])
        ordered = ordered.reshape(16 * ROWS, piece.shape[1])
        stacks += [ordered[: 8 * ROWS], ordered[8 * ROWS :]]
    return tuple(stacks)


def full_piece(keep, send):
    columns = keep.shape[1]
    blocks = jnp.concatenate([keep, wide(send)], axis=0).reshape(32, ROWS, columns)
    order = stack_order(0) + stack_order(1)
    return jnp.stack([blocks[order.index(device)] for device in range(32)]).reshape(32 * ROWS, columns)


def local(
    tokens,
    cotangent,
    reveal_order,
    reveal_step,
    lengths,
    weight_qkv,
    weight_out,
    weight_up,
    weight_down,
    vectors,
    moment_qkv,
    square_qkv,
    moment_out,
    square_out,
    moment_up,
    square_up,
    moment_down,
    square_down,
    moment_vec,
    square_vec,
):
    count = lax.axis_size("dp") * lax.axis_size("fsdp")
    direct = weight_qkv.shape[0] == ROWS and count == 32
    me = lax.axis_index("dp") * lax.axis_size("fsdp") + lax.axis_index("fsdp")
    me = (me if direct else 0 * me).astype(jnp.int32)[None]
    spans, seq = reveal_order.shape
    order = reveal_order.reshape(spans, 1, seq)
    flat = tokens.reshape(spans * seq, D)
    upstream = cotangent.reshape(spans * seq, D)

    columns = jnp.pad(low(vectors).T, ((0, 0), (0, LANES - vectors.shape[0])))
    qkv = jnp.concatenate([low(weight_qkv), columns], axis=1)
    if direct:
        piece_two, piece_three = pack(weight_out, tie(weight_up, qkv), weight_down)
    else:
        halves = [qkv, low(weight_out), low(weight_up), low(weight_down)]
        qkv, out, up, down = [lax.all_gather(half, AXES, axis=0, tiled=True) for half in halves]
        hidden = split_units(up, down)
        piece_two, piece_three = jnp.concatenate([hidden[0], out], axis=1), hidden[1]
    scalar = {"me": me, "step": reveal_step, "length": lengths}

    one = Gather(qkv, count)
    one.far()
    one.near()
    two = Gather(tie(piece_two, one.middle()), count)
    two.far()
    first = one.finish()
    front = attention(scalar, order, flat, first, range(0, spans // 2))
    two.near(front.logs)
    three = Gather(tie(piece_three, front.logs), count)
    three.far()
    rear = attention(
        scalar, order, tie(flat, two.piece), None, range(spans // 2, spans), front
    )
    vec, weight = front.vec, front.weight
    two.middle()
    second = two.finish(rear.logs)
    h = [first_quarter(scalar, order, flat, tie(upstream, three.piece), vec, rear.attended, second)]
    normed = h[0].middle_normed
    three.near(h[0].back)
    h += [next_quarter(1, scalar, tie(upstream, three.piece), second, normed, h[0].back, seq, h[0])]
    three.middle()
    third = three.finish(h[1].back)
    h += [next_quarter(2, scalar, upstream, third, normed, h[1].back, seq)]
    sum_one = Scatter(h[1], count, direct)
    h += [next_quarter(3, scalar, tie(upstream, *sum_one.core(h[2].back)), third, normed, h[2].back, seq)]
    turn = middle_back(
        scalar, tie(upstream, h[3].back), vec, rear.attended, h[0].middle, h[3].back, h[0].out_full, seq, h[2:]
    )
    sum_one.near(turn.dattended)
    sum_two = Scatter(turn, count, direct)

    def part(*waits):
        pair = len(parts)
        dattended = tie(turn.dattended, *waits)
        return attention_back(scalar, pair, rear.normed, rear.p, rear.logs, dattended, seq)

    parts = []
    parts += [part(sum_one.total)]
    parts += [part(sum_one.next(parts[0].dp), *sum_two.core(parts[0].dp))]
    parts_one = sum_one.parts(parts[1].dp)
    parts += [part(*parts_one)]
    parts += [part(*sum_two.near(parts[2].dp))]
    ready = tie(flat, parts[3].dp, sum_two.next(parts[3].dp))
    final = input_back(scalar, order, ready, vec, rear.normed, turn.dmiddle, weight, turn.dvec, parts)
    sum_three = Scatter(final, count, direct)
    parts_two = sum_two.parts(final.input_grad)
    result = branch_output(tie(h[0].middle, *parts_two), h, seq, range(0, spans // 2))
    sum_three.core(result)
    result = branch_output(tie(h[0].middle, sum_three.total), h, seq, range(spans // 2, spans), result)
    sum_three.near(result)
    qkv_state = (weight_qkv, moment_qkv, square_qkv)
    vec_state = (vectors, moment_vec, square_vec)
    out_state = (weight_out, moment_out, square_out)
    up_state = (weight_up, moment_up, square_up)
    down_state = (weight_down, moment_down, square_down)
    if direct:
        total_one = tie(sum_one.total, sum_three.total)
        states = hidden_update(total_one, parts_one, sum_two.total, parts_two, up_state, down_state, out_state)
        new_up, new_down, new_out = states
        sum_three.next(*new_up, *new_down)
        new_qkv, new_vec = last_update(sum_three.total, sum_three.parts(), qkv_state, vec_state)
    else:
        ones, twos, threes = sum_one.full(), sum_two.full(), sum_three.full()
        qkv = [threes[:, (3 * pair + kind) * LANES :][:, :LANES] for kind in range(3) for pair in range(PAIRS)]
        grads = [jnp.concatenate(qkv, axis=1), threes[:, 3 * D : 3 * D + vectors.shape[0]]]
        grads += [twos[:, 4 * QUARTER :], *join_units([ones, twos])]
        grads = [lax.psum_scatter(grad, AXES, scatter_dimension=0, tiled=True) for grad in grads]

        def update(state, grad, rate, decay):
            return adam_update(state[0], grad, state[1], state[2], rate, decay)

        new_qkv = update(qkv_state, grads[0], matrix_rate, weight_decay)
        new_vec = update(vec_state, grads[1].T, vector_rate, 0.0)
        new_out = update(out_state, grads[2], output_rate, weight_decay)
        new_up = update(up_state, grads[3], matrix_rate, weight_decay)
        new_down = update(down_state, grads[4], matrix_rate, weight_decay)
    return (
        result.reshape(tokens.shape),
        final.input_grad.reshape(tokens.shape),
        *new_qkv,
        *new_out,
        *new_up,
        *new_down,
        *new_vec,
    )


def solution(mesh):
    return jax.shard_map(
        local,
        mesh=mesh,
        in_specs=(
            P(("dp", "fsdp"), None, None),
            P(("dp", "fsdp"), None, None),
            P(("dp", "fsdp"), None),
            P(("dp", "fsdp")),
            P(("dp", "fsdp")),
            P(("dp", "fsdp"), None),
            P(("dp", "fsdp"), None),
            P(("dp", "fsdp"), None),
            P(("dp", "fsdp"), None),
            P(None, ("dp", "fsdp")),
            P(("dp", "fsdp"), None),
            P(("dp", "fsdp"), None),
            P(("dp", "fsdp"), None),
            P(("dp", "fsdp"), None),
            P(("dp", "fsdp"), None),
            P(("dp", "fsdp"), None),
            P(("dp", "fsdp"), None),
            P(("dp", "fsdp"), None),
            P(None, ("dp", "fsdp")),
            P(None, ("dp", "fsdp")),
        ),
        out_specs=(
            P(("dp", "fsdp"), None, None),
            P(("dp", "fsdp"), None, None),
            P(("dp", "fsdp"), None),
            P(("dp", "fsdp"), None),
            P(("dp", "fsdp"), None),
            P(("dp", "fsdp"), None),
            P(("dp", "fsdp"), None),
            P(("dp", "fsdp"), None),
            P(("dp", "fsdp"), None),
            P(("dp", "fsdp"), None),
            P(("dp", "fsdp"), None),
            P(("dp", "fsdp"), None),
            P(("dp", "fsdp"), None),
            P(("dp", "fsdp"), None),
            P(None, ("dp", "fsdp")),
            P(None, ("dp", "fsdp")),
            P(None, ("dp", "fsdp")),
        ),
        check_vma=False,
    )
```

```python
import functools

import jax
import jax.numpy as jnp
from jax import lax
from jax.experimental import pallas as pl
from jax.experimental.pallas import tpu as pltpu
from jax.sharding import PartitionSpec as P

D = 512
HEADS = 8
HEAD = 64
FF = 2048
QUARTER = FF // 4
LANES = 128
PAIRS = D // LANES
ROWS = 16
STEP = 10
AXES = ("dp", "fsdp")
SCALE = 1.2
NEAR_PARTS = 3
UNROLL = 2
VMEM_BYTES = 16 * 1024 * 1024

norm_epsilon = 1e-05
beta_first = 0.9
beta_second = 0.999
adam_epsilon = 1e-08
weight_decay = 0.1
matrix_rate = 0.02
output_rate = 0.1
vector_rate = 0.2
masked_score = -1000000000.0
gelu_scale = 0.7978845608028654
gelu_cubic = 0.044715
FIRST_PAD = 224


def low(values):
    return values.astype(jnp.bfloat16)


def wide(values):
    return values.astype(jnp.float32)


def dot(left, right):
    return lax.dot_general(left, right, (((1,), (0,)), ((), ())), preferred_element_type=jnp.float32)


def dot_rows(left, right):
    return lax.dot_general(left, right, (((1,), (1,)), ((), ())), preferred_element_type=jnp.float32)


def dot_columns(left, right):
    return lax.dot_general(left, right, (((0,), (0,)), ((), ())), preferred_element_type=jnp.float32)


def cost(micros):
    return pl.CostEstimate(flops=int(micros * SCALE * 1.15e9), bytes_accessed=0, transcendentals=0)


class Refs:
    pass


def call(body, name, micros, ins, outs, scratch=(), reused=()):
    in_names, out_names = [entry[0] for entry in ins], [entry[0] for entry in outs]
    aliases = {in_names.index(taken): out_names.index(given) for taken, given in reused}
    names = [entry[0] for entry in ins] + [entry[0] for entry in outs] + [entry[0] for entry in scratch]

    def kernel(*refs):
        named = Refs()
        for entry, ref in zip(names, refs):
            setattr(named, entry, ref)
        body(named)

    results = pl.pallas_call(
        kernel,
        out_shape=[jax.ShapeDtypeStruct(shape, kind) for _, shape, kind in outs],
        in_specs=[entry[2] if len(entry) > 2 else whole() for entry in ins],
        out_specs=[whole() for _ in outs],
        scratch_shapes=[pltpu.VMEM(shape, kind) for _, shape, kind in scratch],
        compiler_params=pltpu.CompilerParams(vmem_limit_bytes=VMEM_BYTES),
        cost_estimate=cost(micros),
        input_output_aliases=aliases,
        name=name,
    )(*[entry[1] for entry in ins])
    out = Refs()
    for entry, value in zip(outs, results):
        setattr(out, entry[0], value)
    return out


def whole():
    return pl.BlockSpec(memory_space=pltpu.VMEM)


def scalars():
    return pl.BlockSpec(memory_space=pltpu.SMEM)


FAR = (0, 8, 16, 24)


def block_device(me, core, place):
    first = jnp.where(core == 0, 4, 2)
    near = (0, first, 6 - first, 6)[place // len(FAR)]
    return me ^ near ^ FAR[place % len(FAR)]


def assemble(me, stacks, targets):
    for stream in range(2):
        for upper in range(2):
            stack = stacks[2 * stream + upper]
            for place in range(8):
                device = block_device(me ^ stream, (me & 1) ^ stream, place + upper * 8)
                rows = pl.ds(pl.multiple_of(device * ROWS, ROWS), ROWS)
                for ref, column in targets:
                    ref[rows, :] = stack[pl.ds(place * ROWS, ROWS), pl.ds(column, ref.shape[1])]


def arrange(me, sources, keep_ref, send_ref):
    for place in range(16):
        here = pl.ds(place * ROWS, ROWS)
        for stream, out in ((0, keep_ref), (1, send_ref)):
            device = block_device(me ^ stream, (me & 1) ^ stream, place)
            rows = pl.ds(pl.multiple_of(device * ROWS, ROWS), ROWS)
            at = 0
            for ref in sources:
                out[here, pl.ds(at, ref.shape[1])] = ref[rows, :].astype(out.dtype)
                at += ref.shape[1]


def arranged(columns):
    shape = (16 * ROWS, columns)
    return [("keep", shape, jnp.float32), ("send", shape, jnp.bfloat16)]


def centre(values):
    centred = values - jnp.mean(values, axis=-1, keepdims=True)
    scale = lax.rsqrt(jnp.mean(centred * centred, axis=-1, keepdims=True) + norm_epsilon)
    return centred * scale, scale


def norm_back(grad, gain, hat, scale):
    inner = grad * gain
    return scale * (
        inner - jnp.mean(inner, axis=-1, keepdims=True) - hat * jnp.mean(inner * hat, axis=-1, keepdims=True)
    )


def masked_rows(order_row, step):
    seq = order_row.shape[1]
    flags = jnp.where(order_row >= step, 1.0, 0.0)
    column = jnp.transpose(jnp.broadcast_to(flags, (LANES, seq)))
    return jnp.concatenate([column] * (D // LANES), axis=1) > 0.5


def pair_split(pair, scale=None):
    lane = lax.broadcasted_iota(jnp.int32, pair.shape, 1)
    values = wide(pair)
    if scale is not None:
        values = values * scale
    return jnp.concatenate([low(jnp.where(lane < HEAD, values, 0.0)), low(jnp.where(lane < HEAD, 0.0, values))], axis=0)


def key_scores(keys, both_queries, length):
    scores = dot_rows(keys, both_queries)
    seq = scores.shape[0]
    tail = scores[FIRST_PAD:]
    row = lax.broadcasted_iota(jnp.int32, tail.shape, 0) + FIRST_PAD
    return jnp.concatenate([scores[:FIRST_PAD], jnp.where(row < length, tail, masked_score)], axis=0)


def load_input(r, span, rows):
    masked = masked_rows(r.order[span], r.step[span])
    return masked, jnp.where(masked, r.vec[4:5, :], wide(r.tokens[rows, :]))


def each_span(seq, spans, body):
    def step(index, carry):
        span = spans[0] + index
        body(span, pl.ds(pl.multiple_of(span * seq, seq), seq))
        return carry

    lax.fori_loop(0, len(spans), step, 0, unroll=UNROLL)


def attention(scalar, order, tokens, first, spans, front=None):
    count, _, seq = order.shape
    fresh = front is None

    def body(r):
        if fresh:
            stacks = (r.stack0, r.stack1, r.stack2, r.stack3)
            assemble(r.me[0], stacks, ((r.weight, 0), (r.columns, 3 * D)))
            r.vec[...] = jnp.transpose(wide(r.columns[...]))[:8]
        else:
            for name in ("normed", "p", "attended"):
                old = getattr(r, "front_" + name)
                getattr(r, name)[pl.ds(0, old.shape[0]), :] = old[...]
            r.logs[: spans[0]] = r.front_logs[...]

        def one_span(span, rows):
            started = load_input(r, span, rows)[1]
            normed = low(centre(started)[0] * r.vec[0:1, :] + r.vec[2:3, :])
            r.normed[rows, :] = normed
            r.p[rows, :] = low(dot(normed, r.weight[...]))
            for pair in range(PAIRS):
                lanes = pl.ds(pair * LANES, LANES)
                queries = pair_split(r.p[rows, lanes], HEAD**-0.5)
                scores = key_scores(r.p[rows, pl.ds(D + pair * LANES, LANES)], queries, r.length[span])
                peak = jnp.max(scores, axis=0, keepdims=True)
                exped = jnp.exp(scores - peak)
                total = jnp.sum(exped, axis=0, keepdims=True)
                probability = low(exped / total)
                r.logs[span, pair : pair + 1, :] = peak + jnp.log(total)
                values = jnp.transpose(r.p[rows, pl.ds(2 * D + pair * LANES, LANES)])
                attended = jnp.concatenate(
                    [dot(values[:HEAD], probability[:, :seq]), dot(values[HEAD:], probability[:, seq:])], axis=0
                )
                r.attended[rows, lanes] = jnp.transpose(low(attended))

        each_span(seq, spans, one_span)

    ins = [(name, array, scalars()) for name, array in scalar.items()] + [("order", order), ("tokens", tokens)]
    count = spans[-1] + 1
    rows = count * seq
    outs = [
        ("normed", (rows, D), jnp.bfloat16),
        ("p", (rows, 3 * D), jnp.bfloat16),
        ("attended", (rows, D), jnp.bfloat16),
        ("logs", (count, PAIRS, 2 * seq), jnp.float32),
    ]
    scratch = []
    if fresh:
        ins += [("stack%d" % n, stack) for n, stack in enumerate(first)]
        outs += [("weight", (D, 3 * D), jnp.bfloat16), ("vec", (8, D), jnp.float32)]
        scratch = [("columns", (D, LANES), jnp.bfloat16)]
    else:
        ins += [("weight", front.weight), ("vec", front.vec)]
        ins += [("front_" + name, getattr(front, name)) for name in ("normed", "p", "attended", "logs")]
    return call(body, "attention", 3 * len(spans), ins, outs, scratch)


def hidden_quarter(normed, upstream, up, down):
    hidden = dot(normed, up)
    grad_act = dot_rows(upstream, down)
    squared = hidden * hidden
    tilt = jnp.tanh(hidden * (gelu_scale + (gelu_scale * gelu_cubic) * squared))
    gate = 0.5 + 0.5 * tilt
    active = hidden * gate
    slope = gate + active * (1.0 - tilt) * (gelu_scale + (3.0 * gelu_scale * gelu_cubic) * squared)
    grad_hidden = low(grad_act * slope)
    return low(active), grad_hidden, dot_rows(grad_hidden, up)


def quarter_call(quarter, scalar, cotangent, stacks, ins, outs, seq, before, after, micros, reused=(), mate=None):
    total = cotangent.shape[0]
    column = 2 * QUARTER * (quarter % 2)

    def body(r):
        stacks = (r.stack0, r.stack1, r.stack2, r.stack3)
        targets = [(r.up, column), (r.down_full, column + QUARTER)]
        if quarter == 0:
            targets.append((r.out_full, 4 * QUARTER))
        assemble(r.me[0], stacks, targets)

        def one_span(span, rows):
            normed = before(r, span, rows)
            active, grad_hidden, back = hidden_quarter(normed, r.cot[rows, :], r.up[...], r.down_full[...])
            r.active[rows, :] = active
            r.grad_hidden[rows, :] = grad_hidden
            after(r, rows, back)

        each_span(seq, range(total // seq), one_span)
        r.grad_up[...] = dot_columns(r.middle_normed[...], r.grad_hidden[...])
        r.grad_down[...] = dot_columns(r.active[...], r.cot[...])
        if mate is not None:
            arrange(r.me[0], (r.mate_up, r.mate_down, r.grad_up, r.grad_down), r.keep, r.send)

    ins = [("me", scalar["me"], scalars()), ("cot", cotangent)] + ins
    ins += [("stack%d" % n, stack) for n, stack in enumerate(stacks)]
    outs = outs + [("active", (total, QUARTER), jnp.bfloat16), ("down_full", (QUARTER, D), jnp.bfloat16)]
    grads = [("grad_up", (D, QUARTER), jnp.float32), ("grad_down", (QUARTER, D), jnp.float32)]
    scratch = [("up", (D, QUARTER), jnp.bfloat16), ("grad_hidden", (total, QUARTER), jnp.bfloat16)]
    if mate is None:
        outs = outs + grads
    else:
        ins += [("mate_up", mate.grad_up), ("mate_down", mate.grad_down)]
        outs = outs + arranged(4 * QUARTER)
        scratch = scratch + grads
    return call(body, "hidden%d" % quarter, micros, ins, outs, scratch, reused)


def first_quarter(scalar, order, tokens, cotangent, vec, attended, stacks):
    seq = order.shape[2]
    total = tokens.shape[0]

    def enter(r, span, rows):
        middle = load_input(r, span, rows)[1] + dot(r.attended[rows, :], r.out_full[...])
        r.middle[rows, :] = middle
        normed = low(centre(middle)[0] * r.vec[1:2, :] + r.vec[3:4, :])
        r.middle_normed[rows, :] = normed
        return normed

    def leave(r, rows, back):
        r.back[rows, :] = back

    ins = [("step", scalar["step"], scalars()), ("order", order), ("tokens", tokens), ("vec", vec), ("attended", attended)]
    outs = [("middle", (total, D), jnp.float32), ("middle_normed", (total, D), jnp.bfloat16)]
    outs += [("back", (total, D), jnp.float32), ("out_full", (D, D), jnp.bfloat16)]
    return quarter_call(0, scalar, cotangent, stacks, ins, outs, seq, enter, leave, 8.5)


def next_quarter(quarter, scalar, cotangent, stacks, normed, back, seq, mate=None):
    total = normed.shape[0]

    def take(r, span, rows):
        return r.middle_normed[rows, :]

    def leave(r, rows, back):
        r.back[rows, :] = r.old_back[rows, :] + back

    ins = [("middle_normed", normed), ("old_back", back)]
    outs = [("back", (total, D), jnp.float32)]
    reused = [("old_back", "back")]
    return quarter_call(quarter, scalar, cotangent, stacks, ins, outs, seq, take, leave, 6.5, reused, mate)


def middle_back(scalar, cotangent, vec, attended, middle, back, out_full, seq, quarters):
    total = middle.shape[0]

    def body(r):
        r.dvec[...] = jnp.zeros_like(r.dvec)

        def one_span(span, rows):
            back = r.back[rows, :]
            hat, scale = centre(r.middle[rows, :])
            dmiddle = wide(r.cot[rows, :]) + norm_back(back, r.vec[1:2, :], hat, scale)
            r.dmiddle[rows, :] = dmiddle
            r.dvec[1:2, :] += jnp.sum(back * hat, axis=0, keepdims=True)
            r.dvec[3:4, :] += jnp.sum(back, axis=0, keepdims=True)
            mixed = low(dmiddle)
            r.mixed[rows, :] = mixed
            r.dattended[rows, :] = low(dot_rows(mixed, r.out_full[...]))

        each_span(seq, range(total // seq), one_span)
        r.grad_out[...] = dot_columns(r.attended[...], r.mixed[...])
        arrange(r.me[0], (r.up0, r.down0, r.up1, r.down1, r.grad_out), r.keep, r.send)

    ins = [("me", scalar["me"], scalars()), ("cot", cotangent), ("vec", vec), ("attended", attended)]
    ins += [("middle", middle), ("back", back), ("out_full", out_full)]
    for n, quarter in enumerate(quarters):
        ins += [("up%d" % n, quarter.grad_up), ("down%d" % n, quarter.grad_down)]
    outs = [("dmiddle", (total, D), jnp.float32), ("dattended", (total, D), jnp.bfloat16), ("dvec", (8, D), jnp.float32)]
    outs += arranged(4 * QUARTER + D)
    scratch = [("grad_out", (D, D), jnp.float32), ("mixed", (total, D), jnp.bfloat16)]
    return call(body, "middle_back", 4, ins, outs, scratch)


def branch_output(middle, quarters, seq, spans, front=None):
    def body(r):
        if front is not None:
            r.result[pl.ds(0, front.shape[0]), :] = r.front[...]

        def one_span(span, rows):
            result = r.middle[rows, :]
            for n in range(4):
                result = result + dot(getattr(r, "active%d" % n)[rows, :], getattr(r, "down%d" % n)[...])
            r.result[rows, :] = low(result)

        each_span(seq, spans, one_span)

    ins = [("middle", middle)]
    for n, quarter in enumerate(quarters):
        ins += [("active%d" % n, quarter.active), ("down%d" % n, quarter.down_full)]
    if front is not None:
        ins += [("front", front)]
    return call(body, "branch_output", 25, ins, [("result", ((spans[-1] + 1) * seq, D), jnp.bfloat16)]).result


def attention_back(scalar, pair, normed, p, logs, dattended, seq, mate=None):
    total = normed.shape[0]
    last = pair == PAIRS - 1

    def body(r):
        def one_span(span, rows):
            queries = pair_split(r.p[rows, pl.ds(pair * LANES, LANES)], HEAD**-0.5)
            dattended = pair_split(r.dattended[rows, pl.ds(pair * LANES, LANES)])
            keys = r.p[rows, pl.ds(D + pair * LANES, LANES)]
            scores = key_scores(keys, queries, r.length[span])
            probability = jnp.exp(scores - r.logs[span, pair : pair + 1, :])
            dprobability = dot_rows(r.p[rows, pl.ds(2 * D + pair * LANES, LANES)], dattended)
            inner = jnp.sum(probability * dprobability, axis=0, keepdims=True)
            dscores = low(probability * (dprobability - inner))
            dvalues = low(dot(low(probability), dattended))
            dkeys = low(dot(dscores, queries))
            keys = jnp.transpose(low(wide(keys) * HEAD**-0.5))
            dqueries = jnp.concatenate([dot(keys[:HEAD], dscores[:, :seq]), dot(keys[HEAD:], dscores[:, seq:])], axis=0)
            r.dp[rows, :] = jnp.concatenate([jnp.transpose(low(dqueries)), dkeys, dvalues], axis=1)

        each_span(seq, range(total // seq), one_span)
        if not last:
            r.grad[...] = dot_columns(r.normed[...], r.dp[...])
        if mate is not None:
            arrange(r.me[0], (r.mate, r.grad), r.keep, r.send)

    ins = [("me", scalar["me"], scalars()), ("length", scalar["length"], scalars())]
    ins += [("normed", normed), ("p", p), ("logs", logs), ("dattended", dattended)]
    outs = [("dp", (total, 3 * LANES), jnp.bfloat16)]
    grad = ("grad", (D, 3 * LANES), jnp.float32)
    scratch = []
    if mate is not None:
        ins += [("mate", mate.grad)]
        outs += arranged(6 * LANES)
        scratch = [grad]
    elif not last:
        outs += [grad]
    return call(body, "attention_back", 4.6, ins, outs, scratch)


def input_back(scalar, order, tokens, vec, normed, dmiddle, weight, dvec, parts):
    seq = order.shape[2]
    total = tokens.shape[0]

    def body(r):
        parts = [getattr(r, "dp%d" % n) for n in range(PAIRS)]
        r.dvec[...] = jnp.zeros_like(r.dvec)
        r.dvec[:8, :] = r.dvec_in[...]

        def one_span(span, rows):
            dp = [part[rows, pl.ds(kind * LANES, LANES)] for kind in range(3) for part in parts]
            back = dot_rows(jnp.concatenate(dp, axis=1), r.weight[...])
            masked, started = load_input(r, span, rows)
            hat, scale = centre(started)
            dstarted = r.dmiddle[rows, :] + norm_back(back, r.vec[0:1, :], hat, scale)
            r.input_grad[rows, :] = jnp.where(masked, 0.0, dstarted)
            r.dvec[0:1, :] += jnp.sum(back * hat, axis=0, keepdims=True)
            r.dvec[2:3, :] += jnp.sum(back, axis=0, keepdims=True)
            r.dvec[4:5, :] += jnp.sum(jnp.where(masked, dstarted, 0.0), axis=0, keepdims=True)

        each_span(seq, range(total // seq), one_span)
        r.columns[...] = jnp.transpose(r.dvec[...])
        r.grad[...] = dot_columns(r.normed[...], parts[-1][...])
        arrange(r.me[0], (r.mate, r.grad, r.columns), r.keep, r.send)

    ins = [("me", scalar["me"], scalars()), ("step", scalar["step"], scalars()), ("order", order), ("tokens", tokens)]
    ins += [("vec", vec), ("dmiddle", dmiddle), ("normed", normed), ("weight", weight), ("dvec_in", dvec)]
    ins += [("dp%d" % n, part.dp) for n, part in enumerate(parts)]
    ins += [("mate", parts[-2].grad)]
    outs = [("input_grad", (total, D), jnp.float32)] + arranged(7 * LANES)
    scratch = [
        ("dvec", (LANES, D), jnp.float32),
        ("columns", (D, LANES), jnp.float32),
        ("grad", (D, 3 * LANES), jnp.float32),
    ]
    return call(body, "input_back", 6.5, ins, outs, scratch)


def fold_kernel(keep_ref, taken_ref, total_ref, send_ref):
    half = total_ref.shape[0]
    total_ref[...] = keep_ref[:half, :] + wide(taken_ref[:half, :])
    send_ref[...] = low(keep_ref[half:, :] + wide(taken_ref[half:, :]))


def fold(keep, taken):
    rows, columns = keep.shape
    return pl.pallas_call(
        fold_kernel,
        out_shape=(
            jax.ShapeDtypeStruct((rows // 2, columns), jnp.float32),
            jax.ShapeDtypeStruct((rows // 2, columns), jnp.bfloat16),
        ),
        in_specs=[whole()] * 2,
        out_specs=(whole(), whole()),
        compiler_params=pltpu.CompilerParams(vmem_limit_bytes=VMEM_BYTES),
        cost_estimate=cost(1),
        name="fold",
    )(keep, taken)


def adam_update(master, gradient, moment, square, step_rate, decay_rate):
    moment_new = beta_first * moment + (1.0 - beta_first) * gradient
    square_new = beta_second * square + (1.0 - beta_second) * gradient * gradient
    corrected = (
        moment_new
        / (1.0 - beta_first**STEP)
        / (jnp.sqrt(square_new / (1.0 - beta_second**STEP)) + adam_epsilon)
    )
    return (moment_new, square_new, master - step_rate * (corrected + decay_rate * master))


def unit_order():
    unit = lax.broadcasted_iota(jnp.int32, (D, D), 0)
    place = lax.broadcasted_iota(jnp.int32, (D, D), 1)
    wanted = (place % LANES // ROWS) * 64 + (place // LANES) * ROWS + place % ROWS
    return jnp.where(unit == wanted, 1.0, 0.0).astype(jnp.bfloat16)


def hidden_update_kernel(*refs):
    halves = (refs[0:4], refs[4:8])
    up, down, out = refs[8:11], refs[11:14], refs[14:17]
    new_up, new_down, new_out = refs[17:20], refs[20:23], refs[23:26]

    def summed(half, columns):
        return half[0][:ROWS, columns] + sum(wide(part[:, columns]) for part in half[1:])

    def update(new, old, index, grad, rate):
        results = adam_update(old[0][index], grad, old[1][index], old[2][index], rate, weight_decay)
        for ref, value in zip(new, results):
            ref[index] = value

    sort = unit_order()
    for group in range(FF // D):
        grads = []
        for quarter in range(4):
            columns = pl.ds((quarter % 2) * 2 * QUARTER + group * LANES, LANES)
            grads.append(summed(halves[quarter // 2], columns))
        rest = jnp.concatenate(grads, axis=1)
        grad = 0.0
        for _ in range(3):
            piece = low(rest)
            grad = grad + dot_rows(piece, sort)
            rest = rest - wide(piece)
        update(new_up, up, (slice(None), pl.ds(group * D, D)), grad, matrix_rate)
    for quarter in range(4):
        grad = summed(halves[quarter // 2], pl.ds((quarter % 2) * 2 * QUARTER + QUARTER, D))
        update(new_down, down, (pl.ds(quarter * ROWS, ROWS), slice(None)), grad, matrix_rate)
    update(new_out, out, Ellipsis, summed(halves[1], pl.ds(4 * QUARTER, D)), output_rate)


def hidden_update(total_one, parts_one, total_two, parts_two, up, down, out):
    outs = [jax.ShapeDtypeStruct(state[0].shape, jnp.float32) for state in (up, down, out) for _ in range(3)]
    results = pl.pallas_call(
        hidden_update_kernel,
        out_shape=outs,
        in_specs=[whole()] * 17,
        out_specs=[whole()] * 9,
        compiler_params=pltpu.CompilerParams(vmem_limit_bytes=VMEM_BYTES),
        cost_estimate=cost(3),
        name="hidden_update",
    )(total_one, *parts_one, total_two, *parts_two, *up, *down, *out)
    return results[:3], results[3:6], results[6:]


def last_update_kernel(*refs):
    early, late = refs[:4], refs[4:8]
    qkv, vec = refs[8:11], refs[11:14]
    new_qkv, new_vec = refs[14:17], refs[17:20]

    def summed(group, column):
        columns = pl.ds(column, LANES)
        return group[0][:ROWS, columns] + sum(wide(part[:, columns]) for part in group[1:])

    for pair in range(PAIRS):
        for kind in range(3):
            group, first = (early, 4 * QUARTER + D) if pair < 2 else (late, 0)
            grad = summed(group, first + (3 * (pair % 2) + kind) * LANES)
            here = pl.ds((kind * PAIRS + pair) * LANES, LANES)
            moment, square, master = adam_update(
                qkv[0][:, here], grad, qkv[1][:, here], qkv[2][:, here], matrix_rate, weight_decay
            )
            new_qkv[0][:, here], new_qkv[1][:, here], new_qkv[2][:, here] = moment, square, master
    grad = summed(late, 6 * LANES)
    grad = jnp.transpose(jnp.concatenate([grad, jnp.zeros((LANES - ROWS, LANES), jnp.float32)], axis=0))
    grad = grad[: vec[0].shape[0], :ROWS]
    results = adam_update(vec[0][...], grad, vec[1][...], vec[2][...], vector_rate, 0.0)
    for ref, value in zip(new_vec, results):
        ref[...] = value


def last_update(total_early, parts_early, total_late, parts_late, qkv, vec):
    outs = [jax.ShapeDtypeStruct(qkv[0].shape, jnp.float32)] * 3 + [jax.ShapeDtypeStruct(vec[0].shape, jnp.float32)] * 3
    results = pl.pallas_call(
        last_update_kernel,
        out_shape=outs,
        in_specs=[whole()] * 14,
        out_specs=[whole()] * 6,
        compiler_params=pltpu.CompilerParams(vmem_limit_bytes=VMEM_BYTES),
        cost_estimate=cost(1),
        name="last_update",
    )(total_early, *parts_early, total_late, *parts_late, *qkv, *vec)
    return results[:3], results[3:]


def exchange(values, count, even_mask, odd_mask):
    pairs = [(i, i ^ (odd_mask if i % 2 else even_mask)) for i in range(count)]
    return lax.ppermute(values, AXES, pairs)


def tie(value, *others):
    return lax.optimization_barrier((value, others))[0]


class Gather:
    def __init__(self, piece, count):
        self.piece, self.count, self.direct = piece, count, piece.shape[0] == ROWS
        self.parts, self.other = [], None

    def far(self):
        if self.direct:
            self.parts = [exchange(self.piece, self.count, offset, offset) for offset in FAR[1:]]
        return self.parts

    def split(self, columns):
        pair = [Gather(self.piece[:, :columns], self.count), Gather(self.piece[:, columns:], self.count)]
        parts = self.far()
        pair[0].parts = [part[:, :columns] for part in parts]
        pair[1].parts = [part[:, columns:] for part in parts]
        return pair

    def stack(self, *waits):
        if self.direct:
            self.piece = jnp.concatenate([self.piece] + [tie(part, *waits) for part in self.parts], axis=0)
        return self.piece

    def core(self, *waits):
        if not self.direct:
            return self.piece
        start = self.other.shape[0] if self.other is not None else 0
        taken = tie(exchange(self.piece[start:], self.count, 1, 1), *waits)
        self.other = taken if self.other is None else jnp.concatenate([self.other, taken], axis=0)
        return taken

    def near(self, *waits):
        if self.direct:
            taken = exchange(self.piece, self.count, 4, 2)
            self.piece = jnp.concatenate([self.piece, tie(taken, *waits)], axis=0)
        return self.piece

    def late(self, *waits):
        if self.direct:
            self.rest = tie(exchange(self.piece, self.count, 2, 4), *waits)

    def finish(self, *waits):
        if not self.direct:
            return ordered_stacks(self.piece)
        return (self.piece, self.rest, self.other, tie(exchange(self.rest, self.count, 1, 1), *waits))


class Scatter:
    def __init__(self, arranged, count, direct):
        self.total, self.send, self.count, self.direct = arranged.keep, arranged.send, count, direct

    def step(self, even, odd, *waits):
        if self.direct:
            self.total, self.send = fold(self.total, tie(exchange(self.send, self.count, even, odd), *waits))
        return self.total, self.send

    def core(self, *waits):
        return self.step(1, 1, *waits)

    def near(self, *waits):
        return self.step(2, 4, *waits)

    def next(self, *waits):
        if self.direct:
            self.total = self.total + wide(tie(exchange(self.send, self.count, 4, 2), *waits))
        return self.total

    def join(self, other):
        self.total = jnp.concatenate([self.total, other.total], axis=1)
        self.send = jnp.concatenate([self.send, other.send], axis=1)

    def parts(self, *waits):
        if not self.direct:
            return []
        taken = []
        for place in range(1, len(FAR)):
            part = low(self.total[place * ROWS : (place + 1) * ROWS])
            taken.append(tie(exchange(part, self.count, FAR[place], FAR[place]), *waits))
        return taken

    def full(self):
        return full_piece(self.total, self.send)


def split_units(up, down):
    rows, units = up.shape
    up = up.reshape(rows, units // 64, 4, ROWS)
    down = down.reshape(rows // ROWS, 4, ROWS, D)
    ups = [up[:, :, quarter].reshape(rows, units // 4) for quarter in range(4)]
    downs = [down[:, quarter].reshape(rows, D) for quarter in range(4)]
    return [jnp.concatenate([ups[n], downs[n], ups[n + 1], downs[n + 1]], axis=1) for n in (0, 2)]


def pack_kernel(*refs):
    sources, first, hidden, buffers, done = refs[:5], refs[5], refs[6], refs[7:12], refs[12]
    copies = [pltpu.make_async_copy(sources[n], buffers[n], done.at[n]) for n in range(5)]
    for copy in copies:
        copy.start()
    qkv, vec, out, up, down = buffers
    copies[0].wait()
    first[:, pl.ds(0, 3 * D)] = low(qkv[...])
    copies[1].wait()
    rows, columns = vec.shape
    turned = jnp.concatenate([vec[...], jnp.zeros((rows, LANES - columns), jnp.float32)], axis=1)
    turned = jnp.transpose(jnp.concatenate([turned, jnp.zeros((LANES - rows, LANES), jnp.float32)], axis=0))
    first[:, pl.ds(3 * D, LANES)] = low(turned[:ROWS])
    for copy in copies[2:]:
        copy.wait()
    sort = unit_order()
    for group in range(FF // D):
        mixed = low(dot(low(up[:, pl.ds(group * D, D)]), sort))
        for quarter in range(4):
            column = 2 * QUARTER * ((quarter + 2) % 4) + group * LANES
            hidden[:, pl.ds(column, LANES)] = mixed[:, quarter * LANES : (quarter + 1) * LANES]
    for quarter in range(4):
        rows = down[pl.ds(quarter * ROWS, ROWS), :]
        hidden[:, pl.ds(2 * QUARTER * ((quarter + 2) % 4) + QUARTER, D)] = low(rows)
    hidden[:, pl.ds(8 * QUARTER, D)] = low(out[...])


def pack(*sources):
    return pl.pallas_call(
        pack_kernel,
        out_shape=(
            jax.ShapeDtypeStruct((ROWS, 3 * D + LANES), jnp.bfloat16),
            jax.ShapeDtypeStruct((ROWS, 8 * QUARTER + D), jnp.bfloat16),
        ),
        in_specs=[pl.BlockSpec(memory_space=pl.ANY)] * 5,
        out_specs=(whole(), whole()),
        scratch_shapes=[pltpu.VMEM(source.shape, source.dtype) for source in sources] + [pltpu.SemaphoreType.DMA((5,))],
        compiler_params=pltpu.CompilerParams(vmem_limit_bytes=VMEM_BYTES),
        cost_estimate=cost(1),
        name="pack",
    )(*[pltpu.with_memory_space_constraint(source, pltpu.HBM) for source in sources])


def join_units(pieces):
    rows = pieces[0].shape[0]
    groups = [[piece[:, n * QUARTER : (n + 1) * QUARTER] for n in range(4)] for piece in pieces]
    ups = [groups[0][0], groups[0][2], groups[1][0], groups[1][2]]
    downs = [groups[0][1], groups[0][3], groups[1][1], groups[1][3]]
    up = jnp.stack([group.reshape(rows, QUARTER // ROWS, ROWS) for group in ups], axis=2)
    down = jnp.stack([group.reshape(rows // ROWS, ROWS, D) for group in downs], axis=1)
    return up.reshape(rows, 4 * QUARTER), down.reshape(rows * 4, D)


def stack_order(core):
    near = (0, 4, 2, 6) if core == 0 else (0, 2, 4, 6)
    return [core ^ group ^ offset for group in near for offset in FAR]


def ordered_stacks(piece):
    blocks = piece.reshape(32, ROWS, piece.shape[1])
    stacks = []
    for core in range(2):
        ordered = jnp.stack([blocks[device] for device in stack_order(core)])
        ordered = ordered.reshape(16 * ROWS, piece.shape[1])
        stacks += [ordered[: 8 * ROWS], ordered[8 * ROWS :]]
    return tuple(stacks)


def full_piece(keep, send):
    columns = keep.shape[1]
    blocks = jnp.concatenate([keep, wide(send)], axis=0).reshape(32, ROWS, columns)
    order = stack_order(0) + stack_order(1)
    return jnp.stack([blocks[order.index(device)] for device in range(32)]).reshape(32 * ROWS, columns)


def local(
    tokens,
    cotangent,
    reveal_order,
    reveal_step,
    lengths,
    weight_qkv,
    weight_out,
    weight_up,
    weight_down,
    vectors,
    moment_qkv,
    square_qkv,
    moment_out,
    square_out,
    moment_up,
    square_up,
    moment_down,
    square_down,
    moment_vec,
    square_vec,
):
    count = lax.axis_size("dp") * lax.axis_size("fsdp")
    direct = weight_qkv.shape[0] == ROWS and count == 32
    me = lax.axis_index("dp") * lax.axis_size("fsdp") + lax.axis_index("fsdp")
    me = (me if direct else 0 * me).astype(jnp.int32)[None]
    spans, seq = reveal_order.shape
    order = reveal_order.reshape(spans, 1, seq)
    flat = tokens.reshape(spans * seq, D)
    upstream = cotangent.reshape(spans * seq, D)

    if direct:
        piece_one, piece_rest = pack(weight_qkv, vectors, weight_out, weight_up, weight_down)
    else:
        columns = jnp.pad(low(vectors).T, ((0, 0), (0, LANES - vectors.shape[0])))
        halves = [jnp.concatenate([low(weight_qkv), columns], axis=1), low(weight_out), low(weight_up), low(weight_down)]
        piece_one, out, up, down = [lax.all_gather(half, AXES, axis=0, tiled=True) for half in halves]
        hidden = split_units(up, down)
        piece_rest = jnp.concatenate([hidden[1], hidden[0], out], axis=1)
    scalar = {"me": me, "step": reveal_step, "length": lengths}

    one = Gather(piece_one, count)
    one.far()
    one.stack()
    rest = Gather(tie(piece_rest, one.core()), count)
    three, two = rest.split(4 * QUARTER)
    one.near()
    one.late()
    one.core()
    first = one.finish()
    two.stack(*([one.rest] if direct else []))
    front = attention(scalar, order, flat, first, range(0, spans // 2))
    two.near(front.logs)
    two.late()
    two.core()
    three.stack(front.logs)
    rear = attention(scalar, order, tie(flat, two.piece), None, range(spans // 2, spans), front)
    vec, weight = front.vec, front.weight
    two.rest = tie(two.rest, rear.logs) if direct else None
    second = two.finish()
    three.near(rear.logs)
    h = [first_quarter(scalar, order, flat, tie(upstream, three.piece), vec, rear.attended, second)]
    normed = h[0].middle_normed
    three.late(h[0].back)
    three.core(h[0].back)
    h += [next_quarter(1, scalar, upstream, second, normed, h[0].back, seq, h[0])]
    third = three.finish(h[1].back)
    h += [next_quarter(2, scalar, upstream, third, normed, h[1].back, seq)]
    sum_one = Scatter(h[1], count, direct)
    h += [next_quarter(3, scalar, tie(upstream, *sum_one.core(h[2].back)), third, normed, h[2].back, seq)]
    turn = middle_back(
        scalar, tie(upstream, h[3].back), vec, rear.attended, h[0].middle, h[3].back, h[0].out_full, seq, h[2:]
    )
    sum_one.near(turn.dattended)
    sum_two = Scatter(turn, count, direct)

    def part(pair, *waits, mate=None):
        dattended = tie(turn.dattended, *waits)
        return attention_back(scalar, pair, rear.normed, rear.p, rear.logs, dattended, seq, mate)

    parts = [part(0, sum_one.total)]
    parts += [part(1, sum_one.next(parts[0].dp), *sum_two.core(parts[0].dp), mate=parts[0])]
    early = Scatter(parts[1], count, direct)
    parts += [part(2, sum_one.total)]
    parts_one = sum_one.parts(parts[2].dp)
    early.core(parts[2].dp)
    sum_two.near(parts[2].dp)
    parts += [part(3, sum_two.total, early.total, *parts_one)]
    early.near(parts[3].dp)
    if direct:
        sum_two.join(early)
    ready = tie(flat, parts[3].dp, sum_two.total)
    final = input_back(scalar, order, ready, vec, rear.normed, turn.dmiddle, weight, turn.dvec, parts)
    late = Scatter(final, count, direct)
    sum_two.next(final.input_grad)
    result = branch_output(tie(h[0].middle, sum_two.total), h, seq, range(0, spans // 2))
    late.core(result)
    result = branch_output(tie(h[0].middle, late.total), h, seq, range(spans // 2, spans), result)
    parts_two = sum_two.parts() if direct else []
    late.near(result, *parts_two[:NEAR_PARTS])
    qkv_state = (weight_qkv, moment_qkv, square_qkv)
    vec_state = (vectors, moment_vec, square_vec)
    out_state = (weight_out, moment_out, square_out)
    up_state = (weight_up, moment_up, square_up)
    down_state = (weight_down, moment_down, square_down)
    if direct:
        late.next(*parts_two)
        parts_late = late.parts()
        total_one = tie(sum_one.total, late.total)
        states = hidden_update(total_one, parts_one, sum_two.total, parts_two, up_state, down_state, out_state)
        new_up, new_down, new_out = states
        new_qkv, new_vec = last_update(sum_two.total, parts_two, late.total, parts_late, qkv_state, vec_state)
    else:
        ones, twos = sum_one.full(), sum_two.full()
        threes = jnp.concatenate([early.full(), late.full()], axis=1)
        qkv = [threes[:, (3 * pair + kind) * LANES :][:, :LANES] for kind in range(3) for pair in range(PAIRS)]
        grads = [jnp.concatenate(qkv, axis=1), threes[:, 3 * D : 3 * D + vectors.shape[0]]]
        grads += [twos[:, 4 * QUARTER :], *join_units([ones, twos])]
        grads = [lax.psum_scatter(grad, AXES, scatter_dimension=0, tiled=True) for grad in grads]

        def update(state, grad, rate, decay):
            return adam_update(state[0], grad, state[1], state[2], rate, decay)

        new_qkv = update(qkv_state, grads[0], matrix_rate, weight_decay)
        new_vec = update(vec_state, grads[1].T, vector_rate, 0.0)
        new_out = update(out_state, grads[2], output_rate, weight_decay)
        new_up = update(up_state, grads[3], matrix_rate, weight_decay)
        new_down = update(down_state, grads[4], matrix_rate, weight_decay)
    return (
        result.reshape(tokens.shape),
        final.input_grad.reshape(tokens.shape),
        *new_qkv,
        *new_out,
        *new_up,
        *new_down,
        *new_vec,
    )


def solution(mesh):
    return jax.shard_map(
        local,
        mesh=mesh,
        in_specs=(
            P(("dp", "fsdp"), None, None),
            P(("dp", "fsdp"), None, None),
            P(("dp", "fsdp"), None),
            P(("dp", "fsdp")),
            P(("dp", "fsdp")),
            P(("dp", "fsdp"), None),
            P(("dp", "fsdp"), None),
            P(("dp", "fsdp"), None),
            P(("dp", "fsdp"), None),
            P(None, ("dp", "fsdp")),
            P(("dp", "fsdp"), None),
            P(("dp", "fsdp"), None),
            P(("dp", "fsdp"), None),
            P(("dp", "fsdp"), None),
            P(("dp", "fsdp"), None),
            P(("dp", "fsdp"), None),
            P(("dp", "fsdp"), None),
            P(("dp", "fsdp"), None),
            P(None, ("dp", "fsdp")),
            P(None, ("dp", "fsdp")),
        ),
        out_specs=(
            P(("dp", "fsdp"), None, None),
            P(("dp", "fsdp"), None, None),
            P(("dp", "fsdp"), None),
            P(("dp", "fsdp"), None),
            P(("dp", "fsdp"), None),
            P(("dp", "fsdp"), None),
            P(("dp", "fsdp"), None),
            P(("dp", "fsdp"), None),
            P(("dp", "fsdp"), None),
            P(("dp", "fsdp"), None),
            P(("dp", "fsdp"), None),
            P(("dp", "fsdp"), None),
            P(("dp", "fsdp"), None),
            P(("dp", "fsdp"), None),
            P(None, ("dp", "fsdp")),
            P(None, ("dp", "fsdp")),
            P(None, ("dp", "fsdp")),
        ),
        check_vma=False,
    )
```

```python
import functools

import jax
import jax.numpy as jnp
from jax import lax
from jax.experimental import pallas as pl
from jax.experimental.pallas import tpu as pltpu
from jax.sharding import PartitionSpec as P

D = 512
HEADS = 8
HEAD = 64
FF = 2048
QUARTER = FF // 4
LANES = 128
PAIRS = D // LANES
ROWS = 16
STEP = 10
AXES = ("dp", "fsdp")
SCALE = 1.2
FIRST_HALF = 4 * QUARTER + D + 6 * LANES
REAR_COST = 0.5
IN_VMEM = ("input_grad",)
UNROLL = 2
VMEM_BYTES = 16 * 1024 * 1024

norm_epsilon = 1e-05
beta_first = 0.9
beta_second = 0.999
adam_epsilon = 1e-08
weight_decay = 0.1
matrix_rate = 0.02
output_rate = 0.1
vector_rate = 0.2
masked_score = -1000000000.0
gelu_scale = 0.7978845608028654
gelu_cubic = 0.044715
FIRST_PAD = 224


def low(values):
    return values.astype(jnp.bfloat16)


def wide(values):
    return values.astype(jnp.float32)


def dot(left, right):
    return lax.dot_general(left, right, (((1,), (0,)), ((), ())), preferred_element_type=jnp.float32)


def dot_rows(left, right):
    return lax.dot_general(left, right, (((1,), (1,)), ((), ())), preferred_element_type=jnp.float32)


def dot_columns(left, right):
    return lax.dot_general(left, right, (((0,), (0,)), ((), ())), preferred_element_type=jnp.float32)


def cost(micros):
    return pl.CostEstimate(flops=int(micros * SCALE * 1.15e9), bytes_accessed=0, transcendentals=0)


class Refs:
    pass


def call(body, name, micros, ins, outs, scratch=(), reused=()):
    in_names, out_names = [entry[0] for entry in ins], [entry[0] for entry in outs]
    aliases = {in_names.index(taken): out_names.index(given) for taken, given in reused}
    names = [entry[0] for entry in ins] + [entry[0] for entry in outs] + [entry[0] for entry in scratch]

    def kernel(*refs):
        named = Refs()
        for entry, ref in zip(names, refs):
            setattr(named, entry, ref)
        body(named)

    results = pl.pallas_call(
        kernel,
        out_shape=[(pltpu.VMEM if entry in IN_VMEM and len(_) == 0 else jax.ShapeDtypeStruct)(shape, kind) for entry, shape, kind, *_ in outs],
        in_specs=[entry[2] if len(entry) > 2 else whole() for entry in ins],
        out_specs=[whole() if len(entry) == 3 else pl.BlockSpec(memory_space=pl.ANY) for entry in outs],
        scratch_shapes=[
            pltpu.SemaphoreType.DMA(shape) if kind is None else pltpu.VMEM(shape, kind) for _, shape, kind in scratch
        ],
        compiler_params=pltpu.CompilerParams(vmem_limit_bytes=VMEM_BYTES),
        cost_estimate=cost(micros),
        input_output_aliases=aliases,
        name=name,
    )(*[entry[1] for entry in ins])
    out = Refs()
    for entry, value in zip(outs, results):
        setattr(out, entry[0], value)
    return out


def whole():
    return pl.BlockSpec(memory_space=pltpu.VMEM)


def scalars():
    return pl.BlockSpec(memory_space=pltpu.SMEM)


FAR = (0, 8, 16, 24)


def block_device(me, core, place):
    first = jnp.where(core == 0, 4, 2)
    near = (0, first, 6 - first, 6)[place // len(FAR)]
    return me ^ near ^ FAR[place % len(FAR)]


def assemble(me, stacks, targets):
    for stream in range(2):
        for upper in range(2):
            stack = stacks[2 * stream + upper]
            for place in range(8):
                device = block_device(me ^ stream, (me & 1) ^ stream, place + upper * 8)
                rows = pl.ds(pl.multiple_of(device * ROWS, ROWS), ROWS)
                for ref, column in targets:
                    ref[rows, :] = stack[pl.ds(place * ROWS, ROWS), pl.ds(column, ref.shape[1])]


def arrange(me, sources, keep_ref, send_ref):
    for place in range(16):
        here = pl.ds(place * ROWS, ROWS)
        for stream, out in ((0, keep_ref), (1, send_ref)):
            device = block_device(me ^ stream, (me & 1) ^ stream, place)
            rows = pl.ds(pl.multiple_of(device * ROWS, ROWS), ROWS)
            at = 0
            for ref in sources:
                out[here, pl.ds(at, ref.shape[1])] = ref[rows, :].astype(out.dtype)
                at += ref.shape[1]


def arranged(columns):
    shape = (16 * ROWS, columns)
    return [("keep", shape, jnp.float32), ("send", shape, jnp.bfloat16)]


def centre(values):
    centred = values - jnp.mean(values, axis=-1, keepdims=True)
    scale = lax.rsqrt(jnp.mean(centred * centred, axis=-1, keepdims=True) + norm_epsilon)
    return centred * scale, scale


def norm_back(grad, gain, hat, scale):
    inner = grad * gain
    return scale * (
        inner - jnp.mean(inner, axis=-1, keepdims=True) - hat * jnp.mean(inner * hat, axis=-1, keepdims=True)
    )


def masked_rows(order_row, step):
    seq = order_row.shape[1]
    flags = jnp.where(order_row >= step, 1.0, 0.0)
    column = jnp.transpose(jnp.broadcast_to(flags, (LANES, seq)))
    return jnp.concatenate([column] * (D // LANES), axis=1) > 0.5


def pair_split(pair, scale=None):
    lane = lax.broadcasted_iota(jnp.int32, pair.shape, 1)
    values = wide(pair)
    if scale is not None:
        values = values * scale
    return jnp.concatenate([low(jnp.where(lane < HEAD, values, 0.0)), low(jnp.where(lane < HEAD, 0.0, values))], axis=0)


def key_scores(keys, both_queries, length):
    scores = dot_rows(keys, both_queries)
    seq = scores.shape[0]
    tail = scores[FIRST_PAD:]
    row = lax.broadcasted_iota(jnp.int32, tail.shape, 0) + FIRST_PAD
    return jnp.concatenate([scores[:FIRST_PAD], jnp.where(row < length, tail, masked_score)], axis=0)


def load_input(r, span, rows):
    masked = masked_rows(r.order[span], r.step[span])
    return masked, jnp.where(masked, r.vec[4:5, :], wide(r.tokens[rows, :]))


def each_span(seq, spans, body):
    def step(index, carry):
        span = spans[0] + index
        body(span, pl.ds(pl.multiple_of(span * seq, seq), seq))
        return carry

    lax.fori_loop(0, len(spans), step, 0, unroll=UNROLL)


def attention(scalar, order, tokens, first, spans, front=None):
    count, _, seq = order.shape
    fresh = front is None

    def body(r):
        if fresh:
            stacks = (r.stack0, r.stack1, r.stack2, r.stack3)
            assemble(r.me[0], stacks, ((r.weight, 0), (r.columns, 3 * D)))
            r.vec[...] = jnp.transpose(wide(r.columns[...]))[:8]
        else:
            for name in ("normed", "p", "attended"):
                old = getattr(r, "front_" + name)
                getattr(r, name)[pl.ds(0, old.shape[0]), :] = old[...]
            r.logs[: spans[0]] = r.front_logs[...]

        def one_span(span, rows):
            started = load_input(r, span, rows)[1]
            normed = low(centre(started)[0] * r.vec[0:1, :] + r.vec[2:3, :])
            r.normed[rows, :] = normed
            r.p[rows, :] = low(dot(normed, r.weight[...]))
            for pair in range(PAIRS):
                lanes = pl.ds(pair * LANES, LANES)
                queries = pair_split(r.p[rows, lanes], HEAD**-0.5)
                scores = key_scores(r.p[rows, pl.ds(D + pair * LANES, LANES)], queries, r.length[span])
                peak = jnp.max(scores, axis=0, keepdims=True)
                exped = jnp.exp(scores - peak)
                total = jnp.sum(exped, axis=0, keepdims=True)
                probability = low(exped / total)
                r.logs[span, pair : pair + 1, :] = peak + jnp.log(total)
                values = jnp.transpose(r.p[rows, pl.ds(2 * D + pair * LANES, LANES)])
                attended = jnp.concatenate(
                    [dot(values[:HEAD], probability[:, :seq]), dot(values[HEAD:], probability[:, seq:])], axis=0
                )
                r.attended[rows, lanes] = jnp.transpose(low(attended))

        each_span(seq, spans, one_span)

    ins = [(name, array, scalars()) for name, array in scalar.items()] + [("order", order), ("tokens", tokens)]
    count = spans[-1] + 1
    rows = count * seq
    outs = [
        ("normed", (rows, D), jnp.bfloat16),
        ("p", (rows, 3 * D), jnp.bfloat16),
        ("attended", (rows, D), jnp.bfloat16),
        ("logs", (count, PAIRS, 2 * seq), jnp.float32),
    ]
    scratch = []
    if fresh:
        ins += [("stack%d" % n, stack) for n, stack in enumerate(first)]
        outs += [("weight", (D, 3 * D), jnp.bfloat16), ("vec", (8, D), jnp.float32)]
        scratch = [("columns", (D, LANES), jnp.bfloat16)]
    else:
        ins += [("weight", front.weight), ("vec", front.vec)]
        ins += [("front_" + name, getattr(front, name)) for name in ("normed", "p", "attended", "logs")]
    return call(body, "attention", 6 if fresh else REAR_COST, ins, outs, scratch)


def hidden_quarter(normed, upstream, up, down):
    hidden = dot(normed, up)
    grad_act = dot_rows(upstream, down)
    squared = hidden * hidden
    tilt = jnp.tanh(hidden * (gelu_scale + (gelu_scale * gelu_cubic) * squared))
    gate = 0.5 + 0.5 * tilt
    active = hidden * gate
    slope = gate + active * (1.0 - tilt) * (gelu_scale + (3.0 * gelu_scale * gelu_cubic) * squared)
    grad_hidden = low(grad_act * slope)
    return low(active), grad_hidden, dot_rows(grad_hidden, up)


def quarter_call(quarter, scalar, cotangent, stacks, ins, outs, seq, before, after, micros, reused=(), mate=None):
    total = cotangent.shape[0]
    column = 2 * QUARTER * (quarter % 2)

    def body(r):
        stacks = (r.stack0, r.stack1, r.stack2, r.stack3)
        targets = [(r.up, column), (r.down_full, column + QUARTER)]
        if quarter == 0:
            targets.append((r.out_full, 4 * QUARTER))
        assemble(r.me[0], stacks, targets)

        def one_span(span, rows):
            normed = before(r, span, rows)
            active, grad_hidden, back = hidden_quarter(normed, r.cot[rows, :], r.up[...], r.down_full[...])
            r.active[rows, :] = active
            r.grad_hidden[rows, :] = grad_hidden
            after(r, rows, back)

        each_span(seq, range(total // seq), one_span)
        r.grad_up[...] = dot_columns(r.middle_normed[...], r.grad_hidden[...])
        r.grad_down[...] = dot_columns(r.active[...], r.cot[...])
        if mate is not None:
            arrange(r.me[0], (r.mate_up, r.mate_down, r.grad_up, r.grad_down), r.keep, r.send)

    ins = [("me", scalar["me"], scalars()), ("cot", cotangent)] + ins
    ins += [("stack%d" % n, stack) for n, stack in enumerate(stacks)]
    outs = outs + [("active", (total, QUARTER), jnp.bfloat16), ("down_full", (QUARTER, D), jnp.bfloat16)]
    grads = [("grad_up", (D, QUARTER), jnp.float32), ("grad_down", (QUARTER, D), jnp.float32)]
    scratch = [("up", (D, QUARTER), jnp.bfloat16), ("grad_hidden", (total, QUARTER), jnp.bfloat16)]
    if mate is None:
        outs = outs + grads
    else:
        ins += [("mate_up", mate.grad_up), ("mate_down", mate.grad_down)]
        outs = outs + arranged(4 * QUARTER)
        scratch = scratch + grads
    return call(body, "hidden%d" % quarter, micros, ins, outs, scratch, reused)


def first_quarter(scalar, order, tokens, cotangent, vec, attended, stacks):
    seq = order.shape[2]
    total = tokens.shape[0]

    def enter(r, span, rows):
        middle = load_input(r, span, rows)[1] + dot(r.attended[rows, :], r.out_full[...])
        r.middle[rows, :] = middle
        normed = low(centre(middle)[0] * r.vec[1:2, :] + r.vec[3:4, :])
        r.middle_normed[rows, :] = normed
        return normed

    def leave(r, rows, back):
        r.back[rows, :] = back

    ins = [("step", scalar["step"], scalars()), ("order", order), ("tokens", tokens), ("vec", vec), ("attended", attended)]
    outs = [("middle", (total, D), jnp.float32), ("middle_normed", (total, D), jnp.bfloat16)]
    outs += [("back", (total, D), jnp.float32), ("out_full", (D, D), jnp.bfloat16)]
    return quarter_call(0, scalar, cotangent, stacks, ins, outs, seq, enter, leave, 8.5)


def next_quarter(quarter, scalar, cotangent, stacks, normed, back, seq, mate=None):
    total = normed.shape[0]

    def take(r, span, rows):
        return r.middle_normed[rows, :]

    def leave(r, rows, back):
        r.back[rows, :] = r.old_back[rows, :] + back

    ins = [("middle_normed", normed), ("old_back", back)]
    outs = [("back", (total, D), jnp.float32)]
    reused = [("old_back", "back")]
    return quarter_call(quarter, scalar, cotangent, stacks, ins, outs, seq, take, leave, 6.5, reused, mate)


def middle_back(scalar, cotangent, vec, attended, middle, back, out_full, seq, quarters):
    total = middle.shape[0]

    def body(r):
        r.dvec[...] = jnp.zeros_like(r.dvec)

        def one_span(span, rows):
            back = r.back[rows, :]
            hat, scale = centre(r.middle[rows, :])
            dmiddle = wide(r.cot[rows, :]) + norm_back(back, r.vec[1:2, :], hat, scale)
            r.dmiddle[rows, :] = dmiddle
            r.dvec[1:2, :] += jnp.sum(back * hat, axis=0, keepdims=True)
            r.dvec[3:4, :] += jnp.sum(back, axis=0, keepdims=True)
            mixed = low(dmiddle)
            r.mixed[rows, :] = mixed
            r.dattended[rows, :] = low(dot_rows(mixed, r.out_full[...]))

        each_span(seq, range(total // seq), one_span)
        r.grad_out[...] = dot_columns(r.attended[...], r.mixed[...])
        arrange(r.me[0], (r.up0, r.down0, r.up1, r.down1, r.grad_out), r.keep, r.send)

    ins = [("me", scalar["me"], scalars()), ("cot", cotangent), ("vec", vec), ("attended", attended)]
    ins += [("middle", middle), ("back", back), ("out_full", out_full)]
    for n, quarter in enumerate(quarters):
        ins += [("up%d" % n, quarter.grad_up), ("down%d" % n, quarter.grad_down)]
    outs = [("dmiddle", (total, D), jnp.float32), ("dattended", (total, D), jnp.bfloat16), ("dvec", (8, D), jnp.float32)]
    outs += arranged(4 * QUARTER + D)
    scratch = [("grad_out", (D, D), jnp.float32), ("mixed", (total, D), jnp.bfloat16)]
    return call(body, "middle_back", 4, ins, outs, scratch)


def branch_output(middle, quarters, seq, spans, front=None, grad=None):
    rows_before = spans[0] * seq
    rows_here = len(spans) * seq

    def body(r):
        copies = []
        if front is not None:
            here = pl.ds(rows_before, rows_here)
            copies = [
                pltpu.make_async_copy(r.grad, r.input_grad, r.done.at[0]),
                pltpu.make_async_copy(r.front, r.result.at[pl.ds(0, rows_before), :], r.done.at[1]),
                pltpu.make_async_copy(r.rear, r.result.at[here, :], r.done.at[2]),
            ]
            copies[0].start()
            copies[1].start()
        target = r.result if front is None else r.rear

        def one_span(span, rows):
            result = r.middle[rows, :]
            for n in range(4):
                result = result + dot(getattr(r, "active%d" % n)[rows, :], getattr(r, "down%d" % n)[...])
            target[pl.ds(pl.multiple_of((span - spans[0]) * seq, seq), seq), :] = low(result)

        each_span(seq, spans, one_span)
        if front is not None:
            copies[2].start()
            for copy in copies:
                copy.wait()

    ins = [("middle", middle)]
    for n, quarter in enumerate(quarters):
        ins += [("active%d" % n, quarter.active), ("down%d" % n, quarter.down_full)]
    if front is None:
        return call(body, "branch_output", 25, ins, [("result", (rows_here, D), jnp.bfloat16)]).result
    ins += [("front", front), ("grad", grad)]
    outs = [("result", (rows_before + rows_here, D), jnp.bfloat16, True), ("input_grad", grad.shape, jnp.float32, True)]
    scratch = [("rear", (rows_here, D), jnp.bfloat16), ("done", (3,), None)]
    done = call(body, "branch_output", 25, ins, outs, scratch)
    return done.result, done.input_grad


def attention_back(scalar, pair, normed, p, logs, dattended, seq, mate=None):
    total = normed.shape[0]
    last = pair == PAIRS - 1

    def body(r):
        def one_span(span, rows):
            queries = pair_split(r.p[rows, pl.ds(pair * LANES, LANES)], HEAD**-0.5)
            dattended = pair_split(r.dattended[rows, pl.ds(pair * LANES, LANES)])
            keys = r.p[rows, pl.ds(D + pair * LANES, LANES)]
            scores = key_scores(keys, queries, r.length[span])
            probability = jnp.exp(scores - r.logs[span, pair : pair + 1, :])
            dprobability = dot_rows(r.p[rows, pl.ds(2 * D + pair * LANES, LANES)], dattended)
            inner = jnp.sum(probability * dprobability, axis=0, keepdims=True)
            dscores = low(probability * (dprobability - inner))
            dvalues = low(dot(low(probability), dattended))
            dkeys = low(dot(dscores, queries))
            keys = jnp.transpose(low(wide(keys) * HEAD**-0.5))
            dqueries = jnp.concatenate([dot(keys[:HEAD], dscores[:, :seq]), dot(keys[HEAD:], dscores[:, seq:])], axis=0)
            r.dp[rows, :] = jnp.concatenate([jnp.transpose(low(dqueries)), dkeys, dvalues], axis=1)

        each_span(seq, range(total // seq), one_span)
        if not last:
            r.grad[...] = dot_columns(r.normed[...], r.dp[...])
        if mate is not None:
            arrange(r.me[0], (r.mate, r.grad), r.keep, r.send)

    ins = [("me", scalar["me"], scalars()), ("length", scalar["length"], scalars())]
    ins += [("normed", normed), ("p", p), ("logs", logs), ("dattended", dattended)]
    outs = [("dp", (total, 3 * LANES), jnp.bfloat16)]
    grad = ("grad", (D, 3 * LANES), jnp.float32)
    scratch = []
    if mate is not None:
        ins += [("mate", mate.grad)]
        outs += arranged(6 * LANES)
        scratch = [grad]
    elif not last:
        outs += [grad]
    return call(body, "attention_back", 4.6, ins, outs, scratch)


def input_back(scalar, order, tokens, vec, normed, dmiddle, weight, dvec, parts):
    seq = order.shape[2]
    total = tokens.shape[0]

    def body(r):
        parts = [getattr(r, "dp%d" % n) for n in range(PAIRS)]
        r.dvec[...] = jnp.zeros_like(r.dvec)
        r.dvec[:8, :] = r.dvec_in[...]

        def one_span(span, rows):
            dp = [part[rows, pl.ds(kind * LANES, LANES)] for kind in range(3) for part in parts]
            back = dot_rows(jnp.concatenate(dp, axis=1), r.weight[...])
            masked, started = load_input(r, span, rows)
            hat, scale = centre(started)
            dstarted = r.dmiddle[rows, :] + norm_back(back, r.vec[0:1, :], hat, scale)
            r.input_grad[rows, :] = jnp.where(masked, 0.0, dstarted)
            r.dvec[0:1, :] += jnp.sum(back * hat, axis=0, keepdims=True)
            r.dvec[2:3, :] += jnp.sum(back, axis=0, keepdims=True)
            r.dvec[4:5, :] += jnp.sum(jnp.where(masked, dstarted, 0.0), axis=0, keepdims=True)

        each_span(seq, range(total // seq), one_span)
        r.columns[...] = jnp.transpose(r.dvec[...])
        r.grad[...] = dot_columns(r.normed[...], parts[-1][...])
        arrange(r.me[0], (r.mate, r.grad, r.columns), r.keep, r.send)

    ins = [("me", scalar["me"], scalars()), ("step", scalar["step"], scalars()), ("order", order), ("tokens", tokens)]
    ins += [("vec", vec), ("dmiddle", dmiddle), ("normed", normed), ("weight", weight), ("dvec_in", dvec)]
    ins += [("dp%d" % n, part.dp) for n, part in enumerate(parts)]
    ins += [("mate", parts[-2].grad)]
    outs = [("input_grad", (total, D), jnp.float32)] + arranged(7 * LANES)
    scratch = [
        ("dvec", (LANES, D), jnp.float32),
        ("columns", (D, LANES), jnp.float32),
        ("grad", (D, 3 * LANES), jnp.float32),
    ]
    return call(body, "input_back", 6.5, ins, outs, scratch)


def fold_kernel(keep_ref, taken_ref, total_ref, send_ref):
    half = total_ref.shape[0]
    total_ref[...] = keep_ref[:half, :] + wide(taken_ref[:half, :])
    send_ref[...] = low(keep_ref[half:, :] + wide(taken_ref[half:, :]))


def fold(keep, taken):
    rows, columns = keep.shape
    return pl.pallas_call(
        fold_kernel,
        out_shape=(
            jax.ShapeDtypeStruct((rows // 2, columns), jnp.float32),
            jax.ShapeDtypeStruct((rows // 2, columns), jnp.bfloat16),
        ),
        in_specs=[whole()] * 2,
        out_specs=(whole(), whole()),
        compiler_params=pltpu.CompilerParams(vmem_limit_bytes=VMEM_BYTES),
        cost_estimate=cost(1),
        name="fold",
    )(keep, taken)


def adam_update(master, gradient, moment, square, step_rate, decay_rate):
    moment_new = beta_first * moment + (1.0 - beta_first) * gradient
    square_new = beta_second * square + (1.0 - beta_second) * gradient * gradient
    corrected = (
        moment_new
        / (1.0 - beta_first**STEP)
        / (jnp.sqrt(square_new / (1.0 - beta_second**STEP)) + adam_epsilon)
    )
    return (moment_new, square_new, master - step_rate * (corrected + decay_rate * master))


def unit_order():
    unit = lax.broadcasted_iota(jnp.int32, (D, D), 0)
    place = lax.broadcasted_iota(jnp.int32, (D, D), 1)
    wanted = (place % LANES // ROWS) * 64 + (place // LANES) * ROWS + place % ROWS
    return jnp.where(unit == wanted, 1.0, 0.0).astype(jnp.bfloat16)


def hidden_update_kernel(*refs):
    total, parts = refs[0], refs[1:4]
    up, down, out = refs[4:7], refs[7:10], refs[10:13]
    new_up, new_down, new_out = refs[13:16], refs[16:19], refs[19:22]

    def summed(column, width):
        columns = pl.ds(column, width)
        return total[:ROWS, columns] + sum(wide(part[:, columns]) for part in parts)

    def start(quarter):
        return FIRST_HALF * (1 - quarter // 2) + (quarter % 2) * 2 * QUARTER

    def update(new, old, index, grad, rate):
        results = adam_update(old[0][index], grad, old[1][index], old[2][index], rate, weight_decay)
        for ref, value in zip(new, results):
            ref[index] = value

    sort = unit_order()
    for group in range(FF // D):
        grads = []
        for quarter in range(4):
            grads.append(summed(start(quarter) + group * LANES, LANES))
        rest = jnp.concatenate(grads, axis=1)
        grad = 0.0
        for _ in range(3):
            piece = low(rest)
            grad = grad + dot_rows(piece, sort)
            rest = rest - wide(piece)
        update(new_up, up, (slice(None), pl.ds(group * D, D)), grad, matrix_rate)
    for quarter in range(4):
        grad = summed(start(quarter) + QUARTER, D)
        update(new_down, down, (pl.ds(quarter * ROWS, ROWS), slice(None)), grad, matrix_rate)
    update(new_out, out, Ellipsis, summed(4 * QUARTER, D), output_rate)


def hidden_update(total, parts, up, down, out):
    outs = [jax.ShapeDtypeStruct(state[0].shape, jnp.float32) for state in (up, down, out) for _ in range(3)]
    results = pl.pallas_call(
        hidden_update_kernel,
        out_shape=outs,
        in_specs=[whole()] * 13,
        out_specs=[whole()] * 9,
        compiler_params=pltpu.CompilerParams(vmem_limit_bytes=VMEM_BYTES),
        cost_estimate=cost(3),
        name="hidden_update",
    )(total, *parts, *up, *down, *out)
    return results[:3], results[3:6], results[6:]


def last_update_kernel(*refs):
    early, late = refs[:4], refs[4:8]
    qkv, vec = refs[8:11], refs[11:14]
    new_qkv, new_vec = refs[14:17], refs[17:20]

    def summed(group, column):
        columns = pl.ds(column, LANES)
        return group[0][:ROWS, columns] + sum(wide(part[:, columns]) for part in group[1:])

    for pair in range(PAIRS):
        for kind in range(3):
            group, first = (early, 4 * QUARTER + D) if pair < 2 else (late, 0)
            grad = summed(group, first + (3 * (pair % 2) + kind) * LANES)
            here = pl.ds((kind * PAIRS + pair) * LANES, LANES)
            moment, square, master = adam_update(
                qkv[0][:, here], grad, qkv[1][:, here], qkv[2][:, here], matrix_rate, weight_decay
            )
            new_qkv[0][:, here], new_qkv[1][:, here], new_qkv[2][:, here] = moment, square, master
    grad = summed(late, 6 * LANES)
    grad = jnp.transpose(jnp.concatenate([grad, jnp.zeros((LANES - ROWS, LANES), jnp.float32)], axis=0))
    grad = grad[: vec[0].shape[0], :ROWS]
    results = adam_update(vec[0][...], grad, vec[1][...], vec[2][...], vector_rate, 0.0)
    for ref, value in zip(new_vec, results):
        ref[...] = value


def last_update(total_early, parts_early, total_late, parts_late, qkv, vec):
    outs = [jax.ShapeDtypeStruct(qkv[0].shape, jnp.float32)] * 3 + [jax.ShapeDtypeStruct(vec[0].shape, jnp.float32)] * 3
    results = pl.pallas_call(
        last_update_kernel,
        out_shape=outs,
        in_specs=[whole()] * 14,
        out_specs=[whole()] * 6,
        compiler_params=pltpu.CompilerParams(vmem_limit_bytes=VMEM_BYTES),
        cost_estimate=cost(1),
        name="last_update",
    )(total_early, *parts_early, total_late, *parts_late, *qkv, *vec)
    return results[:3], results[3:]


def exchange(values, count, even_mask, odd_mask):
    pairs = [(i, i ^ (odd_mask if i % 2 else even_mask)) for i in range(count)]
    return lax.ppermute(values, AXES, pairs)


def tie(value, *others):
    return lax.optimization_barrier((value, others))[0]


class Gather:
    def __init__(self, piece, count):
        self.piece, self.count, self.direct = piece, count, piece.shape[0] == ROWS
        self.parts, self.other = [], None

    def far(self):
        if self.direct:
            self.parts = [exchange(self.piece, self.count, offset, offset) for offset in FAR[1:]]
        return self.parts

    def split(self, columns):
        pair = [Gather(self.piece[:, :columns], self.count), Gather(self.piece[:, columns:], self.count)]
        parts = self.far()
        pair[0].parts = [part[:, :columns] for part in parts]
        pair[1].parts = [part[:, columns:] for part in parts]
        return pair

    def stack(self, *waits):
        if self.direct:
            self.piece = jnp.concatenate([self.piece] + [tie(part, *waits) for part in self.parts], axis=0)
        return self.piece

    def core(self, *waits):
        if not self.direct:
            return self.piece
        start = self.other.shape[0] if self.other is not None else 0
        taken = tie(exchange(self.piece[start:], self.count, 1, 1), *waits)
        self.other = taken if self.other is None else jnp.concatenate([self.other, taken], axis=0)
        return taken

    def near(self, *waits):
        if self.direct:
            taken = exchange(self.piece, self.count, 4, 2)
            self.piece = jnp.concatenate([self.piece, tie(taken, *waits)], axis=0)
        return self.piece

    def late(self, *waits):
        if self.direct:
            self.rest = tie(exchange(self.piece, self.count, 2, 4), *waits)

    def finish(self, *waits):
        if not self.direct:
            return ordered_stacks(self.piece)
        return (self.piece, self.rest, self.other, tie(exchange(self.rest, self.count, 1, 1), *waits))


class Scatter:
    def __init__(self, arranged, count, direct):
        self.total, self.send, self.count, self.direct = arranged.keep, arranged.send, count, direct

    def step(self, even, odd, *waits):
        if self.direct:
            self.total, self.send = fold(self.total, tie(exchange(self.send, self.count, even, odd), *waits))
        return self.total, self.send

    def core(self, *waits):
        return self.step(1, 1, *waits)

    def near(self, *waits):
        return self.step(2, 4, *waits)

    def next(self, *waits):
        if self.direct:
            self.total = self.total + wide(tie(exchange(self.send, self.count, 4, 2), *waits))
        return self.total

    def join(self, other):
        self.total = jnp.concatenate([self.total, other.total], axis=1)
        self.send = jnp.concatenate([self.send, other.send], axis=1)

    def parts(self, *waits):
        if not self.direct:
            return []
        taken = []
        for place in range(1, len(FAR)):
            part = low(self.total[place * ROWS : (place + 1) * ROWS])
            taken.append(tie(exchange(part, self.count, FAR[place], FAR[place]), *waits))
        return taken

    def full(self):
        return full_piece(self.total, self.send)


def split_units(up, down):
    rows, units = up.shape
    up = up.reshape(rows, units // 64, 4, ROWS)
    down = down.reshape(rows // ROWS, 4, ROWS, D)
    ups = [up[:, :, quarter].reshape(rows, units // 4) for quarter in range(4)]
    downs = [down[:, quarter].reshape(rows, D) for quarter in range(4)]
    return [jnp.concatenate([ups[n], downs[n], ups[n + 1], downs[n + 1]], axis=1) for n in (0, 2)]


def pack_kernel(*refs):
    sources, first, hidden, buffers, done = refs[:5], refs[5], refs[6], refs[7:12], refs[12]
    copies = [pltpu.make_async_copy(sources[n], buffers[n], done.at[n]) for n in range(5)]
    for copy in copies:
        copy.start()
    qkv, vec, out, up, down = buffers
    copies[0].wait()
    first[:, pl.ds(0, 3 * D)] = low(qkv[...])
    copies[1].wait()
    rows, columns = vec.shape
    turned = jnp.concatenate([vec[...], jnp.zeros((rows, LANES - columns), jnp.float32)], axis=1)
    turned = jnp.transpose(jnp.concatenate([turned, jnp.zeros((LANES - rows, LANES), jnp.float32)], axis=0))
    first[:, pl.ds(3 * D, LANES)] = low(turned[:ROWS])
    for copy in copies[2:]:
        copy.wait()
    sort = unit_order()
    for group in range(FF // D):
        mixed = low(dot(low(up[:, pl.ds(group * D, D)]), sort))
        for quarter in range(4):
            column = 2 * QUARTER * ((quarter + 2) % 4) + group * LANES
            hidden[:, pl.ds(column, LANES)] = mixed[:, quarter * LANES : (quarter + 1) * LANES]
    for quarter in range(4):
        rows = down[pl.ds(quarter * ROWS, ROWS), :]
        hidden[:, pl.ds(2 * QUARTER * ((quarter + 2) % 4) + QUARTER, D)] = low(rows)
    hidden[:, pl.ds(8 * QUARTER, D)] = low(out[...])


def pack(*sources):
    return pl.pallas_call(
        pack_kernel,
        out_shape=(
            jax.ShapeDtypeStruct((ROWS, 3 * D + LANES), jnp.bfloat16),
            jax.ShapeDtypeStruct((ROWS, 8 * QUARTER + D), jnp.bfloat16),
        ),
        in_specs=[pl.BlockSpec(memory_space=pl.ANY)] * 5,
        out_specs=(whole(), whole()),
        scratch_shapes=[pltpu.VMEM(source.shape, source.dtype) for source in sources] + [pltpu.SemaphoreType.DMA((5,))],
        compiler_params=pltpu.CompilerParams(vmem_limit_bytes=VMEM_BYTES),
        cost_estimate=cost(1),
        name="pack",
    )(*[pltpu.with_memory_space_constraint(source, pltpu.HBM) for source in sources])


def join_units(pieces):
    rows = pieces[0].shape[0]
    groups = [[piece[:, n * QUARTER : (n + 1) * QUARTER] for n in range(4)] for piece in pieces]
    ups = [groups[0][0], groups[0][2], groups[1][0], groups[1][2]]
    downs = [groups[0][1], groups[0][3], groups[1][1], groups[1][3]]
    up = jnp.stack([group.reshape(rows, QUARTER // ROWS, ROWS) for group in ups], axis=2)
    down = jnp.stack([group.reshape(rows // ROWS, ROWS, D) for group in downs], axis=1)
    return up.reshape(rows, 4 * QUARTER), down.reshape(rows * 4, D)


def stack_order(core):
    near = (0, 4, 2, 6) if core == 0 else (0, 2, 4, 6)
    return [core ^ group ^ offset for group in near for offset in FAR]


def ordered_stacks(piece):
    blocks = piece.reshape(32, ROWS, piece.shape[1])
    stacks = []
    for core in range(2):
        ordered = jnp.stack([blocks[device] for device in stack_order(core)])
        ordered = ordered.reshape(16 * ROWS, piece.shape[1])
        stacks += [ordered[: 8 * ROWS], ordered[8 * ROWS :]]
    return tuple(stacks)


def full_piece(keep, send):
    columns = keep.shape[1]
    blocks = jnp.concatenate([keep, wide(send)], axis=0).reshape(32, ROWS, columns)
    order = stack_order(0) + stack_order(1)
    return jnp.stack([blocks[order.index(device)] for device in range(32)]).reshape(32 * ROWS, columns)


def local(
    tokens,
    cotangent,
    reveal_order,
    reveal_step,
    lengths,
    weight_qkv,
    weight_out,
    weight_up,
    weight_down,
    vectors,
    moment_qkv,
    square_qkv,
    moment_out,
    square_out,
    moment_up,
    square_up,
    moment_down,
    square_down,
    moment_vec,
    square_vec,
):
    count = lax.axis_size("dp") * lax.axis_size("fsdp")
    direct = weight_qkv.shape[0] == ROWS and count == 32
    me = lax.axis_index("dp") * lax.axis_size("fsdp") + lax.axis_index("fsdp")
    me = (me if direct else 0 * me).astype(jnp.int32)[None]
    spans, seq = reveal_order.shape
    order = reveal_order.reshape(spans, 1, seq)
    flat = tokens.reshape(spans * seq, D)
    upstream = cotangent.reshape(spans * seq, D)

    if direct:
        piece_one, piece_rest = pack(weight_qkv, vectors, weight_out, weight_up, weight_down)
    else:
        columns = jnp.pad(low(vectors).T, ((0, 0), (0, LANES - vectors.shape[0])))
        halves = [jnp.concatenate([low(weight_qkv), columns], axis=1), low(weight_out), low(weight_up), low(weight_down)]
        piece_one, out, up, down = [lax.all_gather(half, AXES, axis=0, tiled=True) for half in halves]
        hidden = split_units(up, down)
        piece_rest = jnp.concatenate([hidden[1], hidden[0], out], axis=1)
    scalar = {"me": me, "step": reveal_step, "length": lengths}

    one = Gather(piece_one, count)
    one.far()
    one.stack()
    two = Gather(tie(piece_rest[:, 4 * QUARTER :], one.core()), count)
    two.far()
    one.near()
    one.late()
    three = Gather(tie(piece_rest[:, : 4 * QUARTER], one.core()), count)
    three.far()
    first = one.finish()
    two.stack()
    front = attention(scalar, order, flat, first, range(0, spans // 2))
    two.near()
    two.late()
    two.core()
    three.stack(front.logs)
    rear = attention(scalar, order, tie(flat, two.piece), None, range(spans // 2, spans), front)
    vec, weight = front.vec, front.weight
    two.rest = tie(two.rest, rear.logs) if direct else None
    second = two.finish()
    three.near(rear.logs)
    h = [first_quarter(scalar, order, flat, tie(upstream, three.piece), vec, rear.attended, second)]
    normed = h[0].middle_normed
    three.late(h[0].back)
    three.core(h[0].back)
    h += [next_quarter(1, scalar, upstream, second, normed, h[0].back, seq, h[0])]
    third = three.finish(h[1].back)
    h += [next_quarter(2, scalar, upstream, third, normed, h[1].back, seq)]
    sum_one = Scatter(h[1], count, direct)
    h += [next_quarter(3, scalar, tie(upstream, *sum_one.core(h[2].back)), third, normed, h[2].back, seq)]
    turn = middle_back(
        scalar, tie(upstream, h[3].back), vec, rear.attended, h[0].middle, h[3].back, h[0].out_full, seq, h[2:]
    )
    sum_one.near(turn.dattended)
    sum_two = Scatter(turn, count, direct)

    def part(pair, *waits, mate=None):
        dattended = tie(turn.dattended, *waits)
        return attention_back(scalar, pair, rear.normed, rear.p, rear.logs, dattended, seq, mate)

    parts = [part(0, sum_one.total)]
    parts += [part(1, sum_one.next(parts[0].dp), *sum_two.core(parts[0].dp), mate=parts[0])]
    early = Scatter(parts[1], count, direct)
    parts += [part(2, sum_one.total)]
    early.core(parts[2].dp)
    sum_two.near(parts[2].dp)
    parts += [part(3, sum_two.total, early.total)]
    early.near(parts[3].dp)
    if direct:
        sum_two.join(early)
    ready = tie(flat, parts[3].dp, sum_two.total)
    final = input_back(scalar, order, ready, vec, rear.normed, turn.dmiddle, weight, turn.dvec, parts)
    late = Scatter(final, count, direct)
    result = branch_output(tie(h[0].middle, final.input_grad), h, seq, range(0, spans // 2))
    sum_two.next(result)
    late.core(result)
    middle = tie(h[0].middle, late.total)
    result, input_grad = branch_output(middle, h, seq, range(spans // 2, spans), result, final.input_grad)
    if direct:
        sum_two.total = jnp.concatenate([sum_two.total, sum_one.total], axis=1)
    parts_two = sum_two.parts()
    late.near(result)
    qkv_state = (weight_qkv, moment_qkv, square_qkv)
    vec_state = (vectors, moment_vec, square_vec)
    out_state = (weight_out, moment_out, square_out)
    up_state = (weight_up, moment_up, square_up)
    down_state = (weight_down, moment_down, square_down)
    if direct:
        states = hidden_update(tie(sum_two.total, late.send), parts_two, up_state, down_state, out_state)
        new_up, new_down, new_out = states
        late.next()
        parts_late = late.parts()
        new_qkv, new_vec = last_update(sum_two.total, parts_two, late.total, parts_late, qkv_state, vec_state)
    else:
        ones, twos = sum_one.full(), sum_two.full()
        threes = jnp.concatenate([early.full(), late.full()], axis=1)
        qkv = [threes[:, (3 * pair + kind) * LANES :][:, :LANES] for kind in range(3) for pair in range(PAIRS)]
        grads = [jnp.concatenate(qkv, axis=1), threes[:, 3 * D : 3 * D + vectors.shape[0]]]
        grads += [twos[:, 4 * QUARTER :], *join_units([ones, twos])]
        grads = [lax.psum_scatter(grad, AXES, scatter_dimension=0, tiled=True) for grad in grads]

        def update(state, grad, rate, decay):
            return adam_update(state[0], grad, state[1], state[2], rate, decay)

        new_qkv = update(qkv_state, grads[0], matrix_rate, weight_decay)
        new_vec = update(vec_state, grads[1].T, vector_rate, 0.0)
        new_out = update(out_state, grads[2], output_rate, weight_decay)
        new_up = update(up_state, grads[3], matrix_rate, weight_decay)
        new_down = update(down_state, grads[4], matrix_rate, weight_decay)
    return (
        result.reshape(tokens.shape),
        input_grad.reshape(tokens.shape),
        *new_qkv,
        *new_out,
        *new_up,
        *new_down,
        *new_vec,
    )


def solution(mesh):
    return jax.shard_map(
        local,
        mesh=mesh,
        in_specs=(
            P(("dp", "fsdp"), None, None),
            P(("dp", "fsdp"), None, None),
            P(("dp", "fsdp"), None),
            P(("dp", "fsdp")),
            P(("dp", "fsdp")),
            P(("dp", "fsdp"), None),
            P(("dp", "fsdp"), None),
            P(("dp", "fsdp"), None),
            P(("dp", "fsdp"), None),
            P(None, ("dp", "fsdp")),
            P(("dp", "fsdp"), None),
            P(("dp", "fsdp"), None),
            P(("dp", "fsdp"), None),
            P(("dp", "fsdp"), None),
            P(("dp", "fsdp"), None),
            P(("dp", "fsdp"), None),
            P(("dp", "fsdp"), None),
            P(("dp", "fsdp"), None),
            P(None, ("dp", "fsdp")),
            P(None, ("dp", "fsdp")),
        ),
        out_specs=(
            P(("dp", "fsdp"), None, None),
            P(("dp", "fsdp"), None, None),
            P(("dp", "fsdp"), None),
            P(("dp", "fsdp"), None),
            P(("dp", "fsdp"), None),
            P(("dp", "fsdp"), None),
            P(("dp", "fsdp"), None),
            P(("dp", "fsdp"), None),
            P(("dp", "fsdp"), None),
            P(("dp", "fsdp"), None),
            P(("dp", "fsdp"), None),
            P(("dp", "fsdp"), None),
            P(("dp", "fsdp"), None),
            P(("dp", "fsdp"), None),
            P(None, ("dp", "fsdp")),
            P(None, ("dp", "fsdp")),
            P(None, ("dp", "fsdp")),
        ),
        check_vma=False,
    )
```

```python
import functools

import jax
import jax.numpy as jnp
from jax import lax
from jax.experimental import pallas as pl
from jax.experimental.pallas import tpu as pltpu
from jax.sharding import PartitionSpec as P

D = 512
HEADS = 8
HEAD = 64
FF = 2048
QUARTER = FF // 4
LANES = 128
PAIRS = D // LANES
ROWS = 16
STEP = 10
AXES = ("dp", "fsdp")
SCALE = 1.2
FIRST_HALF = 4 * QUARTER + D + 6 * LANES
REAR_COST = 0.5
AHEAD = (0,)
IN_VMEM = ("input_grad",)
VMEM_BYTES = 16 * 1024 * 1024

norm_epsilon = 1e-05
beta_first = 0.9
beta_second = 0.999
adam_epsilon = 1e-08
weight_decay = 0.1
matrix_rate = 0.02
output_rate = 0.1
vector_rate = 0.2
masked_score = -1000000000.0
gelu_scale = 0.7978845608028654
gelu_cubic = 0.044715
FIRST_PAD = 224


def low(values):
    return values.astype(jnp.bfloat16)


def wide(values):
    return values.astype(jnp.float32)


def dot(left, right):
    return lax.dot_general(left, right, (((1,), (0,)), ((), ())), preferred_element_type=jnp.float32)


def dot_rows(left, right):
    return lax.dot_general(left, right, (((1,), (1,)), ((), ())), preferred_element_type=jnp.float32)


def dot_columns(left, right):
    return lax.dot_general(left, right, (((0,), (0,)), ((), ())), preferred_element_type=jnp.float32)


def cost(micros):
    return pl.CostEstimate(flops=int(micros * SCALE * 1.15e9), bytes_accessed=0, transcendentals=0)


class Refs:
    pass


def call(body, name, micros, ins, outs, scratch=(), reused=()):
    in_names, out_names = [entry[0] for entry in ins], [entry[0] for entry in outs]
    aliases = {in_names.index(taken): out_names.index(given) for taken, given in reused}
    names = [entry[0] for entry in ins] + [entry[0] for entry in outs] + [entry[0] for entry in scratch]

    def kernel(*refs):
        named = Refs()
        for entry, ref in zip(names, refs):
            setattr(named, entry, ref)
        body(named)

    results = pl.pallas_call(
        kernel,
        out_shape=[(pltpu.VMEM if entry in IN_VMEM and len(_) == 0 else jax.ShapeDtypeStruct)(shape, kind) for entry, shape, kind, *_ in outs],
        in_specs=[entry[2] if len(entry) > 2 else whole() for entry in ins],
        out_specs=[whole() if len(entry) == 3 else pl.BlockSpec(memory_space=pl.ANY) for entry in outs],
        scratch_shapes=[
            pltpu.SemaphoreType.DMA(shape) if kind is None else pltpu.VMEM(shape, kind) for _, shape, kind in scratch
        ],
        compiler_params=pltpu.CompilerParams(vmem_limit_bytes=VMEM_BYTES),
        cost_estimate=cost(micros),
        input_output_aliases=aliases,
        name=name,
    )(*[entry[1] for entry in ins])
    out = Refs()
    for entry, value in zip(outs, results):
        setattr(out, entry[0], value)
    return out


def whole():
    return pl.BlockSpec(memory_space=pltpu.VMEM)


def scalars():
    return pl.BlockSpec(memory_space=pltpu.SMEM)


FAR = (0, 8, 16, 24)


def block_device(me, core, place):
    first = jnp.where(core == 0, 4, 2)
    near = (0, first, 6 - first, 6)[place // len(FAR)]
    return me ^ near ^ FAR[place % len(FAR)]


def assemble(me, stacks, targets):
    for stream in range(2):
        for upper in range(2):
            stack = stacks[2 * stream + upper]
            for place in range(8):
                device = block_device(me ^ stream, (me & 1) ^ stream, place + upper * 8)
                rows = pl.ds(pl.multiple_of(device * ROWS, ROWS), ROWS)
                for ref, column in targets:
                    ref[rows, :] = stack[pl.ds(place * ROWS, ROWS), pl.ds(column, ref.shape[1])]


def arrange(me, sources, keep_ref, send_ref):
    for place in range(16):
        here = pl.ds(place * ROWS, ROWS)
        for stream, out in ((0, keep_ref), (1, send_ref)):
            device = block_device(me ^ stream, (me & 1) ^ stream, place)
            rows = pl.ds(pl.multiple_of(device * ROWS, ROWS), ROWS)
            at = 0
            for ref in sources:
                out[here, pl.ds(at, ref.shape[1])] = ref[rows, :].astype(out.dtype)
                at += ref.shape[1]


def arranged(columns):
    shape = (16 * ROWS, columns)
    return [("keep", shape, jnp.float32), ("send", shape, jnp.bfloat16)]


def centre(values):
    centred = values - jnp.mean(values, axis=-1, keepdims=True)
    scale = lax.rsqrt(jnp.mean(centred * centred, axis=-1, keepdims=True) + norm_epsilon)
    return centred * scale, scale


def norm_back(grad, gain, hat, scale):
    inner = grad * gain
    return scale * (
        inner - jnp.mean(inner, axis=-1, keepdims=True) - hat * jnp.mean(inner * hat, axis=-1, keepdims=True)
    )


def masked_rows(order_row, step):
    seq = order_row.shape[1]
    flags = jnp.where(order_row >= step, 1.0, 0.0)
    column = jnp.transpose(jnp.broadcast_to(flags, (LANES, seq)))
    return jnp.concatenate([column] * (D // LANES), axis=1) > 0.5


def pair_split(pair, scale=None):
    lane = lax.broadcasted_iota(jnp.int32, pair.shape, 1)
    values = wide(pair)
    if scale is not None:
        values = values * scale
    return jnp.concatenate([low(jnp.where(lane < HEAD, values, 0.0)), low(jnp.where(lane < HEAD, 0.0, values))], axis=0)


def key_scores(keys, both_queries, length):
    scores = dot_rows(keys, both_queries)
    seq = scores.shape[0]
    tail = scores[FIRST_PAD:]
    row = lax.broadcasted_iota(jnp.int32, tail.shape, 0) + FIRST_PAD
    return jnp.concatenate([scores[:FIRST_PAD], jnp.where(row < length, tail, masked_score)], axis=0)


def load_input(r, span, rows):
    masked = masked_rows(r.order[span], r.step[span])
    return masked, jnp.where(masked, r.vec[4:5, :], wide(r.tokens[rows, :]))


def each_span(seq, spans, body, ahead=None):
    def step(index, carry):
        here = []
        for n in range(2):
            span = spans[0] + 2 * index + n
            here.append((span, pl.ds(pl.multiple_of(span * seq, seq), seq)))
        made = [ahead(span, rows) if ahead is not None else None for span, rows in here]
        for (span, rows), value in zip(here, made):
            body(span, rows, value)
        return carry

    lax.fori_loop(0, len(spans) // 2, step, 0)


def attention(scalar, order, tokens, first, spans, front=None):
    count, _, seq = order.shape
    fresh = front is None

    def body(r):
        if fresh:
            stacks = (r.stack0, r.stack1, r.stack2, r.stack3)
            assemble(r.me[0], stacks, ((r.weight, 0), (r.columns, 3 * D)))
            r.vec[...] = jnp.transpose(wide(r.columns[...]))[:8]
        else:
            for name in ("normed", "p", "attended"):
                old = getattr(r, "front_" + name)
                getattr(r, name)[pl.ds(0, old.shape[0]), :] = old[...]
            r.logs[: spans[0]] = r.front_logs[...]

        def project(span, rows):
            started = load_input(r, span, rows)[1]
            normed = low(centre(started)[0] * r.vec[0:1, :] + r.vec[2:3, :])
            r.normed[rows, :] = normed
            r.p[rows, :] = low(dot(normed, r.weight[...]))

        def one_span(span, rows, made):
            def scored(pair):
                queries = pair_split(r.p[rows, pl.ds(pair * LANES, LANES)], HEAD**-0.5)
                return key_scores(r.p[rows, pl.ds(D + pair * LANES, LANES)], queries, r.length[span])

            ahead = scored(0)
            for pair in range(PAIRS):
                scores = ahead
                if pair + 1 < PAIRS:
                    ahead = scored(pair + 1)
                peak = jnp.max(scores, axis=0, keepdims=True)
                exped = jnp.exp(scores - peak)
                total = jnp.sum(exped, axis=0, keepdims=True)
                probability = low(exped * (1.0 / total))
                r.logs[span, pair : pair + 1, :] = peak + jnp.log(total)
                values = jnp.transpose(r.p[rows, pl.ds(2 * D + pair * LANES, LANES)])
                attended = jnp.concatenate(
                    [dot(values[:HEAD], probability[:, :seq]), dot(values[HEAD:], probability[:, seq:])], axis=0
                )
                r.attended[rows, pl.ds(pair * LANES, LANES)] = jnp.transpose(low(attended))

        each_span(seq, spans, one_span, project)

    ins = [(name, array, scalars()) for name, array in scalar.items()] + [("order", order), ("tokens", tokens)]
    count = spans[-1] + 1
    rows = count * seq
    outs = [
        ("normed", (rows, D), jnp.bfloat16),
        ("p", (rows, 3 * D), jnp.bfloat16),
        ("attended", (rows, D), jnp.bfloat16),
        ("logs", (count, PAIRS, 2 * seq), jnp.float32),
    ]
    scratch = []
    if fresh:
        ins += [("stack%d" % n, stack) for n, stack in enumerate(first)]
        outs += [("weight", (D, 3 * D), jnp.bfloat16), ("vec", (8, D), jnp.float32)]
        scratch = [("columns", (D, LANES), jnp.bfloat16)]
    else:
        ins += [("weight", front.weight), ("vec", front.vec)]
        ins += [("front_" + name, getattr(front, name)) for name in ("normed", "p", "attended", "logs")]
    return call(body, "attention", 6 if fresh else REAR_COST, ins, outs, scratch)


def hidden_units(hidden, grad_act):
    squared = hidden * hidden
    tilt = jnp.tanh(hidden * (gelu_scale + (gelu_scale * gelu_cubic) * squared))
    gate = 0.5 + 0.5 * tilt
    active = hidden * gate
    slope = gate + active * (1.0 - tilt) * (gelu_scale + (3.0 * gelu_scale * gelu_cubic) * squared)
    return low(active), low(grad_act * slope)


def products_ahead(r, seq, total):
    def products(columns, rows):
        hidden = dot(r.middle_normed[rows, :], r.up[:, columns])
        return hidden, dot_rows(r.cot[rows, :], r.down_full[columns, :])

    spans = [pl.ds(span * seq, seq) for span in range(total // seq)]
    todo = [(pl.ds(first, 2 * LANES), rows) for first in range(0, QUARTER, 2 * LANES) for rows in spans]
    ahead = products(*todo[0])
    for n, (columns, rows) in enumerate(todo):
        here = ahead
        if n + 1 < len(todo):
            ahead = products(*todo[n + 1])
        active, grad_hidden = hidden_units(*here)
        r.active[rows, columns] = active
        r.grad_hidden[rows, columns] = grad_hidden
        if (n + 1) % len(spans) == 0:
            r.grad_up[:, columns] = dot_columns(r.middle_normed[...], r.grad_hidden[:, columns])
            r.grad_down[columns, :] = dot_columns(r.active[:, columns], r.cot[...])


def quarter_call(quarter, scalar, cotangent, stacks, ins, outs, seq, before, after, micros, reused=(), mate=None):
    total = cotangent.shape[0]
    column = 2 * QUARTER * (quarter % 2)

    def body(r):
        stacks = (r.stack0, r.stack1, r.stack2, r.stack3)
        targets = [(r.up, column), (r.down_full, column + QUARTER)]
        if quarter == 0:
            targets.append((r.out_full, 4 * QUARTER))
        assemble(r.me[0], stacks, targets)

        if quarter not in AHEAD:
            def products(span, rows):
                return dot(before(r, span, rows), r.up[...]), dot_rows(r.cot[rows, :], r.down_full[...])

            def one_span(span, rows, made):
                active, grad_hidden = hidden_units(*made)
                r.active[rows, :] = active
                r.grad_hidden[rows, :] = grad_hidden
                after(r, rows, dot_rows(grad_hidden, r.up[...]))

            each_span(seq, range(total // seq), one_span, products)
            r.grad_up[...] = dot_columns(r.middle_normed[...], r.grad_hidden[...])
            r.grad_down[...] = dot_columns(r.active[...], r.cot[...])
        else:

            def enter(span, rows, made):
                before(r, span, rows)

            if quarter == 0:
                each_span(seq, range(total // seq), enter)
            products_ahead(r, seq, total)
            after(r, slice(None), dot_rows(r.grad_hidden[...], r.up[...]))
        if mate is not None:
            arrange(r.me[0], (r.mate_up, r.mate_down, r.grad_up, r.grad_down), r.keep, r.send)

    ins = [("me", scalar["me"], scalars()), ("cot", cotangent)] + ins
    ins += [("stack%d" % n, stack) for n, stack in enumerate(stacks)]
    outs = outs + [("active", (total, QUARTER), jnp.bfloat16), ("down_full", (QUARTER, D), jnp.bfloat16)]
    grads = [("grad_up", (D, QUARTER), jnp.float32), ("grad_down", (QUARTER, D), jnp.float32)]
    scratch = [("up", (D, QUARTER), jnp.bfloat16), ("grad_hidden", (total, QUARTER), jnp.bfloat16)]
    if mate is None:
        outs = outs + grads
    else:
        ins += [("mate_up", mate.grad_up), ("mate_down", mate.grad_down)]
        outs = outs + arranged(4 * QUARTER)
        scratch = scratch + grads
    return call(body, "hidden%d" % quarter, micros, ins, outs, scratch, reused)


def first_quarter(scalar, order, tokens, cotangent, vec, attended, stacks):
    seq = order.shape[2]
    total = tokens.shape[0]

    def enter(r, span, rows):
        middle = load_input(r, span, rows)[1] + dot(r.attended[rows, :], r.out_full[...])
        r.middle[rows, :] = middle
        normed = low(centre(middle)[0] * r.vec[1:2, :] + r.vec[3:4, :])
        r.middle_normed[rows, :] = normed
        return normed

    def leave(r, rows, back):
        r.back[rows, :] = back

    ins = [("step", scalar["step"], scalars()), ("order", order), ("tokens", tokens), ("vec", vec), ("attended", attended)]
    outs = [("middle", (total, D), jnp.float32), ("middle_normed", (total, D), jnp.bfloat16)]
    outs += [("back", (total, D), jnp.float32), ("out_full", (D, D), jnp.bfloat16)]
    return quarter_call(0, scalar, cotangent, stacks, ins, outs, seq, enter, leave, 8.5)


def next_quarter(quarter, scalar, cotangent, stacks, normed, back, seq, mate=None):
    total = normed.shape[0]

    def take(r, span, rows):
        return r.middle_normed[rows, :]

    def leave(r, rows, back):
        r.back[rows, :] = r.old_back[rows, :] + back

    ins = [("middle_normed", normed), ("old_back", back)]
    outs = [("back", (total, D), jnp.float32)]
    reused = [("old_back", "back")]
    return quarter_call(quarter, scalar, cotangent, stacks, ins, outs, seq, take, leave, 6.5, reused, mate)


def middle_back(scalar, cotangent, vec, attended, middle, back, out_full, seq, quarters):
    total = middle.shape[0]

    def body(r):
        r.dvec[...] = jnp.zeros_like(r.dvec)

        def one_span(span, rows, made):
            back = r.back[rows, :]
            hat, scale = centre(r.middle[rows, :])
            dmiddle = wide(r.cot[rows, :]) + norm_back(back, r.vec[1:2, :], hat, scale)
            r.dmiddle[rows, :] = dmiddle
            r.dvec[1:2, :] += jnp.sum(back * hat, axis=0, keepdims=True)
            r.dvec[3:4, :] += jnp.sum(back, axis=0, keepdims=True)
            mixed = low(dmiddle)
            r.mixed[rows, :] = mixed
            r.dattended[rows, :] = low(dot_rows(mixed, r.out_full[...]))

        each_span(seq, range(total // seq), one_span)
        r.grad_out[...] = dot_columns(r.attended[...], r.mixed[...])
        arrange(r.me[0], (r.up0, r.down0, r.up1, r.down1, r.grad_out), r.keep, r.send)

    ins = [("me", scalar["me"], scalars()), ("cot", cotangent), ("vec", vec), ("attended", attended)]
    ins += [("middle", middle), ("back", back), ("out_full", out_full)]
    for n, quarter in enumerate(quarters):
        ins += [("up%d" % n, quarter.grad_up), ("down%d" % n, quarter.grad_down)]
    outs = [("dmiddle", (total, D), jnp.float32), ("dattended", (total, D), jnp.bfloat16), ("dvec", (8, D), jnp.float32)]
    outs += arranged(4 * QUARTER + D)
    scratch = [("grad_out", (D, D), jnp.float32), ("mixed", (total, D), jnp.bfloat16)]
    return call(body, "middle_back", 4, ins, outs, scratch)


def branch_output(middle, quarters, seq, spans, front=None, grad=None):
    rows_before = spans[0] * seq
    rows_here = len(spans) * seq

    def body(r):
        copies = []
        if front is not None:
            here = pl.ds(rows_before, rows_here)
            copies = [
                pltpu.make_async_copy(r.grad, r.input_grad, r.done.at[0]),
                pltpu.make_async_copy(r.front, r.result.at[pl.ds(0, rows_before), :], r.done.at[1]),
                pltpu.make_async_copy(r.rear, r.result.at[here, :], r.done.at[2]),
            ]
            copies[0].start()
            copies[1].start()
        target = r.result if front is None else r.rear

        def one_span(span, rows, made):
            result = r.middle[rows, :]
            for n in range(4):
                result = result + dot(getattr(r, "active%d" % n)[rows, :], getattr(r, "down%d" % n)[...])
            target[pl.ds(pl.multiple_of((span - spans[0]) * seq, seq), seq), :] = low(result)

        each_span(seq, spans, one_span)
        if front is not None:
            copies[2].start()
            for copy in copies:
                copy.wait()

    ins = [("middle", middle)]
    for n, quarter in enumerate(quarters):
        ins += [("active%d" % n, quarter.active), ("down%d" % n, quarter.down_full)]
    if front is None:
        return call(body, "branch_output", 25, ins, [("result", (rows_here, D), jnp.bfloat16)]).result
    ins += [("front", front), ("grad", grad)]
    outs = [("result", (rows_before + rows_here, D), jnp.bfloat16, True), ("input_grad", grad.shape, jnp.float32, True)]
    scratch = [("rear", (rows_here, D), jnp.bfloat16), ("done", (3,), None)]
    done = call(body, "branch_output", 25, ins, outs, scratch)
    return done.result, done.input_grad


def attention_back(scalar, pair, normed, p, logs, dattended, seq, mate=None):
    total = normed.shape[0]
    last = pair == PAIRS - 1

    def body(r):
        def products(span, rows):
            queries = pair_split(r.p[rows, pl.ds(pair * LANES, LANES)], HEAD**-0.5)
            dattended = pair_split(r.dattended[rows, pl.ds(pair * LANES, LANES)])
            scores = key_scores(r.p[rows, pl.ds(D + pair * LANES, LANES)], queries, r.length[span])
            return queries, dattended, scores, dot_rows(r.p[rows, pl.ds(2 * D + pair * LANES, LANES)], dattended)

        def one_span(span, rows, made):
            queries, dattended, scores, dprobability = made
            probability = jnp.exp(scores - r.logs[span, pair : pair + 1, :])
            inner = jnp.sum(probability * dprobability, axis=0, keepdims=True)
            dscores = low(probability * (dprobability - inner))
            dvalues = low(dot(low(probability), dattended))
            dkeys = low(dot(dscores, queries))
            keys = jnp.transpose(low(wide(r.p[rows, pl.ds(D + pair * LANES, LANES)]) * HEAD**-0.5))
            dqueries = jnp.concatenate([dot(keys[:HEAD], dscores[:, :seq]), dot(keys[HEAD:], dscores[:, seq:])], axis=0)
            r.dp[rows, :] = jnp.concatenate([jnp.transpose(low(dqueries)), dkeys, dvalues], axis=1)

        each_span(seq, range(total // seq), one_span, products)
        if not last:
            r.grad[...] = dot_columns(r.normed[...], r.dp[...])
        if mate is not None:
            arrange(r.me[0], (r.mate, r.grad), r.keep, r.send)

    ins = [("me", scalar["me"], scalars()), ("length", scalar["length"], scalars())]
    ins += [("normed", normed), ("p", p), ("logs", logs), ("dattended", dattended)]
    outs = [("dp", (total, 3 * LANES), jnp.bfloat16)]
    grad = ("grad", (D, 3 * LANES), jnp.float32)
    scratch = []
    if mate is not None:
        ins += [("mate", mate.grad)]
        outs += arranged(6 * LANES)
        scratch = [grad]
    elif not last:
        outs += [grad]
    return call(body, "attention_back", 4.6, ins, outs, scratch)


def input_back(scalar, order, tokens, vec, normed, dmiddle, weight, dvec, parts):
    seq = order.shape[2]
    total = tokens.shape[0]

    def body(r):
        parts = [getattr(r, "dp%d" % n) for n in range(PAIRS)]
        r.dvec[...] = jnp.zeros_like(r.dvec)
        r.dvec[:8, :] = r.dvec_in[...]

        def products(span, rows):
            dp = [part[rows, pl.ds(kind * LANES, LANES)] for kind in range(3) for part in parts]
            return dot_rows(jnp.concatenate(dp, axis=1), r.weight[...])

        def one_span(span, rows, back):
            masked, started = load_input(r, span, rows)
            hat, scale = centre(started)
            dstarted = r.dmiddle[rows, :] + norm_back(back, r.vec[0:1, :], hat, scale)
            r.input_grad[rows, :] = jnp.where(masked, 0.0, dstarted)
            r.dvec[0:1, :] += jnp.sum(back * hat, axis=0, keepdims=True)
            r.dvec[2:3, :] += jnp.sum(back, axis=0, keepdims=True)
            r.dvec[4:5, :] += jnp.sum(jnp.where(masked, dstarted, 0.0), axis=0, keepdims=True)

        each_span(seq, range(total // seq), one_span, products)
        r.columns[...] = jnp.transpose(r.dvec[...])
        r.grad[...] = dot_columns(r.normed[...], parts[-1][...])
        arrange(r.me[0], (r.mate, r.grad, r.columns), r.keep, r.send)

    ins = [("me", scalar["me"], scalars()), ("step", scalar["step"], scalars()), ("order", order), ("tokens", tokens)]
    ins += [("vec", vec), ("dmiddle", dmiddle), ("normed", normed), ("weight", weight), ("dvec_in", dvec)]
    ins += [("dp%d" % n, part.dp) for n, part in enumerate(parts)]
    ins += [("mate", parts[-2].grad)]
    outs = [("input_grad", (total, D), jnp.float32)] + arranged(7 * LANES)
    scratch = [
        ("dvec", (LANES, D), jnp.float32),
        ("columns", (D, LANES), jnp.float32),
        ("grad", (D, 3 * LANES), jnp.float32),
    ]
    return call(body, "input_back", 6.5, ins, outs, scratch)


def fold_kernel(keep_ref, taken_ref, total_ref, send_ref):
    half = total_ref.shape[0]
    total_ref[...] = keep_ref[:half, :] + wide(taken_ref[:half, :])
    send_ref[...] = low(keep_ref[half:, :] + wide(taken_ref[half:, :]))


def fold(keep, taken):
    rows, columns = keep.shape
    return pl.pallas_call(
        fold_kernel,
        out_shape=(
            jax.ShapeDtypeStruct((rows // 2, columns), jnp.float32),
            jax.ShapeDtypeStruct((rows // 2, columns), jnp.bfloat16),
        ),
        in_specs=[whole()] * 2,
        out_specs=(whole(), whole()),
        compiler_params=pltpu.CompilerParams(vmem_limit_bytes=VMEM_BYTES),
        cost_estimate=cost(1),
        name="fold",
    )(keep, taken)


def adam_update(master, gradient, moment, square, step_rate, decay_rate):
    moment_new = beta_first * moment + (1.0 - beta_first) * gradient
    square_new = beta_second * square + (1.0 - beta_second) * gradient * gradient
    corrected = (
        moment_new
        / (1.0 - beta_first**STEP)
        / (jnp.sqrt(square_new / (1.0 - beta_second**STEP)) + adam_epsilon)
    )
    return (moment_new, square_new, master - step_rate * (corrected + decay_rate * master))


def unit_order():
    unit = lax.broadcasted_iota(jnp.int32, (D, D), 0)
    place = lax.broadcasted_iota(jnp.int32, (D, D), 1)
    wanted = (place % LANES // ROWS) * 64 + (place // LANES) * ROWS + place % ROWS
    return jnp.where(unit == wanted, 1.0, 0.0).astype(jnp.bfloat16)


def hidden_update_kernel(*refs):
    total, parts = refs[0], refs[1:4]
    up, down, out = refs[4:7], refs[7:10], refs[10:13]
    new_up, new_down, new_out = refs[13:16], refs[16:19], refs[19:22]

    def summed(column, width):
        columns = pl.ds(column, width)
        return total[:ROWS, columns] + sum(wide(part[:, columns]) for part in parts)

    def start(quarter):
        return FIRST_HALF * (1 - quarter // 2) + (quarter % 2) * 2 * QUARTER

    def update(new, old, index, grad, rate):
        results = adam_update(old[0][index], grad, old[1][index], old[2][index], rate, weight_decay)
        for ref, value in zip(new, results):
            ref[index] = value

    sort = unit_order()
    for group in range(FF // D):
        grads = []
        for quarter in range(4):
            grads.append(summed(start(quarter) + group * LANES, LANES))
        rest = jnp.concatenate(grads, axis=1)
        grad = 0.0
        for _ in range(3):
            piece = low(rest)
            grad = grad + dot_rows(piece, sort)
            rest = rest - wide(piece)
        update(new_up, up, (slice(None), pl.ds(group * D, D)), grad, matrix_rate)
    for quarter in range(4):
        grad = summed(start(quarter) + QUARTER, D)
        update(new_down, down, (pl.ds(quarter * ROWS, ROWS), slice(None)), grad, matrix_rate)
    update(new_out, out, Ellipsis, summed(4 * QUARTER, D), output_rate)


def hidden_update(total, parts, up, down, out):
    outs = [jax.ShapeDtypeStruct(state[0].shape, jnp.float32) for state in (up, down, out) for _ in range(3)]
    results = pl.pallas_call(
        hidden_update_kernel,
        out_shape=outs,
        in_specs=[whole()] * 13,
        out_specs=[whole()] * 9,
        compiler_params=pltpu.CompilerParams(vmem_limit_bytes=VMEM_BYTES),
        cost_estimate=cost(3),
        name="hidden_update",
    )(total, *parts, *up, *down, *out)
    return results[:3], results[3:6], results[6:]


def last_update_kernel(*refs):
    early, late = refs[:4], refs[4:8]
    qkv, vec = refs[8:11], refs[11:14]
    new_qkv, new_vec = refs[14:17], refs[17:20]

    def summed(group, column):
        columns = pl.ds(column, LANES)
        return group[0][:ROWS, columns] + sum(wide(part[:, columns]) for part in group[1:])

    for pair in range(PAIRS):
        for kind in range(3):
            group, first = (early, 4 * QUARTER + D) if pair < 2 else (late, 0)
            grad = summed(group, first + (3 * (pair % 2) + kind) * LANES)
            here = pl.ds((kind * PAIRS + pair) * LANES, LANES)
            moment, square, master = adam_update(
                qkv[0][:, here], grad, qkv[1][:, here], qkv[2][:, here], matrix_rate, weight_decay
            )
            new_qkv[0][:, here], new_qkv[1][:, here], new_qkv[2][:, here] = moment, square, master
    grad = summed(late, 6 * LANES)
    grad = jnp.transpose(jnp.concatenate([grad, jnp.zeros((LANES - ROWS, LANES), jnp.float32)], axis=0))
    grad = grad[: vec[0].shape[0], :ROWS]
    results = adam_update(vec[0][...], grad, vec[1][...], vec[2][...], vector_rate, 0.0)
    for ref, value in zip(new_vec, results):
        ref[...] = value


def last_update(total_early, parts_early, total_late, parts_late, qkv, vec):
    outs = [jax.ShapeDtypeStruct(qkv[0].shape, jnp.float32)] * 3 + [jax.ShapeDtypeStruct(vec[0].shape, jnp.float32)] * 3
    results = pl.pallas_call(
        last_update_kernel,
        out_shape=outs,
        in_specs=[whole()] * 14,
        out_specs=[whole()] * 6,
        compiler_params=pltpu.CompilerParams(vmem_limit_bytes=VMEM_BYTES),
        cost_estimate=cost(1),
        name="last_update",
    )(total_early, *parts_early, total_late, *parts_late, *qkv, *vec)
    return results[:3], results[3:]


def exchange(values, count, even_mask, odd_mask):
    pairs = [(i, i ^ (odd_mask if i % 2 else even_mask)) for i in range(count)]
    return lax.ppermute(values, AXES, pairs)


def tie(value, *others):
    return lax.optimization_barrier((value, others))[0]


class Gather:
    def __init__(self, piece, count):
        self.piece, self.count, self.direct = piece, count, piece.shape[0] == ROWS
        self.parts, self.other = [], None

    def far(self):
        if self.direct:
            self.parts = [exchange(self.piece, self.count, offset, offset) for offset in FAR[1:]]
        return self.parts

    def split(self, columns):
        pair = [Gather(self.piece[:, :columns], self.count), Gather(self.piece[:, columns:], self.count)]
        parts = self.far()
        pair[0].parts = [part[:, :columns] for part in parts]
        pair[1].parts = [part[:, columns:] for part in parts]
        return pair

    def stack(self, *waits):
        if self.direct:
            self.piece = jnp.concatenate([self.piece] + [tie(part, *waits) for part in self.parts], axis=0)
        return self.piece

    def core(self, *waits):
        if not self.direct:
            return self.piece
        start = self.other.shape[0] if self.other is not None else 0
        taken = tie(exchange(self.piece[start:], self.count, 1, 1), *waits)
        self.other = taken if self.other is None else jnp.concatenate([self.other, taken], axis=0)
        return taken

    def near(self, *waits):
        if self.direct:
            taken = exchange(self.piece, self.count, 4, 2)
            self.piece = jnp.concatenate([self.piece, tie(taken, *waits)], axis=0)
        return self.piece

    def late(self, *waits):
        if self.direct:
            self.rest = tie(exchange(self.piece, self.count, 2, 4), *waits)

    def finish(self, *waits):
        if not self.direct:
            return ordered_stacks(self.piece)
        return (self.piece, self.rest, self.other, tie(exchange(self.rest, self.count, 1, 1), *waits))


class Scatter:
    def __init__(self, arranged, count, direct):
        self.total, self.send, self.count, self.direct = arranged.keep, arranged.send, count, direct

    def step(self, even, odd, *waits):
        if self.direct:
            self.total, self.send = fold(self.total, tie(exchange(self.send, self.count, even, odd), *waits))
        return self.total, self.send

    def core(self, *waits):
        return self.step(1, 1, *waits)

    def near(self, *waits):
        return self.step(2, 4, *waits)

    def next(self, *waits):
        if self.direct:
            self.total = self.total + wide(tie(exchange(self.send, self.count, 4, 2), *waits))
        return self.total

    def join(self, other):
        self.total = jnp.concatenate([self.total, other.total], axis=1)
        self.send = jnp.concatenate([self.send, other.send], axis=1)

    def parts(self, *waits):
        if not self.direct:
            return []
        taken = []
        for place in range(1, len(FAR)):
            part = low(self.total[place * ROWS : (place + 1) * ROWS])
            taken.append(tie(exchange(part, self.count, FAR[place], FAR[place]), *waits))
        return taken

    def full(self):
        return full_piece(self.total, self.send)


def split_units(up, down):
    rows, units = up.shape
    up = up.reshape(rows, units // 64, 4, ROWS)
    down = down.reshape(rows // ROWS, 4, ROWS, D)
    ups = [up[:, :, quarter].reshape(rows, units // 4) for quarter in range(4)]
    downs = [down[:, quarter].reshape(rows, D) for quarter in range(4)]
    return [jnp.concatenate([ups[n], downs[n], ups[n + 1], downs[n + 1]], axis=1) for n in (0, 2)]


def pack_kernel(*refs):
    sources, first, hidden, buffers, done = refs[:5], refs[5], refs[6], refs[7:12], refs[12]
    copies = [pltpu.make_async_copy(sources[n], buffers[n], done.at[n]) for n in range(5)]
    for copy in copies:
        copy.start()
    qkv, vec, out, up, down = buffers
    copies[0].wait()
    first[:, pl.ds(0, 3 * D)] = low(qkv[...])
    copies[1].wait()
    rows, columns = vec.shape
    turned = jnp.concatenate([vec[...], jnp.zeros((rows, LANES - columns), jnp.float32)], axis=1)
    turned = jnp.transpose(jnp.concatenate([turned, jnp.zeros((LANES - rows, LANES), jnp.float32)], axis=0))
    first[:, pl.ds(3 * D, LANES)] = low(turned[:ROWS])
    for copy in copies[2:]:
        copy.wait()
    sort = unit_order()
    for group in range(FF // D):
        mixed = low(dot(low(up[:, pl.ds(group * D, D)]), sort))
        for quarter in range(4):
            column = 2 * QUARTER * ((quarter + 2) % 4) + group * LANES
            hidden[:, pl.ds(column, LANES)] = mixed[:, quarter * LANES : (quarter + 1) * LANES]
    for quarter in range(4):
        rows = down[pl.ds(quarter * ROWS, ROWS), :]
        hidden[:, pl.ds(2 * QUARTER * ((quarter + 2) % 4) + QUARTER, D)] = low(rows)
    hidden[:, pl.ds(8 * QUARTER, D)] = low(out[...])


def pack(*sources):
    return pl.pallas_call(
        pack_kernel,
        out_shape=(
            jax.ShapeDtypeStruct((ROWS, 3 * D + LANES), jnp.bfloat16),
            jax.ShapeDtypeStruct((ROWS, 8 * QUARTER + D), jnp.bfloat16),
        ),
        in_specs=[pl.BlockSpec(memory_space=pl.ANY)] * 5,
        out_specs=(whole(), whole()),
        scratch_shapes=[pltpu.VMEM(source.shape, source.dtype) for source in sources] + [pltpu.SemaphoreType.DMA((5,))],
        compiler_params=pltpu.CompilerParams(vmem_limit_bytes=VMEM_BYTES),
        cost_estimate=cost(1),
        name="pack",
    )(*[pltpu.with_memory_space_constraint(source, pltpu.HBM) for source in sources])


def join_units(pieces):
    rows = pieces[0].shape[0]
    groups = [[piece[:, n * QUARTER : (n + 1) * QUARTER] for n in range(4)] for piece in pieces]
    ups = [groups[0][0], groups[0][2], groups[1][0], groups[1][2]]
    downs = [groups[0][1], groups[0][3], groups[1][1], groups[1][3]]
    up = jnp.stack([group.reshape(rows, QUARTER // ROWS, ROWS) for group in ups], axis=2)
    down = jnp.stack([group.reshape(rows // ROWS, ROWS, D) for group in downs], axis=1)
    return up.reshape(rows, 4 * QUARTER), down.reshape(rows * 4, D)


def stack_order(core):
    near = (0, 4, 2, 6) if core == 0 else (0, 2, 4, 6)
    return [core ^ group ^ offset for group in near for offset in FAR]


def ordered_stacks(piece):
    blocks = piece.reshape(32, ROWS, piece.shape[1])
    stacks = []
    for core in range(2):
        ordered = jnp.stack([blocks[device] for device in stack_order(core)])
        ordered = ordered.reshape(16 * ROWS, piece.shape[1])
        stacks += [ordered[: 8 * ROWS], ordered[8 * ROWS :]]
    return tuple(stacks)


def full_piece(keep, send):
    columns = keep.shape[1]
    blocks = jnp.concatenate([keep, wide(send)], axis=0).reshape(32, ROWS, columns)
    order = stack_order(0) + stack_order(1)
    return jnp.stack([blocks[order.index(device)] for device in range(32)]).reshape(32 * ROWS, columns)


def local(
    tokens,
    cotangent,
    reveal_order,
    reveal_step,
    lengths,
    weight_qkv,
    weight_out,
    weight_up,
    weight_down,
    vectors,
    moment_qkv,
    square_qkv,
    moment_out,
    square_out,
    moment_up,
    square_up,
    moment_down,
    square_down,
    moment_vec,
    square_vec,
):
    count = lax.axis_size("dp") * lax.axis_size("fsdp")
    direct = weight_qkv.shape[0] == ROWS and count == 32
    me = lax.axis_index("dp") * lax.axis_size("fsdp") + lax.axis_index("fsdp")
    me = (me if direct else 0 * me).astype(jnp.int32)[None]
    spans, seq = reveal_order.shape
    order = reveal_order.reshape(spans, 1, seq)
    flat = tokens.reshape(spans * seq, D)
    upstream = cotangent.reshape(spans * seq, D)

    if direct:
        piece_one, piece_rest = pack(weight_qkv, vectors, weight_out, weight_up, weight_down)
    else:
        columns = jnp.pad(low(vectors).T, ((0, 0), (0, LANES - vectors.shape[0])))
        halves = [jnp.concatenate([low(weight_qkv), columns], axis=1), low(weight_out), low(weight_up), low(weight_down)]
        piece_one, out, up, down = [lax.all_gather(half, AXES, axis=0, tiled=True) for half in halves]
        hidden = split_units(up, down)
        piece_rest = jnp.concatenate([hidden[1], hidden[0], out], axis=1)
    scalar = {"me": me, "step": reveal_step, "length": lengths}

    one = Gather(piece_one, count)
    one.far()
    one.stack()
    two = Gather(tie(piece_rest[:, 4 * QUARTER :], one.core()), count)
    two.far()
    one.near()
    one.late()
    three = Gather(tie(piece_rest[:, : 4 * QUARTER], one.core()), count)
    three.far()
    first = one.finish()
    two.stack()
    front = attention(scalar, order, flat, first, range(0, spans // 2))
    two.near()
    two.late()
    two.core()
    three.stack(front.logs)
    rear = attention(scalar, order, tie(flat, two.piece), None, range(spans // 2, spans), front)
    vec, weight = front.vec, front.weight
    two.rest = tie(two.rest, rear.logs) if direct else None
    second = two.finish()
    three.near(rear.logs)
    h = [first_quarter(scalar, order, flat, tie(upstream, three.piece), vec, rear.attended, second)]
    normed = h[0].middle_normed
    three.late(h[0].back)
    three.core(h[0].back)
    h += [next_quarter(1, scalar, upstream, second, normed, h[0].back, seq, h[0])]
    third = three.finish(h[1].back)
    h += [next_quarter(2, scalar, upstream, third, normed, h[1].back, seq)]
    sum_one = Scatter(h[1], count, direct)
    h += [next_quarter(3, scalar, tie(upstream, *sum_one.core(h[2].back)), third, normed, h[2].back, seq)]
    turn = middle_back(
        scalar, tie(upstream, h[3].back), vec, rear.attended, h[0].middle, h[3].back, h[0].out_full, seq, h[2:]
    )
    sum_one.near(turn.dattended)
    sum_two = Scatter(turn, count, direct)

    def part(pair, *waits, mate=None):
        dattended = tie(turn.dattended, *waits)
        return attention_back(scalar, pair, rear.normed, rear.p, rear.logs, dattended, seq, mate)

    parts = [part(0, sum_one.total)]
    parts += [part(1, sum_one.next(parts[0].dp), *sum_two.core(parts[0].dp), mate=parts[0])]
    early = Scatter(parts[1], count, direct)
    parts += [part(2, sum_one.total)]
    early.core(parts[2].dp)
    sum_two.near(parts[2].dp)
    parts += [part(3, sum_two.total, early.total)]
    early.near(parts[3].dp)
    if direct:
        sum_two.join(early)
    ready = tie(flat, parts[3].dp, sum_two.total)
    final = input_back(scalar, order, ready, vec, rear.normed, turn.dmiddle, weight, turn.dvec, parts)
    late = Scatter(final, count, direct)
    result = branch_output(tie(h[0].middle, final.input_grad), h, seq, range(0, spans // 2))
    sum_two.next(result)
    late.core(result)
    middle = tie(h[0].middle, late.total)
    result, input_grad = branch_output(middle, h, seq, range(spans // 2, spans), result, final.input_grad)
    if direct:
        sum_two.total = jnp.concatenate([sum_two.total, sum_one.total], axis=1)
    parts_two = sum_two.parts()
    late.near(result)
    qkv_state = (weight_qkv, moment_qkv, square_qkv)
    vec_state = (vectors, moment_vec, square_vec)
    out_state = (weight_out, moment_out, square_out)
    up_state = (weight_up, moment_up, square_up)
    down_state = (weight_down, moment_down, square_down)
    if direct:
        states = hidden_update(tie(sum_two.total, late.send), parts_two, up_state, down_state, out_state)
        new_up, new_down, new_out = states
        late.next()
        parts_late = late.parts()
        new_qkv, new_vec = last_update(sum_two.total, parts_two, late.total, parts_late, qkv_state, vec_state)
    else:
        ones, twos = sum_one.full(), sum_two.full()
        threes = jnp.concatenate([early.full(), late.full()], axis=1)
        qkv = [threes[:, (3 * pair + kind) * LANES :][:, :LANES] for kind in range(3) for pair in range(PAIRS)]
        grads = [jnp.concatenate(qkv, axis=1), threes[:, 3 * D : 3 * D + vectors.shape[0]]]
        grads += [twos[:, 4 * QUARTER :], *join_units([ones, twos])]
        grads = [lax.psum_scatter(grad, AXES, scatter_dimension=0, tiled=True) for grad in grads]

        def update(state, grad, rate, decay):
            return adam_update(state[0], grad, state[1], state[2], rate, decay)

        new_qkv = update(qkv_state, grads[0], matrix_rate, weight_decay)
        new_vec = update(vec_state, grads[1].T, vector_rate, 0.0)
        new_out = update(out_state, grads[2], output_rate, weight_decay)
        new_up = update(up_state, grads[3], matrix_rate, weight_decay)
        new_down = update(down_state, grads[4], matrix_rate, weight_decay)
    return (
        result.reshape(tokens.shape),
        input_grad.reshape(tokens.shape),
        *new_qkv,
        *new_out,
        *new_up,
        *new_down,
        *new_vec,
    )


def solution(mesh):
    return jax.shard_map(
        local,
        mesh=mesh,
        in_specs=(
            P(("dp", "fsdp"), None, None),
            P(("dp", "fsdp"), None, None),
            P(("dp", "fsdp"), None),
            P(("dp", "fsdp")),
            P(("dp", "fsdp")),
            P(("dp", "fsdp"), None),
            P(("dp", "fsdp"), None),
            P(("dp", "fsdp"), None),
            P(("dp", "fsdp"), None),
            P(None, ("dp", "fsdp")),
            P(("dp", "fsdp"), None),
            P(("dp", "fsdp"), None),
            P(("dp", "fsdp"), None),
            P(("dp", "fsdp"), None),
            P(("dp", "fsdp"), None),
            P(("dp", "fsdp"), None),
            P(("dp", "fsdp"), None),
            P(("dp", "fsdp"), None),
            P(None, ("dp", "fsdp")),
            P(None, ("dp", "fsdp")),
        ),
        out_specs=(
            P(("dp", "fsdp"), None, None),
            P(("dp", "fsdp"), None, None),
            P(("dp", "fsdp"), None),
            P(("dp", "fsdp"), None),
            P(("dp", "fsdp"), None),
            P(("dp", "fsdp"), None),
            P(("dp", "fsdp"), None),
            P(("dp", "fsdp"), None),
            P(("dp", "fsdp"), None),
            P(("dp", "fsdp"), None),
            P(("dp", "fsdp"), None),
            P(("dp", "fsdp"), None),
            P(("dp", "fsdp"), None),
            P(("dp", "fsdp"), None),
            P(None, ("dp", "fsdp")),
            P(None, ("dp", "fsdp")),
            P(None, ("dp", "fsdp")),
        ),
        check_vma=False,
    )
```
